32 devices in a mesh: wide: 8 (over y, x, core), narrow: 4 (over z).
Axes of the slice: x: 2, y: 2, z: 4, core: 2. Of those that a mesh axis runs over, the one named last changes fastest.
Arguments:
- decode_hidden_input: bfloat16 [256, 8192], P('wide'), may hold values from -6 to 6
- queries: bfloat16 [256, 8192], P('wide', 'narrow'), may hold values from -8 to 8
- cached_key_rows: bfloat16 [256, 256, 1024], P('wide', None, 'narrow'), may hold values from -4 to 4
- cached_value_rows: bfloat16 [256, 256, 1024], P('wide', None, 'narrow'), may hold values from -6 to 6
- lengths: int32 [256], P('wide'), may hold values from 2 to 256, as said below
- decode_adapter_index: int32 [256], P('wide'), may hold values from 0 to 127, as said below
- key_matrix: bfloat16 [8192, 1024], P(None, 'narrow'), may hold values from -0.0625 to 0.0625
- value_matrix: bfloat16 [8192, 1024], P(None, 'narrow'), may hold values from -0.0625 to 0.0625
- adapter_down_map: bfloat16 [128, 16, 8192], P('wide', None, 'narrow'), may hold values from -0.0625 to 0.0625
- adapter_up_map: bfloat16 [128, 16, 1024], P('wide', None, 'narrow'), may hold values from -0.1875 to 0.1875
- training_hidden_input: bfloat16 [8192, 8192], P('wide', 'narrow'), may hold values from -6 to 6
- cotangent: bfloat16 [8192, 1024], P('wide', 'narrow'), may hold values from -0.3984375 to 0.3984375
- training_adapter_index: int32 [8192], P('wide'), may hold values from 0 to 127, as said below
- rewards: int32 [8192], P('wide'), may hold values from -2 to 2
Outputs:
- attended: bfloat16 [256, 8192], P('wide', 'narrow')
- fresh_values: bfloat16 [256, 1024], P('wide', 'narrow')
- grad_down: float32 [128, 16, 8192], P('wide', None, 'narrow')
- grad_up: float32 [128, 16, 1024], P('wide', None, 'narrow')
The draws below stay inside these ranges and needn't reach their ends.
Inputs may be any that keep to these rules, and one draw needn't show every extreme that they name: `decode_adapter_index`: of the 32 rows of one index of wide, at most 8 use adapters of one owner (adapters o * 16 to (o + 1) * 16 - 1); in every draw one owner gets exactly 8 rows from every index of wide. `training_adapter_index`: of the 1024 tokens of one index of wide, at most 256 use adapters of one owner (adapters o * 16 to (o + 1) * 16 - 1); in every draw one owner gets exactly 256 tokens from every index of wide. `lengths`: every block of 32 rows holds a row of length 256.
All inputs are finite; a program needn't handle non-finite values.
Results may differ from the reference program's by a relative error of at most 0.0051.
Values may be sent and summed in bfloat16 or wider, within the bound.
No kernel may reach another device: no remote copies, remote signals or barrier semaphores. Data moves between devices by JAX's collectives and lax.ppermute only.
A program may use at most 128 MiB of HBM per device.

```python
import math
import jax
import jax.numpy as jnp
from jax import lax

MODEL_WIDTH = 8192
HEADS = 64
KEY_VALUE_HEADS = 8
HEAD_SIZE = 128
ADAPTER_RANK = 16
ADP_DEV = 16
ROW_DEV = 32
TOK_DEV = 1024
CACHE = 256
ADAPTER_COUNT = 128
ROWS = 256
TOKENS = 8192


def route_draw(key, blocks, rows, owners, owner_totals, salt):
    capacity = 2 * rows // owners
    slots = owners * capacity
    popular_key, block_key = jax.random.split(jax.random.fold_in(key, salt))
    standing = jax.random.permutation(popular_key, owners).astype(jnp.int32)
    slot_owner = jnp.arange(slots, dtype=jnp.int32) // capacity
    slot_rank = standing[slot_owner]

    def one_block(subkey):
        noise_key, order_key, local_key, mixing_key = jax.random.split(subkey, 4)
        noise_value = jax.random.randint(noise_key, (slots,), 0, 64).astype(jnp.int32)
        tiebreak = jax.random.permutation(order_key, slots).astype(jnp.int32)
        favour = jnp.where(slot_rank == owners - 1, 1024, 0).astype(jnp.int32)
        score = (noise_value + slot_rank * 4 + favour) * slots + tiebreak
        chosen = lax.top_k(score, rows)[1].astype(jnp.int32)
        owner_pick = chosen // capacity
        local_pick = jax.random.randint(local_key, (rows,), 0, owner_totals).astype(jnp.int32)
        picked = owner_pick * owner_totals + local_pick
        return picked[jax.random.permutation(mixing_key, rows)]
    drawn = jax.vmap(one_block)(jax.random.split(block_key, blocks))
    return drawn.reshape(-1).astype(jnp.int32)


def draw_decode_adapter_index(key, part):
    return route_draw(key, ROWS // ROW_DEV, ROW_DEV, ROWS // ROW_DEV, ADP_DEV, 7)


def draw_training_adapter_index(key, part):
    return route_draw(key, TOKENS // TOK_DEV, TOK_DEV, TOKENS // TOK_DEV, ADP_DEV, 11)


def draw_lengths(key, part):
    first_key, second_key = jax.random.split(jax.random.fold_in(key, 13))
    drawn = jax.random.randint(first_key, (ROWS,), 2, CACHE + 1).astype(jnp.int32)
    blocks = ROWS // ROW_DEV
    longest = jax.random.randint(second_key, (blocks,), 0, ROW_DEV).astype(jnp.int32)
    filled = (jnp.arange(ROW_DEV, dtype=jnp.int32)[None, :] == longest[:, None]).reshape(-1)
    return jnp.where(filled, CACHE, drawn).astype(jnp.int32)


def drawn_pair(key):
    key_part, query_part = jax.random.split(jax.random.fold_in(key, 29))
    group = HEADS // KEY_VALUE_HEADS
    key_shape = (ROWS, CACHE, KEY_VALUE_HEADS, HEAD_SIZE)
    query_shape = (ROWS, KEY_VALUE_HEADS, group, HEAD_SIZE)
    key_draw = jnp.clip(jax.random.normal(key_part, key_shape, jnp.float32), -4.0, 4.0)
    query_draw = jnp.clip(jax.random.normal(query_part, query_shape, jnp.float32), -8.0, 8.0)
    return (key_draw.reshape(ROWS, CACHE, KEY_VALUE_HEADS * HEAD_SIZE), query_draw.reshape(ROWS, HEADS * HEAD_SIZE))


def draw_cached_key_rows(key, part):
    return drawn_pair(key)[0].astype(jnp.bfloat16)


def draw_queries(key, part):
    return drawn_pair(key)[1].astype(jnp.bfloat16)


def place_ends(entries, key, smallest, high):
    longest = entries.shape.index(max(entries.shape))
    spots = []
    for shift in (0, 1):
        where = [jax.random.randint(jax.random.fold_in(key, axis), (), 0, length) for axis, length in enumerate(entries.shape)]
        where[longest] = (where[longest] + shift) % entries.shape[longest]
        spots.append(tuple(where))
    return entries.at[spots[0]].set(smallest).at[spots[1]].set(high)


def block_levels(rng, extent, shards, least, top_value):
    def one(position, shards_of):
        steps = jax.random.uniform(jax.random.fold_in(jax.random.fold_in(rng, 6), position), (shards_of,), jnp.float32, least / len(shards), top_value / len(shards))
        return jnp.repeat(jnp.exp(steps), extent[position] // shards_of).reshape((-1,) + (1,) * (len(extent) - position - 1))

    loudness = one(*shards[0])
    for cut in shards[1:]:
        loudness = loudness * one(*cut)
    return loudness


def noise(rng, dims, deviation, bound, cuts=(), kind=jnp.bfloat16):
    values = jax.random.normal(rng, dims, jnp.float32) * deviation
    if len(cuts) > 0:
        values = block_levels(rng, dims, cuts, -0.22, 0.18) * values
    return jnp.clip(values, min=-bound, max=bound).astype(kind)


def setup_inputs(seed: int = 0) -> dict:
    arg_keys = jax.random.split(jax.random.key(seed), 15)
    return {
        "decode_hidden_input": noise(arg_keys[0], (ROWS, MODEL_WIDTH), 1.0, 6.0, ((0, 8),)),
        "queries": draw_queries(jax.random.fold_in(arg_keys[14], 71), 0),
        "cached_key_rows": draw_cached_key_rows(jax.random.fold_in(arg_keys[14], 71), 0),
        "cached_value_rows": noise(arg_keys[3], (ROWS, CACHE, KEY_VALUE_HEADS * HEAD_SIZE), 1.0, 6.0, ((0, 8), (2, 4))),
        "lengths": draw_lengths(jax.random.fold_in(arg_keys[14], 71), 0),
        "decode_adapter_index": draw_decode_adapter_index(jax.random.fold_in(arg_keys[14], 71), 0),
        "key_matrix": noise(arg_keys[6], (MODEL_WIDTH, KEY_VALUE_HEADS * HEAD_SIZE), MODEL_WIDTH ** -0.5, 0.0625, ((1, 4),)),
        "value_matrix": noise(arg_keys[7], (MODEL_WIDTH, KEY_VALUE_HEADS * HEAD_SIZE), MODEL_WIDTH ** -0.5, 0.0625, ((1, 4),)),
        "adapter_down_map": noise(arg_keys[8], (ADAPTER_COUNT, ADAPTER_RANK, MODEL_WIDTH), MODEL_WIDTH ** -0.5, 0.0625, ((0, 8), (2, 4))),
        "adapter_up_map": noise(arg_keys[9], (ADAPTER_COUNT, ADAPTER_RANK, KEY_VALUE_HEADS * HEAD_SIZE), (KEY_VALUE_HEADS * HEAD_SIZE) ** -0.5, 0.1875, ((0, 8), (2, 4))),
        "training_hidden_input": noise(arg_keys[10], (TOKENS, MODEL_WIDTH), 1.0, 6.0, ((0, 8), (1, 4))),
        "cotangent": noise(arg_keys[11], (TOKENS, KEY_VALUE_HEADS * HEAD_SIZE), 0.05, 0.3984375, ((0, 8), (1, 4))),
        "training_adapter_index": draw_training_adapter_index(jax.random.fold_in(arg_keys[14], 71), 0),
        "rewards": place_ends(jax.random.randint(arg_keys[13], (TOKENS,), -2, 3), jax.random.fold_in(arg_keys[13], 1), -2, 2).astype(jnp.int32),
    }


ADAPTER_SCALE = 2.0
NEG_FILL = -1e+30

def attention_block(input_rows, projected_queries, projected_keys, projected_values, row_lengths, adapter_per_row, key_matrix, value_matrix, adapter_down_map, adapter_up_map):
    row_count = input_rows.shape[0]
    group = HEADS // KEY_VALUE_HEADS
    fresh_keys = jnp.dot(input_rows, key_matrix, preferred_element_type=jnp.float32).astype(jnp.bfloat16)
    down_weight_rows = adapter_down_map[adapter_per_row].astype(jnp.float32)
    rank_activations = jnp.einsum('fj,fkj->fk', input_rows.astype(jnp.float32), down_weight_rows).astype(jnp.bfloat16)
    up_weight_rows = adapter_up_map[adapter_per_row].astype(jnp.float32)
    value_delta_rows = (ADAPTER_SCALE * jnp.einsum('xy,xyd->xd', rank_activations.astype(jnp.float32), up_weight_rows)).astype(jnp.bfloat16)
    fresh_values = (jnp.dot(input_rows, value_matrix, preferred_element_type=jnp.float32) + value_delta_rows.astype(jnp.float32)).astype(jnp.bfloat16)
    query_heads = projected_queries.reshape(row_count, KEY_VALUE_HEADS, group, HEAD_SIZE).astype(jnp.float32)
    key_heads = projected_keys.reshape(row_count, CACHE, KEY_VALUE_HEADS, HEAD_SIZE).astype(jnp.float32)
    value_heads = projected_values.reshape(row_count, CACHE, KEY_VALUE_HEADS, HEAD_SIZE).astype(jnp.float32)
    inverse = 1.0 / math.sqrt(HEAD_SIZE)
    scores = jnp.einsum('bhgd,bphd->bhgp', query_heads, key_heads) * inverse
    own_score = jnp.einsum('bhgd,bhd->bhg', query_heads, fresh_keys.reshape(row_count, KEY_VALUE_HEADS, HEAD_SIZE).astype(jnp.float32)) * inverse
    allowed = jnp.arange(CACHE)[None, :] < row_lengths[:, None]
    scores = jnp.where(allowed[:, None, None, :], scores, NEG_FILL)
    highest = jnp.maximum(lax.optimization_barrier(jnp.max(scores, axis=-1)), own_score)
    cache_exp = jnp.exp(scores - highest[..., None])
    own_exp = jnp.exp(own_score - highest)
    denominator = lax.optimization_barrier(jnp.sum(cache_exp, axis=-1)) + own_exp
    cache_weight = (cache_exp / denominator[..., None]).astype(jnp.bfloat16)
    own_weight = (own_exp / denominator).astype(jnp.bfloat16)
    attended = jnp.einsum('bhgp,bphd->bhgd', cache_weight.astype(jnp.float32), value_heads)
    attended = attended + own_weight.astype(jnp.float32)[..., None] * fresh_values.reshape(row_count, KEY_VALUE_HEADS, 1, HEAD_SIZE).astype(jnp.float32)
    return (attended.reshape(row_count, HEADS * HEAD_SIZE).astype(jnp.bfloat16), fresh_values)

def reference(decode_hidden_input, queries, cached_key_rows, cached_value_rows, lengths, decode_adapter_index, key_matrix, value_matrix, adapter_down_map, adapter_up_map, training_hidden_input, cotangent, training_adapter_index, rewards):
    row_block = math.gcd(ROWS, 128)

    def split_rows(array):
        return array.reshape((ROWS // row_block, row_block) + array.shape[1:])

    def decode_piece(split_parts):
        return attention_block(*split_parts, key_matrix, value_matrix, adapter_down_map, adapter_up_map)
    attended, fresh_values = lax.map(decode_piece, (split_rows(decode_hidden_input), split_rows(queries), split_rows(cached_key_rows), split_rows(cached_value_rows), split_rows(lengths), split_rows(decode_adapter_index)))
    attended = attended.reshape(ROWS, HEADS * HEAD_SIZE)
    fresh_values = fresh_values.reshape(ROWS, KEY_VALUE_HEADS * HEAD_SIZE)
    tok_block = math.gcd(TOKENS, 256)

    def split_tokens(array):
        return array.reshape((TOKENS // tok_block, tok_block) + array.shape[1:])

    def train_step(carry, split_parts):
        grad_down, grad_up = carry
        input_rows, incoming_gradient, adapter_per_row, row_rewards = split_parts
        hidden_state = jnp.einsum('fj,fkj->fk', input_rows.astype(jnp.float32), adapter_down_map[adapter_per_row].astype(jnp.float32))
        backward_result = jnp.einsum('ha,hya->hy', incoming_gradient.astype(jnp.float32), adapter_up_map[adapter_per_row].astype(jnp.float32))
        scale_factor = ADAPTER_SCALE * row_rewards.astype(jnp.float32)[:, None]
        scaled_rank = (scale_factor * hidden_state).astype(jnp.bfloat16)
        scaled_back = (scale_factor * backward_result).astype(jnp.bfloat16)
        grad_down = grad_down.at[adapter_per_row].add(jnp.einsum('nr,nd->nrd', scaled_back.astype(jnp.float32), input_rows.astype(jnp.float32)))
        grad_up = grad_up.at[adapter_per_row].add(jnp.einsum('nr,nk->nrk', scaled_rank.astype(jnp.float32), incoming_gradient.astype(jnp.float32)))
        return ((grad_down, grad_up), None)
    start = (jnp.zeros((ADAPTER_COUNT, ADAPTER_RANK, MODEL_WIDTH), jnp.float32), jnp.zeros((ADAPTER_COUNT, ADAPTER_RANK, KEY_VALUE_HEADS * HEAD_SIZE), jnp.float32))
    (grad_down, grad_up), unused = lax.scan(train_step, start, (split_tokens(training_hidden_input), split_tokens(cotangent), split_tokens(training_adapter_index), split_tokens(rewards)))
    return (attended, fresh_values, grad_down, grad_up)
```

```python
import functools
import math

import jax
import jax.numpy as jnp
from jax import lax
from jax.experimental import pallas as pl
from jax.experimental.pallas import tpu as pltpu
from jax.sharding import PartitionSpec as P

HEADS = 64
KEY_VALUE_HEADS = 8
HEAD_SIZE = 128
CACHE = 256

ADAPTER_SCALE = 2.0
NEG_FILL = -1e30
VMEM_LIMIT = 48 * 1024 * 1024


def swap(array, axis, mask):
    count = lax.axis_size(axis)
    return lax.ppermute(array, axis, [(i, i ^ mask) for i in range(count)])


def axis_bits(axis):
    count = lax.axis_size(axis)
    assert count & (count - 1) == 0, "axis size"
    return [1 << k for k in range(count.bit_length() - 1)]


def highest_in(order, mask):
    return [bit for bit in order if bit & mask][-1]


def largest_tile(length, limit):
    tile = length
    while tile > limit and tile % 2 == 0:
        tile //= 2
    return tile


def rank_kernel(chunk_bases, rank, own_tiles, with_rows, *refs):
    codes_ref, own_ref, mate_ref = refs[:3]
    rest = refs[3:]
    if with_rows:
        row_codes_ref, rows_ref = rest[:2]
        rest = rest[2:]
    maps = rest[: len(chunk_bases)]
    out_ref = rest[len(chunk_bases)]
    step = pl.program_id(0)

    def project(codes, tokens):
        total = jnp.zeros((rank, tokens.shape[0]), jnp.float32)
        for base, chunk in zip(chunk_bases, maps):
            products = lax.dot_general(
                chunk[...], tokens, (((1,), (1,)), ((), ())), preferred_element_type=jnp.float32
            )
            for j in range(chunk.shape[0] // rank):
                total += jnp.where(codes == base + j, products[j * rank : (j + 1) * rank], 0.0)
        return total

    @pl.when(step < own_tiles)
    def _():
        out_ref[...] = project(codes_ref[...], own_ref[...])

    @pl.when(step >= own_tiles)
    def _():
        out_ref[...] = project(codes_ref[...], mate_ref[...])

    if with_rows:

        @pl.when(step == 0)
        def _():
            rest[len(chunk_bases) + 1][...] = project(row_codes_ref[...], rows_ref[...])


def project_tokens(codes, own, mate, chunks, rank, row_codes=None, rows=None):
    token_count, width = own.shape
    tile = largest_tile(token_count, 512)
    own_tiles = token_count // tile
    with_rows = rows is not None
    in_specs = [
        pl.BlockSpec((1, tile), lambda i: (0, i)),
        pl.BlockSpec((tile, width), lambda i: (jnp.minimum(i, own_tiles - 1), 0)),
        pl.BlockSpec((tile, width), lambda i: (jnp.maximum(i - own_tiles, 0), 0)),
    ]
    operands = [codes, own, mate]
    out_specs = [pl.BlockSpec((rank, tile), lambda i: (0, i))]
    out_shape = [jax.ShapeDtypeStruct((rank, 2 * token_count), jnp.float32)]
    if with_rows:
        in_specs += [pl.BlockSpec(a.shape, lambda i: (0, 0)) for a in (row_codes, rows)]
        operands += [row_codes, rows]
        out_specs.append(pl.BlockSpec((rank, rows.shape[0]), lambda i: (0, 0)))
        out_shape.append(jax.ShapeDtypeStruct((rank, rows.shape[0]), jnp.float32))
    in_specs += [pl.BlockSpec(chunk.shape, lambda i: (0, 0)) for _, chunk in chunks]
    operands += [chunk for _, chunk in chunks]
    map_rows = sum(chunk.shape[0] for _, chunk in chunks)
    return pl.pallas_call(
        functools.partial(
            rank_kernel, [base for base, _ in chunks], rank, own_tiles, with_rows
        ),
        grid=(2 * own_tiles,),
        in_specs=in_specs,
        out_specs=out_specs,
        out_shape=out_shape,
        compiler_params=pltpu.CompilerParams(vmem_limit_bytes=VMEM_LIMIT),
        cost_estimate=pl.CostEstimate(
            flops=4 * token_count * width * map_rows,
            bytes_accessed=4 * token_count * width + 2 * map_rows * width,
            transcendentals=0,
        ),
    )(*operands)


def gradient_kernel(chunk_bases, rank, adapters, *refs):
    codes_ref, rewards_ref, factor_ref, own_ref, mate_ref = refs[:5]
    outs = refs[5:-1]
    spread_ref = refs[-1]
    token_count = own_ref.shape[0]
    chunk_rows = adapters * rank

    @pl.when(pl.program_id(0) == 0)
    def _():
        scale = ADAPTER_SCALE * rewards_ref[...].astype(jnp.float32)
        scaled = (scale * factor_ref[...]).astype(jnp.bfloat16).astype(jnp.float32)
        codes = codes_ref[...]
        for k, base in enumerate(chunk_bases):
            for j in range(adapters):
                first = k * chunk_rows + j * rank
                spread_ref[first : first + rank, :] = jnp.where(
                    codes == base + j, scaled, 0.0
                ).astype(jnp.bfloat16)

    for k, out_ref in enumerate(outs):
        spread = spread_ref[k * chunk_rows : (k + 1) * chunk_rows, :]
        total = jnp.dot(
            spread[:, :token_count], own_ref[...], preferred_element_type=jnp.float32
        ) + jnp.dot(spread[:, token_count:], mate_ref[...], preferred_element_type=jnp.float32)
        out_ref[...] = total.astype(out_ref.dtype)


def gradient_chunks(codes, rewards, factor, own, mate, chunks, adapters):
    rank = factor.shape[0]
    token_count, width = own.shape
    tile = largest_tile(width, 512)
    rows = adapters * rank
    whole = lambda i: (0, 0)
    return pl.pallas_call(
        functools.partial(gradient_kernel, [base for base, _ in chunks], rank, adapters),
        grid=(width // tile,),
        in_specs=[
            pl.BlockSpec(codes.shape, whole),
            pl.BlockSpec(rewards.shape, whole),
            pl.BlockSpec(factor.shape, whole),
            pl.BlockSpec((token_count, tile), lambda i: (0, i)),
            pl.BlockSpec((token_count, tile), lambda i: (0, i)),
        ],
        out_specs=[pl.BlockSpec((rows, tile), lambda i: (0, i)) for _ in chunks],
        out_shape=[jax.ShapeDtypeStruct((rows, width), dtype) for _, dtype in chunks],
        scratch_shapes=[pltpu.VMEM((len(chunks) * rows, 2 * token_count), jnp.bfloat16)],
        compiler_params=pltpu.CompilerParams(vmem_limit_bytes=VMEM_LIMIT),
        cost_estimate=pl.CostEstimate(
            flops=4 * token_count * width * rows * len(chunks),
            bytes_accessed=4 * token_count * width + 4 * rows * width * len(chunks),
            transcendentals=0,
        ),
    )(codes, rewards, factor, own, mate)


def sum_over(axis, pieces):
    bits = axis_bits(axis)
    for step in range(len(bits)):
        pieces = [
            piece + swap(piece, axis, bits[step] if k % 2 == 0 else bits[-1 - step])
            for k, piece in enumerate(pieces)
        ]
    return pieces


def attend_cached(queries, cached_key_rows, cached_value_rows, lengths, fresh_keys):
    row_count = queries.shape[0]
    kv_local = fresh_keys.shape[1] // HEAD_SIZE
    group = HEADS // KEY_VALUE_HEADS
    query_heads = queries.reshape(row_count, kv_local, group, HEAD_SIZE)
    key_heads = cached_key_rows.reshape(row_count, CACHE, kv_local, HEAD_SIZE)
    value_heads = cached_value_rows.reshape(row_count, CACHE, kv_local, HEAD_SIZE)
    inverse = 1.0 / math.sqrt(HEAD_SIZE)
    scores = (
        jnp.einsum("bhgd,bphd->bhgp", query_heads, key_heads, preferred_element_type=jnp.float32)
        * inverse
    )
    own_score = (
        jnp.einsum(
            "bhgd,bhd->bhg",
            query_heads,
            fresh_keys.reshape(row_count, kv_local, HEAD_SIZE),
            preferred_element_type=jnp.float32,
        )
        * inverse
    )
    allowed = jnp.arange(CACHE, dtype=jnp.int32)[None, :] < lengths[:, None]
    scores = jnp.where(allowed[:, None, None, :], scores, NEG_FILL)
    highest = jnp.maximum(jnp.max(scores, axis=-1), own_score)
    cache_exp = jnp.exp(scores - highest[..., None])
    own_exp = jnp.exp(own_score - highest)
    denominator = jnp.sum(cache_exp, axis=-1) + own_exp
    cache_weight = (cache_exp / denominator[..., None]).astype(jnp.bfloat16)
    own_weight = (own_exp / denominator).astype(jnp.bfloat16)
    attended = jnp.einsum(
        "bhgp,bphd->bhgd", cache_weight, value_heads, preferred_element_type=jnp.float32
    )
    return attended, own_weight


def per_device(
    decode_hidden_input,
    queries,
    cached_key_rows,
    cached_value_rows,
    lengths,
    decode_adapter_index,
    key_matrix,
    value_matrix,
    adapter_down_map,
    adapter_up_map,
    training_hidden_input,
    cotangent,
    training_adapter_index,
    rewards,
):
    core_bit, *chip_bits = axis_bits("wide")
    masks = [m for m in range(lax.axis_size("wide")) if not m & core_bit]
    me = lax.axis_index("wide")
    owner_totals, rank, down_width = adapter_down_map.shape
    up_width = adapter_up_map.shape[2]
    row_count = decode_hidden_input.shape[0]
    token_count = training_hidden_input.shape[0]
    parts = len(chip_bits) if owner_totals % len(chip_bits) == 0 else 1
    orders = [chip_bits[p:] + chip_bits[:p] for p in range(parts)]
    part_adapters = owner_totals // parts
    part_rows = part_adapters * rank

    flattened_down = adapter_down_map.reshape(-1, down_width)
    flattened_up = adapter_up_map.reshape(-1, up_width)

    up_maps = {m: swap(flattened_up, "wide", m) if m else flattened_up for m in masks}
    down_parts = {}
    for p, order in enumerate(orders):
        down_parts[0, p] = flattened_down[p * part_rows : (p + 1) * part_rows]
        held = [0]
        for bit in order:
            for m in held:
                down_parts[m | bit, p] = swap(down_parts[m, p], "wide", bit)
            held = held + [m | bit for m in held]

    numbers = jnp.concatenate([training_adapter_index, rewards, decode_adapter_index])
    mate_numbers = swap(numbers, "wide", core_bit)
    mate_rows = swap(training_hidden_input, "wide", core_bit)
    mate_cotangent = swap(cotangent, "wide", core_bit)
    decode_slice = lax.dynamic_slice_in_dim(
        decode_hidden_input, lax.axis_index("narrow") * down_width, down_width, 1
    )
    mate_slice = swap(decode_slice, "wide", core_bit)

    def codes_of(ids):
        return ((ids // owner_totals) ^ me) * owner_totals + ids % owner_totals

    token_codes = codes_of(
        jnp.concatenate([training_adapter_index, mate_numbers[:token_count]])
    )[None, :]
    token_rewards = jnp.concatenate([rewards, mate_numbers[token_count : 2 * token_count]])[
        None, :
    ]
    pad = -2 * row_count % 128
    row_codes = codes_of(
        jnp.concatenate([decode_adapter_index, mate_numbers[2 * token_count :]])
    )
    padded_codes = jnp.concatenate([row_codes, jnp.full((pad,), -1, jnp.int32)])[None, :]
    chip_slices = jnp.concatenate(
        [decode_slice, mate_slice, jnp.zeros((pad, down_width), decode_slice.dtype)]
    )

    (part_back,) = project_tokens(
        token_codes,
        cotangent,
        mate_cotangent,
        [(m * owner_totals, up_maps[m]) for m in masks],
        rank,
    )
    back = jnp.concatenate(
        sum_over("narrow", [part_back[:, :token_count], part_back[:, token_count:]]), axis=1
    )
    grads = {}

    def down_gradients(chosen):
        keys = [(m, p) for m in chosen for p in range(parts)]
        last = [m & orders[p][-1] for m, p in keys]
        results = gradient_chunks(
            token_codes,
            token_rewards,
            back,
            training_hidden_input,
            mate_rows,
            [
                (m * owner_totals + p * part_adapters, jnp.bfloat16 if sends else jnp.float32)
                for (m, p), sends in zip(keys, last)
            ],
            part_adapters,
        )
        grads.update(zip(keys, results))

    far = [m for m in masks if m.bit_count() > 1]
    near = [m for m in masks if m.bit_count() == 1]
    for chosen in (far, near, [0]):
        if chosen:
            down_gradients(chosen)
    for p, order in enumerate(orders):
        held = list(masks)
        for bit in reversed(order):
            sent = [m for m in held if m & bit]
            held = [m for m in held if not m & bit]
            for m in sorted(sent, key=lambda v: -v.bit_count()):
                arrived = swap(grads[m, p].astype(jnp.bfloat16), "wide", bit)
                grads[m ^ bit, p] = grads[m ^ bit, p] + arrived.astype(jnp.float32)
    grad_down = jnp.concatenate([grads[0, p] for p in range(parts)])

    def down_chunks(chosen):
        return [
            (m * owner_totals + p * part_adapters, down_parts[m, p])
            for m in chosen
            for p in range(parts)
        ]

    part_hidden, part_rank = project_tokens(
        token_codes,
        training_hidden_input,
        mate_rows,
        [(0, flattened_down)] + down_chunks(near),
        rank,
        padded_codes,
        chip_slices,
    )
    if far:
        more_hidden, more_rank = project_tokens(
            token_codes,
            training_hidden_input,
            mate_rows,
            down_chunks(far),
            rank,
            padded_codes,
            chip_slices,
        )
        part_hidden, part_rank = part_hidden + more_hidden, part_rank + more_rank
    first, second = sum_over(
        "narrow",
        [
            part_hidden[:, :token_count],
            jnp.concatenate([part_hidden[:, token_count:], part_rank], axis=1),
        ],
    )
    hidden = jnp.concatenate([first, second[:, :token_count]], axis=1)
    decode_rank = second[:, token_count : token_count + 2 * row_count].astype(jnp.bfloat16)
    up_results = gradient_chunks(
        token_codes,
        token_rewards,
        hidden,
        cotangent,
        mate_cotangent,
        [(m * owner_totals, jnp.bfloat16 if m else jnp.float32) for m in masks],
        owner_totals,
    )
    grad_up = up_results[0]
    for m, result in zip(masks[1:], up_results[1:]):
        grad_up = grad_up + swap(result, "wide", m).astype(jnp.float32)

    delta = jnp.zeros((2 * row_count, up_width), jnp.float32)
    for m in masks:
        codes = m * owner_totals + jnp.arange(owner_totals, dtype=jnp.int32)
        chosen = (row_codes[None, :] == codes[:, None]).astype(jnp.bfloat16)
        spread = (chosen[:, None, :] * decode_rank[None, :, :]).reshape(-1, 2 * row_count)
        delta = delta + jnp.einsum(
            "ab,ak->bk", spread, up_maps[m], preferred_element_type=jnp.float32
        )
    delta = (ADAPTER_SCALE * delta).astype(jnp.bfloat16)
    own_delta = delta[:row_count] + swap(delta[row_count:], "wide", core_bit)
    fresh_keys = jnp.dot(
        decode_hidden_input, key_matrix, preferred_element_type=jnp.float32
    ).astype(jnp.bfloat16)
    base_values = jnp.dot(decode_hidden_input, value_matrix, preferred_element_type=jnp.float32)
    cached, own_weight = attend_cached(
        queries, cached_key_rows, cached_value_rows, lengths, fresh_keys
    )
    cached, own_weight, base_values = lax.optimization_barrier((cached, own_weight, base_values))
    fresh_values = (base_values + own_delta.astype(jnp.float32)).astype(jnp.bfloat16)
    kv_local = up_width // HEAD_SIZE
    attended = cached + own_weight.astype(jnp.float32)[..., None] * fresh_values.reshape(
        row_count, kv_local, 1, HEAD_SIZE
    ).astype(jnp.float32)
    return (
        attended.reshape(row_count, -1).astype(jnp.bfloat16),
        fresh_values,
        grad_down.reshape(adapter_down_map.shape),
        grad_up.reshape(adapter_up_map.shape),
    )


def solution(mesh):
    return jax.shard_map(
        per_device,
        mesh=mesh,
        in_specs=(
            P("wide", None),
            P("wide", "narrow"),
            P("wide", None, "narrow"),
            P("wide", None, "narrow"),
            P("wide"),
            P("wide"),
            P(None, "narrow"),
            P(None, "narrow"),
            P("wide", None, "narrow"),
            P("wide", None, "narrow"),
            P("wide", "narrow"),
            P("wide", "narrow"),
            P("wide"),
            P("wide"),
        ),
        out_specs=(
            P("wide", "narrow"),
            P("wide", "narrow"),
            P("wide", None, "narrow"),
            P("wide", None, "narrow"),
        ),
        check_vma=False,
    )
```

```python
import functools
import math

import jax
import jax.numpy as jnp
from jax import lax
from jax.experimental import pallas as pl
from jax.experimental.pallas import tpu as pltpu
from jax.sharding import PartitionSpec as P

HEADS = 64
KEY_VALUE_HEADS = 8
HEAD_SIZE = 128
CACHE = 256

ADAPTER_SCALE = 2.0
NEG_FILL = -1e30
VMEM_LIMIT = 60 * 1024 * 1024


def swap(array, axis, mask):
    count = lax.axis_size(axis)
    return lax.ppermute(array, axis, [(i, i ^ mask) for i in range(count)])


def axis_bits(axis):
    count = lax.axis_size(axis)
    assert count & (count - 1) == 0, "axis size"
    return [1 << k for k in range(count.bit_length() - 1)]


def highest_in(order, mask):
    return [bit for bit in order if bit & mask][-1]


def largest_tile(length, limit):
    tile = length
    while tile > limit and tile % 2 == 0:
        tile //= 2
    return tile


def pick(codes, products, chunk_bases, rank, adapters):
    total = jnp.zeros((rank, products.shape[1]), jnp.float32)
    for k, base in enumerate(chunk_bases):
        for j in range(adapters):
            first = (k * adapters + j) * rank
            total += jnp.where(codes == base + j, products[first : first + rank], 0.0)
    return total


def spread(codes, values, chunk_bases, adapters, out_ref):
    rank = values.shape[0]
    for k, base in enumerate(chunk_bases):
        for j in range(adapters):
            first = (k * adapters + j) * rank
            out_ref[first : first + rank, :] = jnp.where(codes == base + j, values, 0.0).astype(
                out_ref.dtype
            )


def join(maps, joined_ref):
    rows = maps[0].shape[0]
    for k, chunk in enumerate(maps):
        joined_ref[k * rows : (k + 1) * rows, :] = chunk[...]


def times_transposed(maps, tokens):
    return lax.dot_general(
        maps, tokens, (((1,), (1,)), ((), ())), preferred_element_type=jnp.float32
    )


def token_kernel(chunk_bases, rank, adapters, own_tiles, waits, codes_ref, own_ref, mate_ref, *refs):
    maps = refs[: len(chunk_bases)]
    out_ref, joined_ref = refs[len(chunk_bases) + waits :]
    step = pl.program_id(0)

    @pl.when(step == 0)
    def _():
        join(maps, joined_ref)

    def project(tokens_ref):
        products = times_transposed(joined_ref[...], tokens_ref[...])
        out_ref[...] = pick(codes_ref[...], products, chunk_bases, rank, adapters)

    pl.when(step < own_tiles)(lambda: project(own_ref))
    pl.when(step >= own_tiles)(lambda: project(mate_ref))


def project_tokens(codes, own, mate, mate_column, chunks, rank, after=()):
    token_count, width = own.shape
    tile = largest_tile(token_count, 512)
    own_tiles = token_count // tile
    chunk_rows = chunks[0][1].shape[0]
    map_rows = len(chunks) * chunk_rows
    return pl.pallas_call(
        functools.partial(
            token_kernel,
            [base for base, _ in chunks],
            rank,
            chunk_rows // rank,
            own_tiles,
            len(after),
        ),
        grid=(2 * own_tiles,),
        in_specs=[
            pl.BlockSpec((1, tile), lambda i: (0, i)),
            pl.BlockSpec((tile, width), lambda i: (jnp.minimum(i, own_tiles - 1), 0)),
            pl.BlockSpec((tile, width), lambda i: (jnp.maximum(i - own_tiles, 0), mate_column)),
        ]
        + [pl.BlockSpec((chunk_rows, width), lambda i: (0, 0)) for _ in chunks]
        + [pl.BlockSpec(memory_space=pl.ANY) for _ in after],
        out_specs=pl.BlockSpec((rank, tile), lambda i: (0, i)),
        out_shape=jax.ShapeDtypeStruct((rank, 2 * token_count), jnp.float32),
        scratch_shapes=[pltpu.VMEM((map_rows, width), jnp.bfloat16)],
        compiler_params=pltpu.CompilerParams(vmem_limit_bytes=VMEM_LIMIT),
        cost_estimate=pl.CostEstimate(
            flops=4 * token_count * width * map_rows,
            bytes_accessed=4 * token_count * width + 2 * map_rows * width,
            transcendentals=0,
        ),
    )(codes, own, mate, *[chunk for _, chunk in chunks], *after)


def row_kernel(chunk_bases, rank, adapters, waits, codes_ref, own_ref, mate_ref, *refs):
    maps = refs[: len(chunk_bases)]
    out_ref, rows_ref = refs[len(chunk_bases) + waits :]
    count = own_ref.shape[0]
    rows_ref[:count, :] = own_ref[...]
    rows_ref[count:, :] = mate_ref[...]
    total = jnp.zeros(out_ref.shape, jnp.float32)
    for base, chunk in zip(chunk_bases, maps):
        products = times_transposed(chunk[...], rows_ref[...])
        total += pick(codes_ref[...], products, [base], rank, adapters)
    out_ref[...] = total


def project_rows(codes, own, mate, mate_row, chunks, rank, after=()):
    row_count, width = own.shape
    chunk_rows = chunks[0][1].shape[0]
    return pl.pallas_call(
        functools.partial(
            row_kernel, [base for base, _ in chunks], rank, chunk_rows // rank, len(after)
        ),
        grid=(1,),
        in_specs=[
            pl.BlockSpec((1, 2 * row_count), lambda i: (0, 0)),
            pl.BlockSpec((row_count, width), lambda i: (0, 0)),
            pl.BlockSpec((row_count, width), lambda i: (mate_row, 0)),
        ]
        + [pl.BlockSpec((chunk_rows, width), lambda i: (0, 0)) for _ in chunks]
        + [pl.BlockSpec(memory_space=pl.ANY) for _ in after],
        out_specs=pl.BlockSpec((rank, 2 * row_count), lambda i: (0, 0)),
        out_shape=jax.ShapeDtypeStruct((rank, 2 * row_count), jnp.float32),
        scratch_shapes=[pltpu.VMEM((2 * row_count, width), jnp.bfloat16)],
        compiler_params=pltpu.CompilerParams(vmem_limit_bytes=VMEM_LIMIT),
        cost_estimate=pl.CostEstimate(
            flops=4 * row_count * width * chunk_rows * len(chunks),
            bytes_accessed=2 * width * chunk_rows * len(chunks),
            transcendentals=0,
        ),
    )(codes, own, mate, *[chunk for _, chunk in chunks], *after)


def delta_kernel(chunk_bases, adapters, codes_ref, rank_ref, *refs):
    maps = refs[: len(chunk_bases)]
    out_ref, spread_ref = refs[len(chunk_bases) :]
    values = rank_ref[...].astype(jnp.bfloat16).astype(jnp.float32)
    total = jnp.zeros(out_ref.shape, jnp.float32)
    for base, chunk in zip(chunk_bases, maps):
        spread(codes_ref[...], values, [base], adapters, spread_ref)
        total += lax.dot_general(
            spread_ref[...].T.astype(jnp.bfloat16),
            chunk[...],
            (((1,), (0,)), ((), ())),
            preferred_element_type=jnp.float32,
        )
    out_ref[...] = (ADAPTER_SCALE * total).astype(out_ref.dtype)


def row_deltas(codes, ranks, chunks):
    rank, row_count = ranks.shape
    chunk_rows, width = chunks[0][1].shape
    return pl.pallas_call(
        functools.partial(delta_kernel, [base for base, _ in chunks], chunk_rows // rank),
        out_shape=jax.ShapeDtypeStruct((row_count, width), jnp.bfloat16),
        scratch_shapes=[pltpu.VMEM((chunk_rows, row_count), jnp.float32)],
        compiler_params=pltpu.CompilerParams(vmem_limit_bytes=VMEM_LIMIT),
    )(codes, ranks, *[chunk for _, chunk in chunks])


def gradient_kernel(chunk_bases, adapters, waits, codes_ref, rewards_ref, factor_ref, *refs):
    own_ref, mate_ref = refs[:2]
    outs = refs[2 + waits : -1]
    spread_ref = refs[-1]
    token_count = own_ref.shape[0]

    @pl.when(pl.program_id(0) == 0)
    def _():
        scale = ADAPTER_SCALE * rewards_ref[...].astype(jnp.float32)
        scaled = (scale * factor_ref[...]).astype(jnp.bfloat16).astype(jnp.float32)
        spread(codes_ref[...], scaled, chunk_bases, adapters, spread_ref)

    total = jnp.dot(
        spread_ref[:, :token_count], own_ref[...], preferred_element_type=jnp.float32
    ) + jnp.dot(spread_ref[:, token_count:], mate_ref[...], preferred_element_type=jnp.float32)
    for k, out_ref in enumerate(outs):
        rows = out_ref.shape[0]
        out_ref[...] = total[k * rows : (k + 1) * rows].astype(out_ref.dtype)


def gradient_chunks(codes, rewards, factor, own, mate, mate_column, chunks, adapters, after=()):
    rank = factor.shape[0]
    token_count, width = own.shape
    tile = largest_tile(width, 512)
    rows = adapters * rank
    first_mate = mate_column * (width // tile)
    whole = lambda i: (0, 0)
    return pl.pallas_call(
        functools.partial(gradient_kernel, [base for base, _ in chunks], adapters, len(after)),
        grid=(width // tile,),
        in_specs=[
            pl.BlockSpec(codes.shape, whole),
            pl.BlockSpec(rewards.shape, whole),
            pl.BlockSpec(factor.shape, whole),
            pl.BlockSpec((token_count, tile), lambda i: (0, i)),
            pl.BlockSpec((token_count, tile), lambda i: (0, first_mate + i)),
        ]
        + [pl.BlockSpec(memory_space=pl.ANY) for _ in after],
        out_specs=[pl.BlockSpec((rows, tile), lambda i: (0, i)) for _ in chunks],
        out_shape=[jax.ShapeDtypeStruct((rows, width), dtype) for _, dtype in chunks],
        scratch_shapes=[pltpu.VMEM((len(chunks) * rows, 2 * token_count), jnp.bfloat16)],
        compiler_params=pltpu.CompilerParams(vmem_limit_bytes=VMEM_LIMIT),
        cost_estimate=pl.CostEstimate(
            flops=4 * token_count * width * rows * len(chunks),
            bytes_accessed=4 * token_count * width + 4 * rows * width * len(chunks),
            transcendentals=0,
        ),
    )(codes, rewards, factor, own, mate, *after)


def sum_over(axis, piece):
    for bit in axis_bits(axis):
        piece = piece + swap(piece, axis, bit)
    return piece


def attend_cached(queries, cached_key_rows, cached_value_rows, lengths, fresh_keys):
    row_count = queries.shape[0]
    kv_local = fresh_keys.shape[1] // HEAD_SIZE
    group = HEADS // KEY_VALUE_HEADS
    query_heads = queries.reshape(row_count, kv_local, group, HEAD_SIZE)
    key_heads = cached_key_rows.reshape(row_count, CACHE, kv_local, HEAD_SIZE)
    value_heads = cached_value_rows.reshape(row_count, CACHE, kv_local, HEAD_SIZE)
    inverse = 1.0 / math.sqrt(HEAD_SIZE)
    scores = (
        jnp.einsum("bhgd,bphd->bhgp", query_heads, key_heads, preferred_element_type=jnp.float32)
        * inverse
    )
    own_score = (
        jnp.einsum(
            "bhgd,bhd->bhg",
            query_heads,
            fresh_keys.reshape(row_count, kv_local, HEAD_SIZE),
            preferred_element_type=jnp.float32,
        )
        * inverse
    )
    allowed = jnp.arange(CACHE, dtype=jnp.int32)[None, :] < lengths[:, None]
    scores = jnp.where(allowed[:, None, None, :], scores, NEG_FILL)
    highest = jnp.maximum(jnp.max(scores, axis=-1), own_score)
    cache_exp = jnp.exp(scores - highest[..., None])
    own_exp = jnp.exp(own_score - highest)
    denominator = jnp.sum(cache_exp, axis=-1) + own_exp
    cache_weight = (cache_exp / denominator[..., None]).astype(jnp.bfloat16)
    own_weight = (own_exp / denominator).astype(jnp.bfloat16)
    attended = jnp.einsum(
        "bhgp,bphd->bhgd", cache_weight, value_heads, preferred_element_type=jnp.float32
    )
    return attended, own_weight


def per_device(
    decode_hidden_input,
    queries,
    cached_key_rows,
    cached_value_rows,
    lengths,
    decode_adapter_index,
    key_matrix,
    value_matrix,
    adapter_down_map,
    adapter_up_map,
    training_hidden_input,
    cotangent,
    training_adapter_index,
    rewards,
):
    core_bit, *chip_bits = axis_bits("wide")
    masks = [m for m in range(lax.axis_size("wide")) if not m & core_bit]
    me = lax.axis_index("wide")
    owner_totals, rank, down_width = adapter_down_map.shape
    up_width = adapter_up_map.shape[2]
    row_count = decode_hidden_input.shape[0]
    token_count = training_hidden_input.shape[0]
    parts = len(chip_bits) if owner_totals % len(chip_bits) == 0 else 1
    orders = [chip_bits[p:] + chip_bits[:p] for p in range(parts)]
    part_adapters = owner_totals // parts
    part_rows = part_adapters * rank

    flattened_down = adapter_down_map.reshape(-1, down_width)
    flattened_up = adapter_up_map.reshape(-1, up_width)

    up_maps = {m: swap(flattened_up, "wide", m) if m else flattened_up for m in masks}
    down_parts = {}
    for p, order in enumerate(orders):
        down_parts[0, p] = flattened_down[p * part_rows : (p + 1) * part_rows]
        held = [0]
        for bit in order:
            for m in held:
                down_parts[m | bit, p] = swap(down_parts[m, p], "wide", bit)
            held = held + [m | bit for m in held]

    numbers = jnp.concatenate([training_adapter_index, rewards, decode_adapter_index])
    mate_numbers = swap(numbers, "wide", core_bit)
    decode_slice = lax.dynamic_slice_in_dim(
        decode_hidden_input, lax.axis_index("narrow") * down_width, down_width, 1
    )
    own_all = jnp.concatenate(
        [
            jnp.concatenate([training_hidden_input, cotangent], axis=1),
            jnp.pad(decode_slice, ((0, 0), (0, up_width))),
        ]
    )
    mate_all = swap(own_all, "wide", core_bit)
    assert token_count % row_count == 0 and down_width % up_width == 0, "block sizes"

    def codes_of(ids):
        return (((ids // owner_totals) ^ me) * owner_totals + ids % owner_totals)[None, :]

    token_codes = codes_of(
        jnp.concatenate([training_adapter_index, mate_numbers[:token_count]])
    )
    token_rewards = jnp.concatenate([rewards, mate_numbers[token_count : 2 * token_count]])[
        None, :
    ]
    row_codes = codes_of(
        jnp.concatenate([decode_adapter_index, mate_numbers[2 * token_count :]])
    )
    up_chunks = [(m * owner_totals, up_maps[m]) for m in masks]
    up_column = down_width // up_width

    def down_chunks(chosen):
        return [
            (m * owner_totals + p * part_adapters, down_parts[m, p])
            for m in chosen
            for p in range(parts)
        ]

    part_back = project_tokens(token_codes, cotangent, mate_all, up_column, up_chunks, rank)
    back = sum_over("narrow", part_back)
    grads = {}

    def down_gradients(chosen, after):
        keys = [(m, p) for m in chosen for p in range(parts)]
        results = gradient_chunks(
            token_codes,
            token_rewards,
            back,
            training_hidden_input,
            mate_all,
            0,
            [
                (
                    m * owner_totals + p * part_adapters,
                    jnp.bfloat16 if m & orders[p][-1] else jnp.float32,
                )
                for m, p in keys
            ],
            part_adapters,
            after,
        )
        grads.update(zip(keys, results))
        return results[:1]

    far = [m for m in masks if m.bit_count() > 1]
    near = [m for m in masks if m.bit_count() == 1]
    order_token = down_gradients(far, ()) if far else ()
    order_token = down_gradients(near, order_token)

    part_hidden = project_tokens(
        token_codes,
        training_hidden_input,
        mate_all,
        0,
        down_chunks([0] + near),
        rank,
        order_token,
    )
    part_ranks = project_rows(
        row_codes,
        decode_slice,
        mate_all,
        token_count // row_count,
        down_chunks(masks),
        rank,
        (part_hidden,),
    )
    if far:
        part_hidden = part_hidden + project_tokens(
            token_codes,
            training_hidden_input,
            mate_all,
            0,
            down_chunks(far),
            rank,
            (part_ranks,),
        )
    down_gradients([0], (part_hidden,))
    hidden = sum_over("narrow", part_hidden)
    decode_ranks = sum_over("narrow", part_ranks)

    for p, order in enumerate(orders):
        held = list(masks)
        for bit in reversed(order):
            sent = [m for m in held if m & bit]
            held = [m for m in held if not m & bit]
            for m in sorted(sent, key=lambda v: -v.bit_count()):
                arrived = swap(grads[m, p].astype(jnp.bfloat16), "wide", bit)
                grads[m ^ bit, p] = grads[m ^ bit, p] + arrived.astype(jnp.float32)
    grad_down = jnp.concatenate([grads[0, p] for p in range(parts)])

    up_results = gradient_chunks(
        token_codes,
        token_rewards,
        hidden,
        cotangent,
        mate_all,
        up_column,
        [(m * owner_totals, jnp.bfloat16 if m else jnp.float32) for m in masks],
        owner_totals,
    )
    grad_up = up_results[0]
    for m, result in zip(masks[1:], up_results[1:]):
        grad_up = grad_up + swap(result, "wide", m).astype(jnp.float32)

    delta = row_deltas(row_codes, decode_ranks, up_chunks)
    own_delta = delta[:row_count] + swap(delta[row_count:], "wide", core_bit)
    decode_hidden_input, queries, part_back = lax.optimization_barrier(
        (decode_hidden_input, queries, part_back)
    )
    fresh_keys = jnp.dot(
        decode_hidden_input, key_matrix, preferred_element_type=jnp.float32
    ).astype(jnp.bfloat16)
    base_values = jnp.dot(decode_hidden_input, value_matrix, preferred_element_type=jnp.float32)
    cached, own_weight = attend_cached(
        queries, cached_key_rows, cached_value_rows, lengths, fresh_keys
    )
    cached, own_weight, base_values = lax.optimization_barrier((cached, own_weight, base_values))
    fresh_values = (base_values + own_delta.astype(jnp.float32)).astype(jnp.bfloat16)
    kv_local = up_width // HEAD_SIZE
    attended = cached + own_weight.astype(jnp.float32)[..., None] * fresh_values.reshape(
        row_count, kv_local, 1, HEAD_SIZE
    ).astype(jnp.float32)
    return (
        attended.reshape(row_count, -1).astype(jnp.bfloat16),
        fresh_values,
        grad_down.reshape(adapter_down_map.shape),
        grad_up.reshape(adapter_up_map.shape),
    )


def solution(mesh):
    return jax.shard_map(
        per_device,
        mesh=mesh,
        in_specs=(
            P("wide", None),
            P("wide", "narrow"),
            P("wide", None, "narrow"),
            P("wide", None, "narrow"),
            P("wide"),
            P("wide"),
            P(None, "narrow"),
            P(None, "narrow"),
            P("wide", None, "narrow"),
            P("wide", None, "narrow"),
            P("wide", "narrow"),
            P("wide", "narrow"),
            P("wide"),
            P("wide"),
        ),
        out_specs=(
            P("wide", "narrow"),
            P("wide", "narrow"),
            P("wide", None, "narrow"),
            P("wide", None, "narrow"),
        ),
        check_vma=False,
    )
```

```python
import functools
import math

import jax
import jax.numpy as jnp
from jax import lax
from jax.experimental import pallas as pl
from jax.experimental.pallas import tpu as pltpu
from jax.sharding import PartitionSpec as P

HEADS = 64
KEY_VALUE_HEADS = 8
HEAD_SIZE = 128
CACHE = 256

ADAPTER_SCALE = 2.0
NEG_FILL = -1e30
VMEM_LIMIT = 60 * 1024 * 1024


def swap(array, axis, mask):
    count = lax.axis_size(axis)
    return lax.ppermute(array, axis, [(i, i ^ mask) for i in range(count)])


def axis_bits(axis):
    count = lax.axis_size(axis)
    assert count & (count - 1) == 0, "axis size"
    return [1 << k for k in range(count.bit_length() - 1)]


def highest_in(order, mask):
    return [bit for bit in order if bit & mask][-1]


def largest_tile(length, limit):
    tile = length
    while tile > limit and tile % 2 == 0:
        tile //= 2
    return tile


def code_list(chunks, rank):
    return [base + j for base, rows in chunks for j in range(rows // rank)]


def pick(codes, products, row_codes, rank):
    total = jnp.zeros((rank, products.shape[1]), jnp.float32)
    for k, code in enumerate(row_codes):
        total += jnp.where(codes == code, products[k * rank : (k + 1) * rank], 0.0)
    return total


def spread(codes, values, row_codes, out_ref):
    rank = values.shape[0]
    for k, code in enumerate(row_codes):
        out_ref[k * rank : (k + 1) * rank, :] = jnp.where(codes == code, values, 0.0).astype(
            out_ref.dtype
        )


def join(maps, joined_ref):
    first = 0
    for chunk in maps:
        joined_ref[first : first + chunk.shape[0], :] = chunk[...]
        first += chunk.shape[0]


def times_transposed(maps, tokens):
    return lax.dot_general(
        maps, tokens, (((1,), (1,)), ((), ())), preferred_element_type=jnp.float32
    )


def token_kernel(
    map_codes, rank, own_tiles, has_rows, map_count, codes_ref, own_ref, mate_ref, *refs
):
    refs = list(refs)
    row_refs = [refs.pop(0) for _ in range(2 * has_rows)]
    maps = refs[:map_count]
    out_ref, joined_ref, *rest = refs[-2 - has_rows :]
    step = pl.program_id(0)

    @pl.when(step == 0)
    def _():
        join(maps, joined_ref)

    def project(tokens):
        products = times_transposed(joined_ref[...], tokens)
        codes = codes_ref[:, : tokens.shape[0]]
        return pick(codes, products, map_codes, rank)

    def store(total):
        out_ref[...] = total

    pl.when(step < own_tiles)(lambda: store(project(own_ref[...])))
    pl.when((step >= own_tiles) & (step < 2 * own_tiles))(lambda: store(project(mate_ref[...])))
    if has_rows:
        rows_ref = rest[0]

        @pl.when(step == 2 * own_tiles)
        def _():
            rows_ref[...] = jnp.zeros_like(rows_ref)
            join(row_refs, rows_ref)
            store(jnp.zeros_like(out_ref))
            out_ref[:, : rows_ref.shape[0]] += project(rows_ref[...])


def token_tile(token_count):
    return largest_tile(token_count, 512)


def project_tokens(codes, own, mate, chunks, rank, rows=(), after=()):
    token_count, width = own.shape
    tile = token_tile(token_count)
    own_tiles = token_count // tile
    steps = 2 * own_tiles + bool(rows)
    map_rows = sum(chunk.shape[0] for _, chunk in chunks)
    scratch = [pltpu.VMEM((map_rows, width), jnp.bfloat16)]
    if rows:
        padded = -(-2 * rows[0].shape[0] // 128) * 128
        assert padded <= tile, "row count"
        scratch.append(pltpu.VMEM((padded, width), jnp.bfloat16))
    result_spec = pl.BlockSpec((rank, tile), lambda i: (0, i))
    whole = lambda i: (0, 0)
    last = own_tiles - 1
    return pl.pallas_call(
        functools.partial(
            token_kernel,
            code_list([(base, chunk.shape[0]) for base, chunk in chunks], rank),
            rank,
            own_tiles,
            bool(rows),
            len(chunks),
        ),
        grid=(steps,),
        in_specs=[
            pl.BlockSpec((1, tile), lambda i: (0, i)),
            pl.BlockSpec((tile, width), lambda i: (jnp.minimum(i, last), 0)),
            pl.BlockSpec((tile, width), lambda i: (jnp.clip(i - own_tiles, 0, last), 0)),
        ]
        + [pl.BlockSpec(a.shape, whole) for a in rows]
        + [pl.BlockSpec(chunk.shape, whole) for _, chunk in chunks]
        + [pl.BlockSpec(memory_space=pl.ANY) for _ in after],
        out_specs=result_spec,
        out_shape=jax.ShapeDtypeStruct((rank, steps * tile), jnp.float32),
        scratch_shapes=scratch,
        compiler_params=pltpu.CompilerParams(vmem_limit_bytes=VMEM_LIMIT),
        cost_estimate=pl.CostEstimate(flops=1, bytes_accessed=1, transcendentals=0),
    )(codes, own, mate, *rows, *[chunk for _, chunk in chunks], *after)


def delta_kernel(chunk_codes, codes_ref, rank_ref, *refs):
    maps = refs[: len(chunk_codes)]
    out_ref, spread_ref = refs[-2:]
    count = codes_ref.shape[1]
    values = rank_ref[:, :count].astype(jnp.bfloat16).astype(jnp.float32)
    total = jnp.zeros(out_ref.shape, jnp.float32)
    for map_codes, chunk in zip(chunk_codes, maps):
        spread(codes_ref[...], values, map_codes, spread_ref)
        total += lax.dot_general(
            spread_ref[...].T.astype(jnp.bfloat16),
            chunk[...],
            (((1,), (0,)), ((), ())),
            preferred_element_type=jnp.float32,
        )
    out_ref[...] = (ADAPTER_SCALE * total).astype(out_ref.dtype)


def row_deltas(codes, ranks, first, width_of_ranks, chunks, after=()):
    rank = ranks.shape[0]
    row_count = codes.shape[1]
    chunk_rows, width = chunks[0][1].shape
    whole = lambda i: (0, 0)
    return pl.pallas_call(
        functools.partial(
            delta_kernel, [code_list([(base, chunk_rows)], rank) for base, _ in chunks]
        ),
        grid=(1,),
        in_specs=[
            pl.BlockSpec(codes.shape, whole),
            pl.BlockSpec((rank, width_of_ranks), lambda i: (0, first // width_of_ranks)),
        ]
        + [pl.BlockSpec((chunk_rows, width), whole) for _ in chunks]
        + [pl.BlockSpec(memory_space=pl.ANY) for _ in after],
        out_specs=pl.BlockSpec((row_count, width), whole),
        out_shape=jax.ShapeDtypeStruct((row_count, width), jnp.bfloat16),
        scratch_shapes=[pltpu.VMEM((chunk_rows, row_count), jnp.float32)],
        compiler_params=pltpu.CompilerParams(vmem_limit_bytes=VMEM_LIMIT),
    )(codes, ranks, *[chunk for _, chunk in chunks], *after)


def gradient_kernel(row_codes, rows, arrived_counts, waits, joined, *refs):
    codes_ref, rewards_ref, factor_ref, own_ref, mate_ref = refs[:5]
    refs = list(refs[5:])
    arrived = [[refs.pop(0) for _ in range(count)] for count in arrived_counts]
    outs = refs[waits:-1]
    spread_ref = refs[-1]
    token_count = own_ref.shape[0]

    @pl.when(pl.program_id(0) == 0)
    def _():
        scale = ADAPTER_SCALE * rewards_ref[...].astype(jnp.float32)
        scaled = (scale * factor_ref[...]).astype(jnp.bfloat16).astype(jnp.float32)
        spread(codes_ref[...], scaled, row_codes, spread_ref)

    total = jnp.dot(
        spread_ref[:, :token_count], own_ref[...], preferred_element_type=jnp.float32
    ) + jnp.dot(spread_ref[:, token_count:], mate_ref[...], preferred_element_type=jnp.float32)
    for k in range(len(arrived)):
        piece = total[k * rows : (k + 1) * rows]
        for ref in arrived[k]:
            piece += ref[...].astype(jnp.float32)
        if joined:
            outs[0][k * rows : (k + 1) * rows, :] = piece
        else:
            outs[k][...] = piece.astype(outs[k].dtype)


def gradient_chunks(
    codes, rewards, factor, own, mate, chunks, adapters, joined=False, after=()
):
    rank = factor.shape[0]
    token_count, width = own.shape
    tile = largest_tile(width, 512)
    rows = adapters * rank
    out_rows = [rows * len(chunks)] if joined else [rows] * len(chunks)
    arrived = [a for _, arrays in chunks for a in arrays]
    whole = lambda i: (0, 0)
    across = lambda i: (0, i)
    return pl.pallas_call(
        functools.partial(
            gradient_kernel,
            code_list([(base, rows) for base, _ in chunks], rank),
            rows,
            [len(arrays) for _, arrays in chunks],
            len(after),
            joined,
        ),
        grid=(width // tile,),
        in_specs=[
            pl.BlockSpec((1, 2 * token_count), whole),
            pl.BlockSpec(rewards.shape, whole),
            pl.BlockSpec((rank, 2 * token_count), whole),
            pl.BlockSpec((token_count, tile), across),
            pl.BlockSpec((token_count, tile), across),
        ]
        + [pl.BlockSpec((rows, tile), across) for _ in arrived]
        + [pl.BlockSpec(memory_space=pl.ANY) for _ in after],
        out_specs=[pl.BlockSpec((r, tile), across) for r in out_rows],
        out_shape=[
            jax.ShapeDtypeStruct((r, width), jnp.bfloat16 if base else jnp.float32)
            for r, (base, _) in zip(out_rows, chunks)
        ],
        scratch_shapes=[pltpu.VMEM((len(chunks) * rows, 2 * token_count), jnp.bfloat16)],
        compiler_params=pltpu.CompilerParams(vmem_limit_bytes=VMEM_LIMIT),
        cost_estimate=pl.CostEstimate(flops=1, bytes_accessed=1, transcendentals=0),
    )(codes, rewards, factor, own, mate, *arrived, *after)


def finish_kernel(start_ref, *refs):
    arrived, out_ref = refs[:-1], refs[-1]
    rows = arrived[0].shape[0]
    for p, ref in enumerate(arrived):
        part = slice(p * rows, (p + 1) * rows)
        out_ref[part, :] = start_ref[part, :] + ref[...].astype(jnp.float32)


def finish(start, arrived):
    rows, width = start.shape
    tile = largest_tile(width, 512)
    across = lambda i: (0, i)
    return pl.pallas_call(
        finish_kernel,
        grid=(width // tile,),
        in_specs=[pl.BlockSpec((a.shape[0], tile), across) for a in (start, *arrived)],
        out_specs=pl.BlockSpec((rows, tile), across),
        out_shape=jax.ShapeDtypeStruct(start.shape, start.dtype),
        compiler_params=pltpu.CompilerParams(vmem_limit_bytes=VMEM_LIMIT),
    )(start, *arrived)


def wait_for(array, *others):
    return lax.optimization_barrier((array, *others))[0]


def sum_over(axis, piece, waits=()):
    for k, bit in enumerate(axis_bits(axis)):
        arrived = swap(piece, axis, bit)
        if k < len(waits):
            arrived = wait_for(arrived, *waits[k])
        piece = piece + arrived
    return piece


def attend_cached(queries, cached_key_rows, cached_value_rows, lengths, fresh_keys):
    row_count = queries.shape[0]
    kv_local = fresh_keys.shape[1] // HEAD_SIZE
    group = HEADS // KEY_VALUE_HEADS
    query_heads = queries.reshape(row_count, kv_local, group, HEAD_SIZE)
    key_heads = cached_key_rows.reshape(row_count, CACHE, kv_local, HEAD_SIZE)
    value_heads = cached_value_rows.reshape(row_count, CACHE, kv_local, HEAD_SIZE)
    inverse = 1.0 / math.sqrt(HEAD_SIZE)
    scores = (
        jnp.einsum("bhgd,bphd->bhgp", query_heads, key_heads, preferred_element_type=jnp.float32)
        * inverse
    )
    own_score = (
        jnp.einsum(
            "bhgd,bhd->bhg",
            query_heads,
            fresh_keys.reshape(row_count, kv_local, HEAD_SIZE),
            preferred_element_type=jnp.float32,
        )
        * inverse
    )
    allowed = jnp.arange(CACHE, dtype=jnp.int32)[None, :] < lengths[:, None]
    scores = jnp.where(allowed[:, None, None, :], scores, NEG_FILL)
    highest = jnp.maximum(jnp.max(scores, axis=-1), own_score)
    cache_exp = jnp.exp(scores - highest[..., None])
    own_exp = jnp.exp(own_score - highest)
    denominator = jnp.sum(cache_exp, axis=-1) + own_exp
    cache_weight = (cache_exp / denominator[..., None]).astype(jnp.bfloat16)
    own_weight = (own_exp / denominator).astype(jnp.bfloat16)
    attended = jnp.einsum(
        "bhgp,bphd->bhgd", cache_weight, value_heads, preferred_element_type=jnp.float32
    )
    return attended, own_weight


def per_device(
    decode_hidden_input,
    queries,
    cached_key_rows,
    cached_value_rows,
    lengths,
    decode_adapter_index,
    key_matrix,
    value_matrix,
    adapter_down_map,
    adapter_up_map,
    training_hidden_input,
    cotangent,
    training_adapter_index,
    rewards,
):
    core_bit, *chip_bits = axis_bits("wide")
    masks = [m for m in range(lax.axis_size("wide")) if not m & core_bit]
    me = lax.axis_index("wide")
    owner_totals, rank, down_width = adapter_down_map.shape
    up_width = adapter_up_map.shape[2]
    row_count = decode_hidden_input.shape[0]
    token_count = training_hidden_input.shape[0]
    parts = len(chip_bits) if owner_totals % len(chip_bits) == 0 else 1
    orders = [chip_bits[p:] + chip_bits[:p] for p in range(parts)]
    part_adapters = owner_totals // parts
    part_rows = part_adapters * rank

    flattened_down = adapter_down_map.reshape(-1, down_width)
    flattened_up = adapter_up_map.reshape(-1, up_width)

    far = [m for m in masks if m.bit_count() > 1]
    near = [m for m in masks if m.bit_count() == 1]

    numbers = jnp.concatenate([training_adapter_index, rewards, decode_adapter_index])
    mate_numbers = swap(numbers, "wide", core_bit)
    mate_cotangent = swap(wait_for(cotangent, mate_numbers), "wide", core_bit)
    up_maps = {0: flattened_up}
    for m in near:
        up_maps[m] = swap(flattened_up, "wide", m)
    for m in far:
        up_maps[m] = swap(wait_for(flattened_up, mate_numbers), "wide", m)
    mate_hidden = swap(wait_for(training_hidden_input, up_maps[near[0]]), "wide", core_bit)
    down_parts = {}
    for p, order in enumerate(orders):
        own_part = flattened_down[p * part_rows : (p + 1) * part_rows]
        held = []
        for bit in order:
            for m in held:
                down_parts[m | bit, p] = swap(down_parts[m, p], "wide", bit)
            sent = wait_for(own_part, *[down_parts[m | bit, p] for m in held[-1:]])
            down_parts[bit, p] = swap(sent, "wide", bit)
            held = held + [bit] + [m | bit for m in held]
    first_maps = [down_parts[order[0], p] for p, order in enumerate(orders)]
    decode_slice = lax.dynamic_slice_in_dim(
        decode_hidden_input, lax.axis_index("narrow") * down_width, down_width, 1
    )

    def codes_of(ids):
        return (((ids // owner_totals) ^ me) * owner_totals + ids % owner_totals)[None, :]

    token_codes = codes_of(
        jnp.concatenate([training_adapter_index, mate_numbers[:token_count]])
    )
    token_rewards = jnp.concatenate([rewards, mate_numbers[token_count : 2 * token_count]])[
        None, :
    ]
    row_codes = codes_of(
        jnp.concatenate([decode_adapter_index, mate_numbers[2 * token_count :]])
    )
    tile = token_tile(token_count)
    all_codes = jnp.concatenate(
        [token_codes, jnp.pad(row_codes, ((0, 0), (0, tile - 2 * row_count)), constant_values=-1)],
        axis=1,
    )
    up_chunks = [(m * owner_totals, up_maps[m]) for m in masks]
    down_chunks = [(0, flattened_down)] + [
        (m * owner_totals + p * part_adapters, down_parts[m, p])
        for m in near + far
        for p in range(parts)
    ]

    hidden_rows = wait_for(decode_hidden_input, mate_numbers, *[up_maps[m] for m in near])
    fresh_keys = jnp.dot(
        hidden_rows, key_matrix, preferred_element_type=jnp.float32
    ).astype(jnp.bfloat16)
    base_values = jnp.dot(hidden_rows, value_matrix, preferred_element_type=jnp.float32)

    cached, own_weight = attend_cached(
        wait_for(queries, *[up_maps[m] for m in near]),
        cached_key_rows,
        cached_value_rows,
        lengths,
        fresh_keys,
    )

    part_back = project_tokens(
        token_codes,
        cotangent,
        mate_cotangent,
        up_chunks,
        rank,
        after=(*first_maps, mate_hidden, cached, base_values),
    )
    mate_slice = swap(wait_for(decode_slice, part_back), "wide", core_bit)
    back = sum_over("narrow", part_back)
    arrived = {(m, p): [] for m in masks for p in range(parts)}

    def level_gradients(level, after):
        keys = [
            (m, p)
            for m in far + near
            for p, order in enumerate(orders)
            if m & order[level] and not any(m & bit for bit in order[level + 1 :])
        ]
        results = gradient_chunks(
            token_codes,
            token_rewards,
            back,
            training_hidden_input,
            mate_hidden,
            [(m * owner_totals + p * part_adapters, arrived[m, p]) for m, p in keys],
            part_adapters,
            after=after,
        )
        for (m, p), result in zip(keys, results):
            bit = orders[p][level]
            arrived[m ^ bit, p].append(swap(result, "wide", bit))
        return results[:1]

    levels = list(reversed(range(len(chip_bits))))
    order_token = level_gradients(levels[0], ())

    part_hidden = project_tokens(
        all_codes,
        training_hidden_input,
        mate_hidden,
        down_chunks,
        rank,
        rows=(decode_slice, mate_slice),
        after=order_token,
    )

    order_token = (part_hidden,)
    for level in levels[1:]:
        order_token = level_gradients(level, order_token)
    (own_down,) = gradient_chunks(
        token_codes,
        token_rewards,
        back,
        training_hidden_input,
        mate_hidden,
        [(p * part_adapters, arrived[0, p][:-1]) for p in range(parts)],
        part_adapters,
        joined=True,
        after=order_token,
    )
    last_down = [arrived[0, p][-1] for p in range(parts)]
    grad_down = finish(own_down, last_down)

    hidden = sum_over("narrow", part_hidden, [order_token, (own_down,)])
    up_results = gradient_chunks(
        token_codes,
        token_rewards,
        hidden,
        cotangent,
        mate_cotangent,
        [(m * owner_totals, ()) for m in masks],
        owner_totals,
        after=(own_down,),
    )
    grad_up = grad_up_own = up_results[0]
    for m, result in zip(masks[1:], up_results[1:]):
        result = wait_for(result, *last_down)
        grad_up = grad_up + swap(result, "wide", m).astype(jnp.float32)

    delta = row_deltas(row_codes, hidden, 2 * token_count, tile, up_chunks, (grad_up_own,))
    own_delta = delta[:row_count] + swap(delta[row_count:], "wide", core_bit)
    fresh_values = (base_values + own_delta.astype(jnp.float32)).astype(jnp.bfloat16)
    kv_local = up_width // HEAD_SIZE
    attended = cached + own_weight.astype(jnp.float32)[..., None] * fresh_values.reshape(
        row_count, kv_local, 1, HEAD_SIZE
    ).astype(jnp.float32)
    return (
        attended.reshape(row_count, -1).astype(jnp.bfloat16),
        fresh_values,
        grad_down.reshape(adapter_down_map.shape),
        grad_up.reshape(adapter_up_map.shape),
    )


def solution(mesh):
    return jax.shard_map(
        per_device,
        mesh=mesh,
        in_specs=(
            P("wide", None),
            P("wide", "narrow"),
            P("wide", None, "narrow"),
            P("wide", None, "narrow"),
            P("wide"),
            P("wide"),
            P(None, "narrow"),
            P(None, "narrow"),
            P("wide", None, "narrow"),
            P("wide", None, "narrow"),
            P("wide", "narrow"),
            P("wide", "narrow"),
            P("wide"),
            P("wide"),
        ),
        out_specs=(
            P("wide", "narrow"),
            P("wide", "narrow"),
            P("wide", None, "narrow"),
            P("wide", None, "narrow"),
        ),
        check_vma=False,
    )
```

```python
import functools
import math

import jax
import jax.numpy as jnp
from jax import lax
from jax.experimental import pallas as pl
from jax.experimental.pallas import tpu as pltpu
from jax.sharding import PartitionSpec as P

HEADS = 64
KEY_VALUE_HEADS = 8
HEAD_SIZE = 128
CACHE = 256

ADAPTER_SCALE = 2.0
NEG_FILL = -1e30
VMEM_LIMIT = 48 * 1024 * 1024


def swap(array, axis, mask):
    count = lax.axis_size(axis)
    return lax.ppermute(array, axis, [(i, i ^ mask) for i in range(count)])


def axis_bits(axis):
    count = lax.axis_size(axis)
    assert count & (count - 1) == 0, "axis size"
    return [1 << k for k in range(count.bit_length() - 1)]


def highest_in(order, mask):
    return [bit for bit in order if bit & mask][-1]


def largest_tile(length, limit):
    tile = length
    while tile > limit and tile % 2 == 0:
        tile //= 2
    return tile


def code_list(chunks, rank):
    return [base + j for base, rows in chunks for j in range(rows // rank)]


def pick(codes, products, row_codes, rank):
    total = jnp.zeros((rank, products.shape[1]), jnp.float32)
    for k, code in enumerate(row_codes):
        total += jnp.where(codes == code, products[k * rank : (k + 1) * rank], 0.0)
    return total


def spread(codes, values, row_codes, out_ref):
    rank = values.shape[0]
    for k, code in enumerate(row_codes):
        out_ref[k * rank : (k + 1) * rank, :] = jnp.where(codes == code, values, 0.0).astype(
            out_ref.dtype
        )


def join(maps, joined_ref):
    first = 0
    for chunk in maps:
        joined_ref[first : first + chunk.shape[0], :] = chunk[...]
        first += chunk.shape[0]


def times_transposed(maps, tokens):
    return lax.dot_general(
        maps, tokens, (((1,), (1,)), ((), ())), preferred_element_type=jnp.float32
    )


def token_kernel(
    map_codes, rank, own_tiles, has_rows, has_start, map_count, codes_ref, own_ref, mate_ref, *refs
):
    refs = list(refs)
    row_refs = [refs.pop(0) for _ in range(2 * has_rows)]
    start_ref = refs.pop(0) if has_start else None
    maps = refs[:map_count]
    out_ref, joined_ref, *rest = refs[-2 - has_rows :]
    step = pl.program_id(0)

    @pl.when(step == 0)
    def _():
        join(maps, joined_ref)

    def project(tokens):
        products = times_transposed(joined_ref[...], tokens)
        codes = codes_ref[:, : tokens.shape[0]]
        return pick(codes, products, map_codes, rank)

    def store(total):
        out_ref[...] = total if start_ref is None else total + start_ref[...]

    pl.when(step < own_tiles)(lambda: store(project(own_ref[...])))
    pl.when((step >= own_tiles) & (step < 2 * own_tiles))(lambda: store(project(mate_ref[...])))
    if has_rows:
        rows_ref = rest[0]

        @pl.when(step == 2 * own_tiles)
        def _():
            rows_ref[...] = jnp.zeros_like(rows_ref)
            join(row_refs, rows_ref)
            store(jnp.zeros_like(out_ref))
            out_ref[:, : rows_ref.shape[0]] += project(rows_ref[...])


def token_tile(token_count, width=0):
    return largest_tile(token_count, 512 if width > 512 else 1024)


def project_tokens(codes, own, mate, chunks, rank, rows=(), start=None, after=()):
    token_count, width = own.shape
    tile = token_tile(token_count, width)
    own_tiles = token_count // tile
    steps = 2 * own_tiles + bool(rows)
    map_rows = sum(chunk.shape[0] for _, chunk in chunks)
    scratch = [pltpu.VMEM((map_rows, width), jnp.bfloat16)]
    if rows:
        padded = -(-2 * rows[0].shape[0] // 128) * 128
        assert padded <= tile, "row count"
        scratch.append(pltpu.VMEM((padded, width), jnp.bfloat16))
    result_spec = pl.BlockSpec((rank, tile), lambda i: (0, i))
    starts = [] if start is None else [start]
    whole = lambda i: (0, 0)
    last = own_tiles - 1
    return pl.pallas_call(
        functools.partial(
            token_kernel,
            code_list([(base, chunk.shape[0]) for base, chunk in chunks], rank),
            rank,
            own_tiles,
            bool(rows),
            bool(starts),
            len(chunks),
        ),
        grid=(steps,),
        in_specs=[
            pl.BlockSpec((1, tile), lambda i: (0, i)),
            pl.BlockSpec((tile, width), lambda i: (jnp.minimum(i, last), 0)),
            pl.BlockSpec((tile, width), lambda i: (jnp.clip(i - own_tiles, 0, last), 0)),
        ]
        + [pl.BlockSpec(a.shape, whole) for a in rows]
        + [result_spec for _ in starts]
        + [pl.BlockSpec(chunk.shape, whole) for _, chunk in chunks]
        + [pl.BlockSpec(memory_space=pl.ANY) for _ in after],
        out_specs=result_spec,
        out_shape=jax.ShapeDtypeStruct((rank, steps * tile), jnp.float32),
        scratch_shapes=scratch,
        compiler_params=pltpu.CompilerParams(vmem_limit_bytes=VMEM_LIMIT),
        cost_estimate=pl.CostEstimate(flops=1, bytes_accessed=1, transcendentals=0),
    )(codes, own, mate, *rows, *starts, *[chunk for _, chunk in chunks], *after)


def delta_kernel(chunk_codes, codes_ref, rank_ref, *refs):
    maps = refs[: len(chunk_codes)]
    own_ref, mate_ref, spread_ref = refs[-3:]
    count = codes_ref.shape[1]
    values = rank_ref[:, :count].astype(jnp.bfloat16).astype(jnp.float32)
    total = jnp.zeros((count, own_ref.shape[1]), jnp.float32)
    for map_codes, chunk in zip(chunk_codes, maps):
        spread(codes_ref[...], values, map_codes, spread_ref)
        total += lax.dot_general(
            spread_ref[...].T.astype(jnp.bfloat16),
            chunk[...],
            (((1,), (0,)), ((), ())),
            preferred_element_type=jnp.float32,
        )
    deltas = ADAPTER_SCALE * total
    own_ref[...] = deltas[: count // 2].astype(own_ref.dtype)
    mate_ref[...] = deltas[count // 2 :].astype(mate_ref.dtype)


def row_deltas(codes, ranks, first, width_of_ranks, chunks, after=()):
    rank = ranks.shape[0]
    row_count = codes.shape[1]
    chunk_rows, width = chunks[0][1].shape
    whole = lambda i: (0, 0)
    return pl.pallas_call(
        functools.partial(
            delta_kernel, [code_list([(base, chunk_rows)], rank) for base, _ in chunks]
        ),
        grid=(1,),
        in_specs=[
            pl.BlockSpec(codes.shape, whole),
            pl.BlockSpec((rank, width_of_ranks), lambda i: (0, first // width_of_ranks)),
        ]
        + [pl.BlockSpec((chunk_rows, width), whole) for _ in chunks]
        + [pl.BlockSpec(memory_space=pl.ANY) for _ in after],
        out_specs=[pl.BlockSpec((row_count // 2, width), whole)] * 2,
        out_shape=[jax.ShapeDtypeStruct((row_count // 2, width), jnp.bfloat16)] * 2,
        scratch_shapes=[pltpu.VMEM((chunk_rows, row_count), jnp.float32)],
        compiler_params=pltpu.CompilerParams(vmem_limit_bytes=VMEM_LIMIT),
    )(codes, ranks, *[chunk for _, chunk in chunks], *after)


def gradient_kernel(row_codes, waits, codes_ref, rewards_ref, factor_ref, own_ref, mate_ref, *refs):
    outs = refs[waits:-1]
    spread_ref = refs[-1]
    token_count = own_ref.shape[0]

    @pl.when(pl.program_id(0) == 0)
    def _():
        scale = ADAPTER_SCALE * rewards_ref[...].astype(jnp.float32)
        scaled = (scale * factor_ref[...]).astype(jnp.bfloat16).astype(jnp.float32)
        spread(codes_ref[...], scaled, row_codes, spread_ref)

    total = jnp.dot(
        spread_ref[:, :token_count], own_ref[...], preferred_element_type=jnp.float32
    ) + jnp.dot(spread_ref[:, token_count:], mate_ref[...], preferred_element_type=jnp.float32)
    first = 0
    for out_ref in outs:
        rows = out_ref.shape[0]
        out_ref[...] = total[first : first + rows].astype(out_ref.dtype)
        first += rows


def gradient_chunks(codes, rewards, factor, own, mate, chunks, after=()):
    rank = factor.shape[0]
    token_count, width = own.shape
    tile = largest_tile(width, 512)
    out_rows = [adapters * rank for _, adapters, _ in chunks]
    whole = lambda i: (0, 0)
    across = lambda i: (0, i)
    return pl.pallas_call(
        functools.partial(
            gradient_kernel,
            code_list([(base, rows) for (base, _, _), rows in zip(chunks, out_rows)], rank),
            len(after),
        ),
        grid=(width // tile,),
        in_specs=[
            pl.BlockSpec((1, 2 * token_count), whole),
            pl.BlockSpec(rewards.shape, whole),
            pl.BlockSpec((rank, 2 * token_count), whole),
            pl.BlockSpec((token_count, tile), across),
            pl.BlockSpec((token_count, tile), across),
        ]
        + [pl.BlockSpec(memory_space=pl.ANY) for _ in after],
        out_specs=[pl.BlockSpec((rows, tile), across) for rows in out_rows],
        out_shape=[
            jax.ShapeDtypeStruct((rows, width), dtype)
            for rows, (_, _, dtype) in zip(out_rows, chunks)
        ],
        scratch_shapes=[pltpu.VMEM((sum(out_rows), 2 * token_count), jnp.bfloat16)],
        compiler_params=pltpu.CompilerParams(vmem_limit_bytes=VMEM_LIMIT),
        cost_estimate=pl.CostEstimate(flops=1, bytes_accessed=1, transcendentals=0),
    )(codes, rewards, factor, own, mate, *after)


def add_kernel(groups, *refs):
    starts, refs = refs[: len(groups)], refs[len(groups) :]
    outs = refs[len(refs) - len(groups) :]
    arrived = list(refs[: sum(sum(counts) for counts in groups)])
    for counts, start_ref, out_ref in zip(groups, starts, outs):
        rows = out_ref.shape[0] // len(counts)
        for p, count in enumerate(counts):
            part = slice(p * rows, (p + 1) * rows)
            total = start_ref[part, :]
            for _ in range(count):
                total += arrived.pop(0)[...].astype(jnp.float32)
            out_ref[part, :] = total.astype(out_ref.dtype)


def add_arrived(groups, dtype, after=()):
    width = groups[0][0].shape[1]
    tile = largest_tile(width, 1024)
    arrays = [start for start, _ in groups]
    arrays += [a for _, parts in groups for arrived in parts for a in arrived]
    across = lambda i: (0, i)
    return pl.pallas_call(
        functools.partial(
            add_kernel, [[len(arrived) for arrived in parts] for _, parts in groups]
        ),
        grid=(width // tile,),
        in_specs=[pl.BlockSpec((a.shape[0], tile), across) for a in arrays]
        + [pl.BlockSpec(memory_space=pl.ANY) for _ in after],
        out_specs=[pl.BlockSpec((start.shape[0], tile), across) for start, _ in groups],
        out_shape=[jax.ShapeDtypeStruct(start.shape, dtype) for start, _ in groups],
        compiler_params=pltpu.CompilerParams(vmem_limit_bytes=VMEM_LIMIT),
        cost_estimate=pl.CostEstimate(flops=1, bytes_accessed=1, transcendentals=0),
    )(*arrays, *after)


def wait_for(array, *others):
    return lax.optimization_barrier((array, *others))[0]


def sum_over(axis, piece, waits=()):
    for k, bit in enumerate(axis_bits(axis)):
        arrived = swap(piece, axis, bit)
        if k < len(waits):
            arrived = wait_for(arrived, *waits[k])
        piece = piece + arrived
    return piece


def attend_cached(queries, cached_key_rows, cached_value_rows, lengths, fresh_keys):
    row_count = queries.shape[0]
    kv_local = fresh_keys.shape[1] // HEAD_SIZE
    group = HEADS // KEY_VALUE_HEADS
    query_heads = queries.reshape(row_count, kv_local, group, HEAD_SIZE)
    key_heads = cached_key_rows.reshape(row_count, CACHE, kv_local, HEAD_SIZE)
    value_heads = cached_value_rows.reshape(row_count, CACHE, kv_local, HEAD_SIZE)
    inverse = 1.0 / math.sqrt(HEAD_SIZE)
    scores = (
        jnp.einsum("bhgd,bphd->bhgp", query_heads, key_heads, preferred_element_type=jnp.float32)
        * inverse
    )
    own_score = (
        jnp.einsum(
            "bhgd,bhd->bhg",
            query_heads,
            fresh_keys.reshape(row_count, kv_local, HEAD_SIZE),
            preferred_element_type=jnp.float32,
        )
        * inverse
    )
    allowed = jnp.arange(CACHE, dtype=jnp.int32)[None, :] < lengths[:, None]
    scores = jnp.where(allowed[:, None, None, :], scores, NEG_FILL)
    highest = jnp.maximum(jnp.max(scores, axis=-1), own_score)
    cache_exp = jnp.exp(scores - highest[..., None])
    own_exp = jnp.exp(own_score - highest)
    denominator = jnp.sum(cache_exp, axis=-1) + own_exp
    cache_weight = (cache_exp / denominator[..., None]).astype(jnp.bfloat16)
    own_weight = (own_exp / denominator).astype(jnp.bfloat16)
    attended = jnp.einsum(
        "bhgp,bphd->bhgd", cache_weight, value_heads, preferred_element_type=jnp.float32
    )
    return attended, own_weight


def per_device(
    decode_hidden_input,
    queries,
    cached_key_rows,
    cached_value_rows,
    lengths,
    decode_adapter_index,
    key_matrix,
    value_matrix,
    adapter_down_map,
    adapter_up_map,
    training_hidden_input,
    cotangent,
    training_adapter_index,
    rewards,
):
    core_bit, *chip_bits = axis_bits("wide")
    masks = [m for m in range(lax.axis_size("wide")) if not m & core_bit]
    me = lax.axis_index("wide")
    owner_totals, rank, down_width = adapter_down_map.shape
    up_width = adapter_up_map.shape[2]
    row_count = decode_hidden_input.shape[0]
    token_count = training_hidden_input.shape[0]
    parts = len(chip_bits) if owner_totals % len(chip_bits) == 0 else 1
    orders = [chip_bits[p:] + chip_bits[:p] for p in range(parts)]
    part_adapters = owner_totals // parts
    part_rows = part_adapters * rank

    flattened_down = adapter_down_map.reshape(-1, down_width)
    flattened_up = adapter_up_map.reshape(-1, up_width)

    far = [m for m in masks if m.bit_count() > 1]
    near = [m for m in masks if m.bit_count() == 1]

    numbers = jnp.concatenate([training_adapter_index, rewards, decode_adapter_index])
    mate_numbers = swap(numbers, "wide", core_bit)
    mate_cotangent = swap(wait_for(cotangent, mate_numbers), "wide", core_bit)
    up_maps = {0: flattened_up}
    own_parts = [flattened_down[p * part_rows : (p + 1) * part_rows] for p in range(parts)]
    for m in near:
        up_maps[m] = swap(wait_for(flattened_up, *own_parts), "wide", m)
    for m in far:
        up_maps[m] = swap(wait_for(flattened_up, mate_numbers), "wide", m)
    mate_hidden = swap(wait_for(training_hidden_input, mate_numbers), "wide", core_bit)
    down_parts = {}
    for p, order in enumerate(orders):
        held = []
        for bit in order:
            for m in held:
                down_parts[m | bit, p] = swap(down_parts[m, p], "wide", bit)
            sent = wait_for(own_parts[p], *[down_parts[m | bit, p] for m in held[-1:]])
            down_parts[bit, p] = swap(sent, "wide", bit)
            held = held + [bit] + [m | bit for m in held]
    first_maps = [down_parts[order[0], p] for p, order in enumerate(orders)]
    decode_slice = lax.dynamic_slice_in_dim(
        decode_hidden_input, lax.axis_index("narrow") * down_width, down_width, 1
    )
    mate_slice = swap(wait_for(decode_slice, mate_cotangent), "wide", core_bit)

    def codes_of(ids):
        return (((ids // owner_totals) ^ me) * owner_totals + ids % owner_totals)[None, :]

    token_codes = codes_of(
        jnp.concatenate([training_adapter_index, mate_numbers[:token_count]])
    )
    token_rewards = jnp.concatenate([rewards, mate_numbers[token_count : 2 * token_count]])[
        None, :
    ]
    row_codes = codes_of(
        jnp.concatenate([decode_adapter_index, mate_numbers[2 * token_count :]])
    )
    tile = token_tile(token_count, down_width)
    all_codes = jnp.concatenate(
        [token_codes, jnp.pad(row_codes, ((0, 0), (0, tile - 2 * row_count)), constant_values=-1)],
        axis=1,
    )
    up_chunks = [(m * owner_totals, up_maps[m]) for m in masks]
    def down_chunk(m, p):
        return (m * owner_totals + p * part_adapters, down_parts[m, p])

    hidden_rows = wait_for(decode_hidden_input, mate_numbers, *[up_maps[m] for m in near])
    fresh_keys = jnp.dot(
        hidden_rows, key_matrix, preferred_element_type=jnp.float32
    ).astype(jnp.bfloat16)
    base_values = jnp.dot(hidden_rows, value_matrix, preferred_element_type=jnp.float32)

    cached, own_weight = attend_cached(
        wait_for(queries, *[up_maps[m] for m in near]),
        cached_key_rows,
        cached_value_rows,
        lengths,
        fresh_keys,
    )

    part_back = project_tokens(
        all_codes,
        cotangent,
        mate_cotangent,
        up_chunks,
        rank,
        after=(*first_maps, mate_hidden, own_weight),
    )
    back = sum_over("narrow", part_back, [(cached,), (base_values,)])

    def level_of(m, p):
        return max((k for k, bit in enumerate(orders[p]) if m & bit), default=-1)

    last_level = len(chip_bits) - 1
    keys = sorted(
        ((m, p) for m in far + near for p in range(parts)), key=lambda key: -level_of(*key)
    )
    own_down, *down_results = gradient_chunks(
        token_codes,
        token_rewards,
        back,
        training_hidden_input,
        mate_hidden,
        [(0, owner_totals, jnp.float32)]
        + [
            (
                m * owner_totals + p * part_adapters,
                part_adapters,
                jnp.bfloat16 if level_of(m, p) == last_level else jnp.float32,
            )
            for m, p in keys
        ],
    )
    grads = dict(zip(keys, down_results))
    arrived = {(m, p): [] for m in masks for p in range(parts)}

    def send_level(level):
        for m, p in keys:
            if level_of(m, p) == level:
                bit = orders[p][level]
                arrived[m ^ bit, p].append(swap(grads[m, p], "wide", bit))

    send_level(last_level)
    part_hidden = project_tokens(
        all_codes,
        training_hidden_input,
        mate_hidden,
        [(0, flattened_down)] + [down_chunk(m, p) for m in near + far for p in range(parts)],
        rank,
        rows=(decode_slice, mate_slice),
        after=(own_down,),
    )
    token = part_hidden
    for level in reversed(range(last_level)):
        added = [key for key in keys if level_of(*key) == level]
        sums = add_arrived([(grads[key], [arrived[key]]) for key in added], jnp.bfloat16, (token,))
        grads.update(zip(added, sums))
        token = sums[0]
        send_level(level)
    (own_down,) = add_arrived(
        [(own_down, [arrived[0, p][:-1] for p in range(parts)])], jnp.float32, (token,)
    )
    last_down = [arrived[0, p][-1] for p in range(parts)]
    (grad_down,) = add_arrived([(own_down, [[a] for a in last_down])], jnp.float32)

    hidden = sum_over("narrow", part_hidden, [(token,), (own_down,)])
    grad_up, *up_results = gradient_chunks(
        token_codes,
        token_rewards,
        hidden,
        cotangent,
        mate_cotangent,
        [(m * owner_totals, owner_totals, jnp.bfloat16 if m else jnp.float32) for m in masks],
    )
    own_delta, mate_delta = row_deltas(row_codes, hidden, 2 * token_count, tile, up_chunks, (grad_up,))
    for m, result in zip(masks[1:], up_results):
        result = wait_for(result, *last_down)
        grad_up = grad_up + swap(result, "wide", m).astype(jnp.float32)

    own_delta = own_delta + swap(mate_delta, "wide", core_bit)
    fresh_values = (base_values + own_delta.astype(jnp.float32)).astype(jnp.bfloat16)
    kv_local = up_width // HEAD_SIZE
    attended = cached + own_weight.astype(jnp.float32)[..., None] * fresh_values.reshape(
        row_count, kv_local, 1, HEAD_SIZE
    ).astype(jnp.float32)
    return (
        attended.reshape(row_count, -1).astype(jnp.bfloat16),
        fresh_values,
        grad_down.reshape(adapter_down_map.shape),
        grad_up.reshape(adapter_up_map.shape),
    )


def solution(mesh):
    return jax.shard_map(
        per_device,
        mesh=mesh,
        in_specs=(
            P("wide", None),
            P("wide", "narrow"),
            P("wide", None, "narrow"),
            P("wide", None, "narrow"),
            P("wide"),
            P("wide"),
            P(None, "narrow"),
            P(None, "narrow"),
            P("wide", None, "narrow"),
            P("wide", None, "narrow"),
            P("wide", "narrow"),
            P("wide", "narrow"),
            P("wide"),
            P("wide"),
        ),
        out_specs=(
            P("wide", "narrow"),
            P("wide", "narrow"),
            P("wide", None, "narrow"),
            P("wide", None, "narrow"),
        ),
        check_vma=False,
    )
```

```python
import functools
import math

import jax
import jax.numpy as jnp
from jax import lax
from jax.experimental import pallas as pl
from jax.experimental.pallas import tpu as pltpu
from jax.sharding import PartitionSpec as P

HEAD_SIZE = 128

ADAPTER_SCALE = 2.0
NEG_FILL = -1e30
VMEM_LIMIT = 48 * 1024 * 1024
SHORT = pl.CostEstimate(flops=1, bytes_accessed=1, transcendentals=0)


def swap(array, axis, mask):
    count = lax.axis_size(axis)
    return lax.ppermute(array, axis, [(i, i ^ mask) for i in range(count)])


def axis_bits(axis):
    count = lax.axis_size(axis)
    assert count & (count - 1) == 0, "axis size"
    return [1 << k for k in range(count.bit_length() - 1)]


def highest_in(order, mask):
    return [bit for bit in order if bit & mask][-1]


def largest_tile(length, limit):
    tile = length
    while tile > limit and tile % 2 == 0:
        tile //= 2
    return tile


def code_list(chunks, rank):
    return [
        base + j
        for bases, rows in chunks
        for base in bases
        for j in range(rows // rank // len(bases))
    ]


def pick(codes, products, row_codes, rank):
    total = jnp.zeros((rank, products.shape[1]), jnp.float32)
    for k, code in enumerate(row_codes):
        total += jnp.where(codes == code, products[k * rank : (k + 1) * rank], 0.0)
    return total


def spread(codes, values, row_codes, out_ref):
    rank = values.shape[0]
    for k, code in enumerate(row_codes):
        out_ref[k * rank : (k + 1) * rank, :] = jnp.where(codes == code, values, 0.0).astype(
            out_ref.dtype
        )


def join(maps, joined_ref):
    first = 0
    for chunk in maps:
        joined_ref[first : first + chunk.shape[0], :] = chunk[...]
        first += chunk.shape[0]


def times_transposed(maps, tokens):
    return lax.dot_general(
        maps, tokens, (((1,), (1,)), ((), ())), preferred_element_type=jnp.float32
    )


def token_kernel(map_codes, rank, tiles, source_count, has_rows, map_count, codes_ref, *refs):
    refs = list(refs)
    sources = [refs.pop(0) for _ in range(source_count)]
    row_refs = [refs.pop(0) for _ in range(2 * has_rows)]
    maps = refs[:map_count]
    out_ref, sent_ref, joined_ref, *rest = refs[-3 - has_rows :]
    step = pl.program_id(0)

    @pl.when(step == 0)
    def _():
        join(maps, joined_ref)

    def project(tokens):
        products = times_transposed(joined_ref[...], tokens)
        return pick(codes_ref[:, : tokens.shape[0]], products, map_codes, rank)

    def store(total):
        out_ref[...] = total
        sent_ref[...] = total.astype(sent_ref.dtype)

    for k, source_ref in enumerate(sources):
        pl.when(step // tiles == k)(lambda ref=source_ref: store(project(ref[...])))
    if has_rows:
        rows_ref = rest[0]

        @pl.when(step == source_count * tiles)
        def _():
            rows_ref[...] = jnp.zeros_like(rows_ref)
            join(row_refs, rows_ref)
            total = project(rows_ref[...])
            rest_shape = (total.shape[0], out_ref.shape[1] - total.shape[1])
            store(jnp.concatenate([total, jnp.zeros(rest_shape, jnp.float32)], axis=1))


def token_tile(token_count, width=0):
    return largest_tile(token_count, 512 if width > 512 else 1024)


def project_tokens(codes, sources, chunks, rank, rows=(), after=(), cost=SHORT):
    token_count, width = sources[0].shape
    tile = token_tile(token_count, width)
    tiles = token_count // tile
    map_rows = sum(chunk.shape[0] for _, chunk in chunks)
    scratch = [pltpu.VMEM((map_rows, width), jnp.bfloat16)]
    if rows:
        padded = -(-2 * rows[0].shape[0] // 128) * 128
        assert padded <= tile, "row count"
        scratch.append(pltpu.VMEM((padded, width), jnp.bfloat16))
    steps = len(sources) * tiles + bool(rows)
    across = lambda i: (0, i)
    whole = lambda i: (0, 0)
    operands = [codes, *sources, *rows, *[chunk for _, chunk in chunks], *after]
    return pl.pallas_call(
        functools.partial(
            token_kernel,
            code_list([(bases, chunk.shape[0]) for bases, chunk in chunks], rank),
            rank,
            tiles,
            len(sources),
            bool(rows),
            len(chunks),
        ),
        grid=(steps,),
        in_specs=[pl.BlockSpec((1, tile), across)]
        + [
            pl.BlockSpec((tile, width), lambda i, k=k: (jnp.clip(i - k * tiles, 0, tiles - 1), 0))
            for k in range(len(sources))
        ]
        + [pl.BlockSpec(a.shape, whole) for a in rows]
        + [pl.BlockSpec(chunk.shape, whole) for _, chunk in chunks]
        + [pl.BlockSpec(memory_space=pl.ANY) for _ in after],
        out_specs=[pl.BlockSpec((rank, tile), across)] * 2,
        out_shape=[
            jax.ShapeDtypeStruct((rank, steps * tile), dtype)
            for dtype in (jnp.float32, jnp.bfloat16)
        ],
        scratch_shapes=scratch,
        compiler_params=pltpu.CompilerParams(vmem_limit_bytes=VMEM_LIMIT),
        cost_estimate=cost,
    )(*operands)


def delta_kernel(chunk_codes, codes_ref, rank_ref, *refs):
    maps = refs[: len(chunk_codes)]
    own_ref, mate_ref, spread_ref = refs[-3:]
    count = codes_ref.shape[1]
    values = rank_ref[:, :count].astype(jnp.bfloat16).astype(jnp.float32)
    total = jnp.zeros((count, own_ref.shape[1]), jnp.float32)
    for map_codes, chunk in zip(chunk_codes, maps):
        spread(codes_ref[...], values, map_codes, spread_ref)
        total += lax.dot_general(
            spread_ref[...].T.astype(jnp.bfloat16),
            chunk[...],
            (((1,), (0,)), ((), ())),
            preferred_element_type=jnp.float32,
        )
    deltas = ADAPTER_SCALE * total
    own_ref[...] = deltas[: count // 2].astype(own_ref.dtype)
    mate_ref[...] = deltas[count // 2 :].astype(mate_ref.dtype)


def row_deltas(codes, ranks, first, width_of_ranks, chunks, after=()):
    rank = ranks.shape[0]
    row_count = codes.shape[1]
    chunk_rows, width = chunks[0][1].shape
    whole = lambda i: (0, 0)
    return pl.pallas_call(
        functools.partial(
            delta_kernel, [code_list([(bases, chunk_rows)], rank) for bases, _ in chunks]
        ),
        grid=(1,),
        in_specs=[
            pl.BlockSpec(codes.shape, whole),
            pl.BlockSpec((rank, width_of_ranks), lambda i: (0, first // width_of_ranks)),
        ]
        + [pl.BlockSpec((chunk_rows, width), whole) for _ in chunks]
        + [pl.BlockSpec(memory_space=pl.ANY) for _ in after],
        out_specs=[pl.BlockSpec((row_count // 2, width), whole)] * 2,
        out_shape=[jax.ShapeDtypeStruct((row_count // 2, width), jnp.bfloat16)] * 2,
        scratch_shapes=[pltpu.VMEM((chunk_rows, row_count), jnp.float32)],
        compiler_params=pltpu.CompilerParams(vmem_limit_bytes=VMEM_LIMIT),
    )(codes, ranks, *[chunk for _, chunk in chunks], *after)


def place_kernel(buffer_ref, piece_ref, *refs):
    refs[-1][...] = piece_ref[...]


def place(buffer, piece, k, after=()):
    return pl.pallas_call(
        place_kernel,
        grid=(1,),
        in_specs=[
            pl.BlockSpec(memory_space=pl.ANY),
            pl.BlockSpec(piece.shape, lambda i: (0, 0)),
        ]
        + [pl.BlockSpec(memory_space=pl.ANY) for _ in after],
        out_specs=pl.BlockSpec(piece.shape, lambda i: (k, 0)),
        out_shape=jax.ShapeDtypeStruct(buffer.shape, buffer.dtype),
        input_output_aliases={0: 0},
        compiler_params=pltpu.CompilerParams(vmem_limit_bytes=VMEM_LIMIT),
        cost_estimate=SHORT,
    )(buffer, piece, *after)


def finish_rows_kernel(cached_ref, weight_ref, base_ref, own_ref, mate_ref, attended_ref, fresh_ref):
    delta = own_ref[...].astype(jnp.float32) + mate_ref[...].astype(jnp.float32)
    fresh = (base_ref[...] + delta).astype(jnp.bfloat16)
    fresh_ref[...] = fresh
    heads = cached_ref.shape[1]
    group = heads * HEAD_SIZE // fresh.shape[1]
    for j in range(heads):
        value = slice(j // group * HEAD_SIZE, (j // group + 1) * HEAD_SIZE)
        attended = cached_ref[:, j, :] + weight_ref[:, j, :] * fresh[:, value].astype(jnp.float32)
        attended_ref[:, j * HEAD_SIZE : (j + 1) * HEAD_SIZE] = attended.astype(jnp.bfloat16)


def finish_rows(cached, own_weight, base_values, own_delta, mate_delta):
    row_count, heads, size = cached.shape
    return pl.pallas_call(
        finish_rows_kernel,
        out_shape=[
            jax.ShapeDtypeStruct((row_count, heads * size), jnp.bfloat16),
            jax.ShapeDtypeStruct(base_values.shape, jnp.bfloat16),
        ],
        compiler_params=pltpu.CompilerParams(vmem_limit_bytes=VMEM_LIMIT),
        cost_estimate=SHORT,
    )(cached, own_weight, base_values, own_delta, mate_delta)


def gradient_kernel(
    row_codes, arrived_counts, codes_ref, rewards_ref, factor_ref, own_ref, mate_ref, *refs
):
    arrived = list(refs[: sum(arrived_counts)])
    outs = refs[-1 - len(arrived_counts) : -1]
    spread_ref = refs[-1]
    token_count = own_ref.shape[0]

    @pl.when(pl.program_id(0) == 0)
    def _():
        scale = ADAPTER_SCALE * rewards_ref[...].astype(jnp.float32)
        scaled = (scale * factor_ref[...]).astype(jnp.bfloat16).astype(jnp.float32)
        spread(codes_ref[...], scaled, row_codes, spread_ref)

    total = jnp.dot(
        spread_ref[:, :token_count], own_ref[...], preferred_element_type=jnp.float32
    ) + jnp.dot(spread_ref[:, token_count:], mate_ref[...], preferred_element_type=jnp.float32)
    first = 0
    for out_ref, count in zip(outs, arrived_counts):
        rows = out_ref.shape[0]
        piece = total[first : first + rows]
        for _ in range(count):
            piece += arrived.pop(0)[...].astype(jnp.float32)
        out_ref[...] = piece.astype(out_ref.dtype)
        first += rows


def gradient_chunks(codes, rewards, factor, own, mate, chunks, after=(), cost=SHORT):
    rank = factor.shape[0]
    token_count, width = own.shape
    tile = largest_tile(width, 512)
    out_rows = [adapters * rank for _, adapters, _, _ in chunks]
    arrived = [(a, rows) for (_, _, _, arrays), rows in zip(chunks, out_rows) for a in arrays]
    whole = lambda i: (0, 0)
    across = lambda i: (0, i)
    return pl.pallas_call(
        functools.partial(
            gradient_kernel,
            code_list([(chunk[0], rows) for chunk, rows in zip(chunks, out_rows)], rank),
            [len(arrays) for _, _, _, arrays in chunks],
        ),
        grid=(width // tile,),
        in_specs=[
            pl.BlockSpec((1, 2 * token_count), whole),
            pl.BlockSpec(rewards.shape, whole),
            pl.BlockSpec((rank, 2 * token_count), whole),
            pl.BlockSpec((token_count, tile), across),
            pl.BlockSpec((token_count, tile), across),
        ]
        + [pl.BlockSpec((rows, tile), across) for _, rows in arrived]
        + [pl.BlockSpec(memory_space=pl.ANY) for _ in after],
        out_specs=[pl.BlockSpec((rows, tile), across) for rows in out_rows],
        out_shape=[
            jax.ShapeDtypeStruct((rows, width), dtype)
            for rows, (_, _, dtype, _) in zip(out_rows, chunks)
        ],
        scratch_shapes=[pltpu.VMEM((sum(out_rows), 2 * token_count), jnp.bfloat16)],
        compiler_params=pltpu.CompilerParams(vmem_limit_bytes=VMEM_LIMIT),
        cost_estimate=cost,
    )(codes, rewards, factor, own, mate, *[a for a, _ in arrived], *after)


def add_kernel(groups, *refs):
    starts, refs = refs[: len(groups)], refs[len(groups) :]
    outs = refs[len(refs) - len(groups) :]
    arrived = list(refs)
    for places, start_ref, out_ref in zip(groups, starts, outs):
        rows = out_ref.shape[0] // len(places)
        for p, firsts in enumerate(places):
            part = slice(p * rows, (p + 1) * rows)
            total = start_ref[part, :]
            for k in firsts:
                total += arrived.pop(0)[k * rows : (k + 1) * rows, :].astype(jnp.float32)
            out_ref[part, :] = total.astype(out_ref.dtype)


def add_arrived(groups, after=(), dtype=jnp.bfloat16):
    width = groups[0][0].shape[1]
    tile = largest_tile(width, 1024)
    arrays = [start for start, _ in groups]
    arrays += [a for _, parts in groups for arrived in parts for a, _ in arrived]
    across = lambda i: (0, i)
    return pl.pallas_call(
        functools.partial(
            add_kernel, [[[k for _, k in arrived] for arrived in parts] for _, parts in groups]
        ),
        grid=(width // tile,),
        in_specs=[pl.BlockSpec((a.shape[0], tile), across) for a in arrays]
        + [pl.BlockSpec(memory_space=pl.ANY) for _ in after],
        out_specs=[pl.BlockSpec((start.shape[0], tile), across) for start, _ in groups],
        out_shape=[jax.ShapeDtypeStruct(start.shape, dtype) for start, _ in groups],
        compiler_params=pltpu.CompilerParams(vmem_limit_bytes=VMEM_LIMIT),
        cost_estimate=SHORT,
    )(*arrays, *after)


def wait_for(array, *others):
    return lax.optimization_barrier((array, *others))[0]


def step_kernel(piece_ref, came_ref, *refs):
    out_ref, sent_ref = refs[-2:]
    total = piece_ref[...] + came_ref[...].astype(jnp.float32)
    out_ref[...] = total
    sent_ref[...] = total.astype(sent_ref.dtype)


def sum_over(axis, piece, sent, waits=()):
    for k, bit in enumerate(axis_bits(axis)):
        came = swap(sent, axis, bit)
        after = waits[k] if k < len(waits) else ()
        whole = pl.BlockSpec(piece.shape, lambda: (0, 0))
        piece, sent = pl.pallas_call(
            step_kernel,
            in_specs=[whole, whole] + [pl.BlockSpec(memory_space=pl.ANY) for _ in after],
            out_specs=[whole, whole],
            out_shape=[
                jax.ShapeDtypeStruct(piece.shape, dtype) for dtype in (jnp.float32, jnp.bfloat16)
            ],
            compiler_params=pltpu.CompilerParams(vmem_limit_bytes=VMEM_LIMIT),
            cost_estimate=SHORT,
        )(piece, came, *after)
    return piece


def attend_kernel(kv_local, lengths_ref, queries_ref, keys_ref, values_ref, fresh_ref, *refs):
    out_ref, own_ref = refs[-2:]
    block, heads, size = queries_ref.shape
    slots = keys_ref.shape[1]
    group = heads // kv_local
    first_row = pl.program_id(0) * block
    inverse = 1.0 / math.sqrt(size)
    head_of = lax.broadcasted_iota(jnp.int32, (heads, slots), 0) // group
    slot = lax.broadcasted_iota(jnp.int32, (heads, slots), 1)

    def by_head(pieces):
        chosen = pieces[0]
        for h, piece in enumerate(pieces[1:], 1):
            chosen = jnp.where(head_of[:, : piece.shape[1]] == h, piece, chosen)
        return chosen

    scores, own_scores = [], []
    for r in range(block):
        queries = queries_ref[r]
        products = by_head(
            [
                times_transposed(queries, keys_ref[r, :, h * size : (h + 1) * size])
                for h in range(kv_local)
            ]
        )
        scores.append(jnp.where(slot < lengths_ref[first_row + r], inverse * products, NEG_FILL))
        fresh = by_head(
            [
                jnp.broadcast_to(fresh_ref[r : r + 1, h * size : (h + 1) * size], (heads, size))
                for h in range(kv_local)
            ]
        )
        own_scores.append(queries.astype(jnp.float32) * fresh)
    scores = jnp.concatenate(scores)
    own_score = inverse * jnp.sum(jnp.concatenate(own_scores), axis=1, keepdims=True)
    highest = jnp.maximum(jnp.max(scores, axis=1, keepdims=True), own_score)
    cache_exp = jnp.exp(scores - highest)
    own_exp = jnp.exp(own_score - highest)
    denominator = jnp.sum(cache_exp, axis=1, keepdims=True) + own_exp
    weights = cache_exp / denominator
    own_weight = (own_exp / denominator).astype(jnp.bfloat16).astype(jnp.float32)
    for r in range(block):
        mine = slice(r * heads, (r + 1) * heads)
        row_weights = weights[mine].astype(jnp.bfloat16)
        out_ref[r] = by_head(
            [
                jnp.dot(
                    row_weights,
                    values_ref[r, :, h * size : (h + 1) * size],
                    preferred_element_type=jnp.float32,
                )
                for h in range(kv_local)
            ]
        )
        own_ref[r] = jnp.broadcast_to(own_weight[mine], (heads, size))


def attend_cached(queries, cached_key_rows, cached_value_rows, lengths, fresh_keys, after=()):
    row_count, slots, kv_width = cached_key_rows.shape
    heads = queries.shape[1] // HEAD_SIZE
    block = largest_tile(row_count, 8)
    rows_of = lambda i, *_: (i, 0, 0)
    head_spec = pl.BlockSpec((block, heads, HEAD_SIZE), rows_of)
    cache_spec = pl.BlockSpec((block, slots, kv_width), rows_of)
    shape = (row_count, heads, HEAD_SIZE)
    return pl.pallas_call(
        functools.partial(attend_kernel, kv_width // HEAD_SIZE),
        grid_spec=pltpu.PrefetchScalarGridSpec(
            num_scalar_prefetch=1,
            grid=(row_count // block,),
            in_specs=[
                head_spec,
                cache_spec,
                cache_spec,
                pl.BlockSpec((block, kv_width), lambda i, *_: (i, 0)),
            ]
            + [pl.BlockSpec(memory_space=pl.ANY) for _ in after],
            out_specs=[head_spec, head_spec],
        ),
        out_shape=[jax.ShapeDtypeStruct(shape, jnp.float32)] * 2,
        compiler_params=pltpu.CompilerParams(vmem_limit_bytes=VMEM_LIMIT),
        cost_estimate=SHORT,
    )(
        lengths,
        queries.reshape(shape),
        cached_key_rows,
        cached_value_rows,
        fresh_keys.astype(jnp.float32),
        *after,
    )


def per_device(
    decode_hidden_input,
    queries,
    cached_key_rows,
    cached_value_rows,
    lengths,
    decode_adapter_index,
    key_matrix,
    value_matrix,
    adapter_down_map,
    adapter_up_map,
    training_hidden_input,
    cotangent,
    training_adapter_index,
    rewards,
):
    core_bit, *chip_bits = axis_bits("wide")
    masks = [m for m in range(lax.axis_size("wide")) if not m & core_bit]
    me = lax.axis_index("wide")
    owner_totals, rank, down_width = adapter_down_map.shape
    up_width = adapter_up_map.shape[2]
    row_count = decode_hidden_input.shape[0]
    token_count = training_hidden_input.shape[0]
    parts = len(chip_bits) if owner_totals % len(chip_bits) == 0 else 1
    orders = [chip_bits[p:] + chip_bits[:p] for p in range(parts)]
    part_adapters = owner_totals // parts
    part_rows = part_adapters * rank

    flattened_down = adapter_down_map.reshape(-1, down_width)
    flattened_up = adapter_up_map.reshape(-1, up_width)

    far = [m for m in masks if m.bit_count() > 1]
    near = [m for m in masks if m.bit_count() == 1]

    numbers = jnp.concatenate([training_adapter_index, rewards, decode_adapter_index])
    mate_numbers = swap(numbers, "wide", core_bit)
    mate_cotangent = swap(wait_for(cotangent, mate_numbers), "wide", core_bit)
    up_maps = {0: flattened_up}
    own_parts = [flattened_down[p * part_rows : (p + 1) * part_rows] for p in range(parts)]
    for m in near:
        up_maps[m] = swap(wait_for(flattened_up, *own_parts), "wide", m)
    for m in far:
        up_maps[m] = swap(wait_for(flattened_up, mate_numbers), "wide", m)
    mate_hidden = swap(wait_for(training_hidden_input, mate_numbers), "wide", core_bit)
    decode_slice = lax.dynamic_slice_in_dim(
        decode_hidden_input, lax.axis_index("narrow") * down_width, down_width, 1
    )
    mate_slice = swap(wait_for(decode_slice, mate_cotangent), "wide", core_bit)

    def codes_of(ids):
        return (((ids // owner_totals) ^ me) * owner_totals + ids % owner_totals)[None, :]

    token_codes = codes_of(
        jnp.concatenate([training_adapter_index, mate_numbers[:token_count]])
    )
    token_rewards = jnp.concatenate([rewards, mate_numbers[token_count : 2 * token_count]])[
        None, :
    ]
    row_codes = codes_of(
        jnp.concatenate([decode_adapter_index, mate_numbers[2 * token_count :]])
    )
    tile = token_tile(token_count, down_width)
    all_codes = jnp.concatenate(
        [token_codes, jnp.pad(row_codes, ((0, 0), (0, tile - 2 * row_count)), constant_values=-1)],
        axis=1,
    )
    up_chunks = [([m * owner_totals], up_maps[m]) for m in masks]
    hidden_rows = wait_for(decode_hidden_input, mate_numbers, *[up_maps[m] for m in near])
    fresh_keys = jnp.dot(
        hidden_rows, key_matrix, preferred_element_type=jnp.float32
    ).astype(jnp.bfloat16)
    base_values = jnp.dot(hidden_rows, value_matrix, preferred_element_type=jnp.float32)

    cached, own_weight = attend_cached(
        queries, cached_key_rows, cached_value_rows, lengths, fresh_keys
    )

    stages, second_sent = [], []
    down_parts = {(0, p): own_parts[p] for p in range(parts)}
    for p, order in enumerate(orders):
        held = [0]
        for bit in order:
            sent = own_parts[p]
            if len(held) > 1:
                sent = jnp.pad(sent, ((0, (len(held) - 1) * part_rows), (0, 0)))
                for k, m in enumerate(held[1:], 1):
                    sent = place(sent, down_parts[m, p], k, (cached, base_values))
                second_sent.append(sent)
            came = swap(sent, "wide", bit)
            for k, m in enumerate(held):
                down_parts[m | bit, p] = came[k * part_rows : (k + 1) * part_rows]
            if bit == order[0]:
                down_stages = [(bit, p, [bit], came)]
            else:
                down_stages.append((bit, p, [m | bit for m in held], came))
            held = held + [m | bit for m in held]
        stages.extend(down_stages)
    last_maps = [came for bit, p, _, came in stages if bit == orders[p][-1]]
    first_maps = [came for bit, p, _, came in stages if bit == orders[p][0]]

    def down_code(m, p):
        return m * owner_totals + p * part_adapters

    down_chunks = [([0], flattened_down)] + [
        ([down_code(m, p) for m in came_from], came) for _, p, came_from, came in stages
    ]

    part_back, sent_back = project_tokens(
        all_codes,
        [cotangent, mate_cotangent],
        up_chunks,
        rank,
        after=(*first_maps, *second_sent),
    )
    back = sum_over("narrow", part_back, sent_back)

    groups = {}
    for m in far + near:
        for p, order in enumerate(orders):
            level = max(k for k, bit in enumerate(order) if m & bit)
            groups.setdefault((level, p, m == order[level]), []).append(m)
    group_keys = sorted(groups, key=lambda key: (-key[0], key[2]))
    last_level = len(chip_bits) - 1
    own_down, *results = gradient_chunks(
        token_codes,
        token_rewards,
        back,
        training_hidden_input,
        mate_hidden,
        [([0], owner_totals, jnp.float32, ())]
        + [
            (
                [down_code(m, p) for m in groups[level, p, direct]],
                part_adapters * len(groups[level, p, direct]),
                jnp.bfloat16 if level == last_level else jnp.float32,
                (),
            )
            for level, p, direct in group_keys
        ],
        (mate_slice,),
    )
    grads = dict(zip(group_keys, results))
    token = own_down
    arrived = {(m, p): [] for m in masks for p in range(parts)}

    def send_level(level):
        for key in group_keys:
            if key[0] == level:
                bit = orders[key[1]][level]
                came = swap(wait_for(grads[key], *last_maps), "wide", bit)
                for k, m in enumerate(groups[key]):
                    arrived[m ^ bit, key[1]].append((came, k))

    send_level(last_level)

    part_hidden, sent_hidden = project_tokens(
        all_codes,
        [training_hidden_input, mate_hidden],
        down_chunks,
        rank,
        rows=(decode_slice, mate_slice),
        after=(token,),
    )
    token = part_hidden
    for level in reversed(range(last_level)):
        added = [key for key in group_keys if key[0] == level]
        sums = add_arrived(
            [(grads[key], [arrived[m, key[1]] for m in groups[key]]) for key in added], (token,)
        )
        grads.update(zip(added, sums))
        send_level(level)
        token = sums[0]
    early = [[arrived[0, p][:-1] for p in range(parts)]]
    (own_down,) = add_arrived([(own_down, *early)], (token,), jnp.float32)
    last_down = [arrived[0, p][-1:] for p in range(parts)]

    hidden = sum_over(
        "narrow",
        part_hidden,
        sent_hidden,
        [(token,), (own_down,)],
    )
    own_up, *up_results = gradient_chunks(
        token_codes,
        token_rewards,
        hidden,
        cotangent,
        mate_cotangent,
        [([m * owner_totals], owner_totals, jnp.bfloat16 if m else jnp.float32, ()) for m in masks],
    )
    own_delta, mate_delta = row_deltas(
        row_codes, hidden, 2 * token_count, tile, up_chunks, (own_up,)
    )
    mate_delta = wait_for(mate_delta, *[came for part in last_down for came, _ in part])
    came_up = [(swap(result, "wide", m), 0) for m, result in zip(masks[1:], up_results)]
    (grad_up,) = add_arrived([(own_up, [came_up])], (), jnp.float32)
    (grad_down,) = add_arrived([(own_down, last_down)], (), jnp.float32)
    attended, fresh_values = finish_rows(
        cached, own_weight, base_values, own_delta, swap(mate_delta, "wide", core_bit)
    )
    return (
        attended,
        fresh_values,
        grad_down.reshape(adapter_down_map.shape),
        grad_up.reshape(adapter_up_map.shape),
    )


def solution(mesh):
    return jax.shard_map(
        per_device,
        mesh=mesh,
        in_specs=(
            P("wide", None),
            P("wide", "narrow"),
            P("wide", None, "narrow"),
            P("wide", None, "narrow"),
            P("wide"),
            P("wide"),
            P(None, "narrow"),
            P(None, "narrow"),
            P("wide", None, "narrow"),
            P("wide", None, "narrow"),
            P("wide", "narrow"),
            P("wide", "narrow"),
            P("wide"),
            P("wide"),
        ),
        out_specs=(
            P("wide", "narrow"),
            P("wide", "narrow"),
            P("wide", None, "narrow"),
            P("wide", None, "narrow"),
        ),
        check_vma=False,
    )
```

```python
import functools
import math

import jax
import jax.numpy as jnp
from jax import lax
from jax.experimental import pallas as pl
from jax.experimental.pallas import tpu as pltpu
from jax.sharding import PartitionSpec as P

HEAD_SIZE = 128

ADAPTER_SCALE = 2.0
NEG_FILL = -1e30
VMEM_LIMIT = 48 * 1024 * 1024
TOKEN = jax.ShapeDtypeStruct((8, 128), jnp.float32)
TOKEN_SPEC = pl.BlockSpec(TOKEN.shape, lambda *_: (0, 0))
SENT = pltpu.HBM
SHORT = pl.CostEstimate(flops=1, bytes_accessed=1, transcendentals=0)


def swap(array, axis, mask):
    count = lax.axis_size(axis)
    return lax.ppermute(array, axis, [(i, i ^ mask) for i in range(count)])


def axis_bits(axis):
    count = lax.axis_size(axis)
    assert count & (count - 1) == 0, "axis size"
    return [1 << k for k in range(count.bit_length() - 1)]


def highest_in(order, mask):
    return [bit for bit in order if bit & mask][-1]


def largest_tile(length, limit):
    tile = length
    while tile > limit and tile % 2 == 0:
        tile //= 2
    return tile


def code_list(chunks, rank):
    return [
        base + j
        for bases, rows in chunks
        for base in bases
        for j in range(rows // rank // len(bases))
    ]


def pick(codes, products, row_codes, rank):
    total = jnp.zeros((rank, products.shape[1]), jnp.float32)
    for k, code in enumerate(row_codes):
        total += jnp.where(codes == code, products[k * rank : (k + 1) * rank], 0.0)
    return total


def spread(codes, values, row_codes, out_ref):
    rank = values.shape[0]
    for k, code in enumerate(row_codes):
        out_ref[k * rank : (k + 1) * rank, :] = jnp.where(codes == code, values, 0.0).astype(
            out_ref.dtype
        )


def join(maps, joined_ref):
    first = 0
    for chunk in maps:
        joined_ref[first : first + chunk.shape[0], :] = chunk[...]
        first += chunk.shape[0]


def times_transposed(maps, tokens):
    return lax.dot_general(
        maps, tokens, (((1,), (1,)), ((), ())), preferred_element_type=jnp.float32
    )


def token_kernel(map_codes, rank, tiles, source_count, has_rows, map_count, codes_ref, *refs):
    refs = list(refs)
    sources = [refs.pop(0) for _ in range(source_count)]
    row_refs = [refs.pop(0) for _ in range(2 * has_rows)]
    maps = refs[:map_count]
    out_ref, sent_ref, joined_ref, *rest = refs[-3 - has_rows :]
    step = pl.program_id(0)

    @pl.when(step == 0)
    def _():
        join(maps, joined_ref)

    def project(tokens):
        products = times_transposed(joined_ref[...], tokens)
        return pick(codes_ref[:, : tokens.shape[0]], products, map_codes, rank)

    def store(total):
        out_ref[...] = total
        sent_ref[...] = total.astype(sent_ref.dtype)

    for k, source_ref in enumerate(sources):
        pl.when(step // tiles == k)(lambda ref=source_ref: store(project(ref[...])))
    if has_rows:
        rows_ref = rest[0]

        @pl.when(step == source_count * tiles)
        def _():
            rows_ref[...] = jnp.zeros_like(rows_ref)
            join(row_refs, rows_ref)
            total = project(rows_ref[...])
            rest_shape = (total.shape[0], out_ref.shape[1] - total.shape[1])
            store(jnp.concatenate([total, jnp.zeros(rest_shape, jnp.float32)], axis=1))


def token_tile(token_count, width=0):
    return largest_tile(token_count, 512 if width > 512 else 1024)


def project_tokens(codes, sources, chunks, rank, rows=(), after=(), cost=SHORT):
    token_count, width = sources[0].shape
    tile = token_tile(token_count, width)
    tiles = token_count // tile
    map_rows = sum(chunk.shape[0] for _, chunk in chunks)
    scratch = [pltpu.VMEM((map_rows, width), jnp.bfloat16)]
    if rows:
        padded = -(-2 * rows[0].shape[0] // 128) * 128
        assert padded <= tile, "row count"
        scratch.append(pltpu.VMEM((padded, width), jnp.bfloat16))
    steps = len(sources) * tiles + bool(rows)
    across = lambda i: (0, i)
    whole = lambda i: (0, 0)
    operands = [codes, *sources, *rows, *[chunk for _, chunk in chunks], *after]
    return pl.pallas_call(
        functools.partial(
            token_kernel,
            code_list([(bases, chunk.shape[0]) for bases, chunk in chunks], rank),
            rank,
            tiles,
            len(sources),
            bool(rows),
            len(chunks),
        ),
        grid=(steps,),
        in_specs=[pl.BlockSpec((1, tile), across)]
        + [
            pl.BlockSpec((tile, width), lambda i, k=k: (jnp.clip(i - k * tiles, 0, tiles - 1), 0))
            for k in range(len(sources))
        ]
        + [pl.BlockSpec(a.shape, whole) for a in rows]
        + [pl.BlockSpec(chunk.shape, whole) for _, chunk in chunks]
        + [pl.BlockSpec(memory_space=pl.ANY) for _ in after],
        out_specs=[pl.BlockSpec((rank, tile), across)] * 2,
        out_shape=[
            jax.ShapeDtypeStruct((rank, steps * tile), dtype)
            for dtype in (jnp.float32, jnp.bfloat16)
        ],
        scratch_shapes=scratch,
        compiler_params=pltpu.CompilerParams(vmem_limit_bytes=VMEM_LIMIT),
        cost_estimate=cost,
    )(*operands)


def delta_kernel(chunk_codes, codes_ref, rank_ref, *refs):
    maps = refs[: len(chunk_codes)]
    own_ref, mate_ref, spread_ref = refs[-3:]
    count = codes_ref.shape[1]
    values = rank_ref[:, :count].astype(jnp.bfloat16).astype(jnp.float32)
    total = jnp.zeros((count, own_ref.shape[1]), jnp.float32)
    for map_codes, chunk in zip(chunk_codes, maps):
        spread(codes_ref[...], values, map_codes, spread_ref)
        total += lax.dot_general(
            spread_ref[...].T.astype(jnp.bfloat16),
            chunk[...],
            (((1,), (0,)), ((), ())),
            preferred_element_type=jnp.float32,
        )
    deltas = ADAPTER_SCALE * total
    own_ref[...] = deltas[: count // 2].astype(own_ref.dtype)
    mate_ref[...] = deltas[count // 2 :].astype(mate_ref.dtype)


def row_deltas(codes, ranks, first, width_of_ranks, chunks, after=()):
    rank = ranks.shape[0]
    row_count = codes.shape[1]
    chunk_rows, width = chunks[0][1].shape
    whole = lambda i: (0, 0)
    return pl.pallas_call(
        functools.partial(
            delta_kernel, [code_list([(bases, chunk_rows)], rank) for bases, _ in chunks]
        ),
        grid=(1,),
        in_specs=[
            pl.BlockSpec(codes.shape, whole),
            pl.BlockSpec((rank, width_of_ranks), lambda i: (0, first // width_of_ranks)),
        ]
        + [pl.BlockSpec((chunk_rows, width), whole) for _ in chunks]
        + [pl.BlockSpec(memory_space=pl.ANY) for _ in after],
        out_specs=[pl.BlockSpec((row_count // 2, width), whole)] * 2,
        out_shape=[jax.ShapeDtypeStruct((row_count // 2, width), jnp.bfloat16)] * 2,
        scratch_shapes=[pltpu.VMEM((chunk_rows, row_count), jnp.float32)],
        compiler_params=pltpu.CompilerParams(vmem_limit_bytes=VMEM_LIMIT),
    )(codes, ranks, *[chunk for _, chunk in chunks], *after)


def cut_kernel(maps_ref, *refs):
    half = len(refs) // 2
    rows = refs[0].shape[0]
    for p in range(half):
        part = maps_ref[p * rows : (p + 1) * rows, :]
        refs[p][...] = part
        refs[half + p][:rows, :] = part


def cut(maps, parts):
    rows, width = maps.shape[0] // parts, maps.shape[1]
    return pl.pallas_call(
        cut_kernel,
        out_shape=[SENT((rows, width), maps.dtype)] * parts
        + [SENT((2 * rows, width), maps.dtype)] * parts,
        compiler_params=pltpu.CompilerParams(vmem_limit_bytes=VMEM_LIMIT),
        cost_estimate=SHORT,
    )(pltpu.with_memory_space_constraint(maps, pltpu.HBM))


def place_kernel(buffer_ref, piece_ref, *refs):
    out_ref, token_ref = refs[-2:]
    out_ref[...] = piece_ref[...]
    token_ref[...] = jnp.zeros_like(token_ref)


def place(buffer, piece, k, after=()):
    return pl.pallas_call(
        place_kernel,
        grid=(1,),
        in_specs=[
            pl.BlockSpec(memory_space=pl.ANY),
            pl.BlockSpec(piece.shape, lambda i: (0, 0)),
        ]
        + [pl.BlockSpec(memory_space=pl.ANY) for _ in after],
        out_specs=[pl.BlockSpec(piece.shape, lambda i: (k, 0)), TOKEN_SPEC],
        out_shape=[SENT(buffer.shape, buffer.dtype), TOKEN],
        input_output_aliases={0: 0},
        compiler_params=pltpu.CompilerParams(vmem_limit_bytes=VMEM_LIMIT),
        cost_estimate=SHORT,
    )(buffer, piece, *after)


def finish_rows_kernel(cached_ref, weight_ref, base_ref, own_ref, mate_ref, attended_ref, fresh_ref):
    delta = own_ref[...].astype(jnp.float32) + mate_ref[...].astype(jnp.float32)
    fresh = (base_ref[...] + delta).astype(jnp.bfloat16)
    fresh_ref[...] = fresh
    heads = cached_ref.shape[1]
    group = heads * HEAD_SIZE // fresh.shape[1]
    for j in range(heads):
        value = slice(j // group * HEAD_SIZE, (j // group + 1) * HEAD_SIZE)
        attended = cached_ref[:, j, :] + weight_ref[:, j, :] * fresh[:, value].astype(jnp.float32)
        attended_ref[:, j * HEAD_SIZE : (j + 1) * HEAD_SIZE] = attended.astype(jnp.bfloat16)


def finish_rows(cached, own_weight, base_values, own_delta, mate_delta):
    row_count, heads, size = cached.shape
    return pl.pallas_call(
        finish_rows_kernel,
        out_shape=[
            jax.ShapeDtypeStruct((row_count, heads * size), jnp.bfloat16),
            jax.ShapeDtypeStruct(base_values.shape, jnp.bfloat16),
        ],
        compiler_params=pltpu.CompilerParams(vmem_limit_bytes=VMEM_LIMIT),
        cost_estimate=SHORT,
    )(cached, own_weight, base_values, own_delta, mate_delta)


def gradient_kernel(
    row_codes, arrived_counts, codes_ref, rewards_ref, factor_ref, own_ref, mate_ref, *refs
):
    arrived = list(refs[: sum(arrived_counts)])
    *outs, token_ref, spread_ref = refs[-2 - len(arrived_counts) :]
    token_count = own_ref.shape[0]

    @pl.when(pl.program_id(0) == 0)
    def _():
        token_ref[...] = jnp.zeros_like(token_ref)
        scale = ADAPTER_SCALE * rewards_ref[...].astype(jnp.float32)
        scaled = (scale * factor_ref[...]).astype(jnp.bfloat16).astype(jnp.float32)
        spread(codes_ref[...], scaled, row_codes, spread_ref)

    total = jnp.dot(
        spread_ref[:, :token_count], own_ref[...], preferred_element_type=jnp.float32
    ) + jnp.dot(spread_ref[:, token_count:], mate_ref[...], preferred_element_type=jnp.float32)
    first = 0
    for out_ref, count in zip(outs, arrived_counts):
        rows = out_ref.shape[0]
        piece = total[first : first + rows]
        for _ in range(count):
            piece += arrived.pop(0)[...].astype(jnp.float32)
        out_ref[...] = piece.astype(out_ref.dtype)
        first += rows


def gradient_chunks(codes, rewards, factor, own, mate, chunks, after=(), cost=SHORT):
    rank = factor.shape[0]
    token_count, width = own.shape
    tile = largest_tile(width, 512)
    out_rows = [adapters * rank for _, adapters, _, _ in chunks]
    arrived = [(a, rows) for (_, _, _, arrays), rows in zip(chunks, out_rows) for a in arrays]
    whole = lambda i: (0, 0)
    across = lambda i: (0, i)
    return pl.pallas_call(
        functools.partial(
            gradient_kernel,
            code_list([(chunk[0], rows) for chunk, rows in zip(chunks, out_rows)], rank),
            [len(arrays) for _, _, _, arrays in chunks],
        ),
        grid=(width // tile,),
        in_specs=[
            pl.BlockSpec((1, 2 * token_count), whole),
            pl.BlockSpec(rewards.shape, whole),
            pl.BlockSpec((rank, 2 * token_count), whole),
            pl.BlockSpec((token_count, tile), across),
            pl.BlockSpec((token_count, tile), across),
        ]
        + [pl.BlockSpec((rows, tile), across) for _, rows in arrived]
        + [pl.BlockSpec(memory_space=pl.ANY) for _ in after],
        out_specs=[pl.BlockSpec((rows, tile), across) for rows in out_rows] + [TOKEN_SPEC],
        out_shape=[
            (SENT if dtype == jnp.bfloat16 else jax.ShapeDtypeStruct)((rows, width), dtype)
            for rows, (_, _, dtype, _) in zip(out_rows, chunks)
        ]
        + [TOKEN],
        scratch_shapes=[pltpu.VMEM((sum(out_rows), 2 * token_count), jnp.bfloat16)],
        compiler_params=pltpu.CompilerParams(vmem_limit_bytes=VMEM_LIMIT),
        cost_estimate=cost,
    )(codes, rewards, factor, own, mate, *[a for a, _ in arrived], *after)


def add_kernel(groups, *refs):
    starts, refs = refs[: len(groups)], refs[len(groups) :]
    *outs, token_ref = refs[-1 - len(groups) :]
    token_ref[...] = jnp.zeros_like(token_ref)
    arrived = list(refs)
    for places, start_ref, out_ref in zip(groups, starts, outs):
        rows = out_ref.shape[0] // len(places)
        for p, firsts in enumerate(places):
            part = slice(p * rows, (p + 1) * rows)
            total = start_ref[part, :]
            for k in firsts:
                total += arrived.pop(0)[k * rows : (k + 1) * rows, :].astype(jnp.float32)
            out_ref[part, :] = total.astype(out_ref.dtype)


def add_arrived(groups, after=(), dtype=jnp.bfloat16):
    width = groups[0][0].shape[1]
    tile = largest_tile(width, 1024)
    arrays = [start for start, _ in groups]
    arrays += [a for _, parts in groups for arrived in parts for a, _ in arrived]
    across = lambda i: (0, i)
    return pl.pallas_call(
        functools.partial(
            add_kernel, [[[k for _, k in arrived] for arrived in parts] for _, parts in groups]
        ),
        grid=(width // tile,),
        in_specs=[pl.BlockSpec((a.shape[0], tile), across) for a in arrays]
        + [pl.BlockSpec(memory_space=pl.ANY) for _ in after],
        out_specs=[pl.BlockSpec((start.shape[0], tile), across) for start, _ in groups]
        + [TOKEN_SPEC],
        out_shape=[
            (SENT if dtype == jnp.bfloat16 else jax.ShapeDtypeStruct)(start.shape, dtype)
            for start, _ in groups
        ]
        + [TOKEN],
        compiler_params=pltpu.CompilerParams(vmem_limit_bytes=VMEM_LIMIT),
        cost_estimate=SHORT,
    )(*arrays, *after)


def wait_for(array, *others):
    return lax.optimization_barrier((array, *others))[0]


def step_kernel(piece_ref, came_ref, *refs):
    out_ref, sent_ref = refs[-2:]
    total = piece_ref[...] + came_ref[...].astype(jnp.float32)
    out_ref[...] = total
    sent_ref[...] = total.astype(sent_ref.dtype)


def sum_over(axis, piece, sent, waits=()):
    for k, bit in enumerate(axis_bits(axis)):
        came = swap(sent, axis, bit)
        after = waits[k] if k < len(waits) else ()
        whole = pl.BlockSpec(piece.shape, lambda: (0, 0))
        piece, sent = pl.pallas_call(
            step_kernel,
            in_specs=[whole, whole] + [pl.BlockSpec(memory_space=pl.ANY) for _ in after],
            out_specs=[whole, whole],
            out_shape=[
                jax.ShapeDtypeStruct(piece.shape, dtype) for dtype in (jnp.float32, jnp.bfloat16)
            ],
            compiler_params=pltpu.CompilerParams(vmem_limit_bytes=VMEM_LIMIT),
            cost_estimate=SHORT,
        )(piece, came, *after)
    return piece


def attend_kernel(kv_local, lengths_ref, queries_ref, keys_ref, values_ref, fresh_ref, *refs):
    out_ref, own_ref = refs[-2:]
    block, heads, size = queries_ref.shape
    slots = keys_ref.shape[1]
    group = heads // kv_local
    first_row = pl.program_id(0) * block
    inverse = 1.0 / math.sqrt(size)
    head_of = lax.broadcasted_iota(jnp.int32, (heads, slots), 0) // group
    slot = lax.broadcasted_iota(jnp.int32, (heads, slots), 1)

    def by_head(pieces):
        chosen = pieces[0]
        for h, piece in enumerate(pieces[1:], 1):
            chosen = jnp.where(head_of[:, : piece.shape[1]] == h, piece, chosen)
        return chosen

    scores, own_scores = [], []
    for r in range(block):
        queries = queries_ref[r]
        products = by_head(
            [
                times_transposed(queries, keys_ref[r, :, h * size : (h + 1) * size])
                for h in range(kv_local)
            ]
        )
        scores.append(jnp.where(slot < lengths_ref[first_row + r], inverse * products, NEG_FILL))
        fresh = by_head(
            [
                jnp.broadcast_to(fresh_ref[r : r + 1, h * size : (h + 1) * size], (heads, size))
                for h in range(kv_local)
            ]
        )
        own_scores.append(queries.astype(jnp.float32) * fresh)
    scores = jnp.concatenate(scores)
    own_score = inverse * jnp.sum(jnp.concatenate(own_scores), axis=1, keepdims=True)
    highest = jnp.maximum(jnp.max(scores, axis=1, keepdims=True), own_score)
    cache_exp = jnp.exp(scores - highest)
    own_exp = jnp.exp(own_score - highest)
    denominator = jnp.sum(cache_exp, axis=1, keepdims=True) + own_exp
    weights = cache_exp / denominator
    own_weight = (own_exp / denominator).astype(jnp.bfloat16).astype(jnp.float32)
    for r in range(block):
        mine = slice(r * heads, (r + 1) * heads)
        row_weights = weights[mine].astype(jnp.bfloat16)
        out_ref[r] = by_head(
            [
                jnp.dot(
                    row_weights,
                    values_ref[r, :, h * size : (h + 1) * size],
                    preferred_element_type=jnp.float32,
                )
                for h in range(kv_local)
            ]
        )
        own_ref[r] = jnp.broadcast_to(own_weight[mine], (heads, size))


def attend_cached(queries, cached_key_rows, cached_value_rows, lengths, fresh_keys, after=()):
    row_count, slots, kv_width = cached_key_rows.shape
    heads = queries.shape[1] // HEAD_SIZE
    block = largest_tile(row_count, 8)
    rows_of = lambda i, *_: (i, 0, 0)
    head_spec = pl.BlockSpec((block, heads, HEAD_SIZE), rows_of)
    cache_spec = pl.BlockSpec((block, slots, kv_width), rows_of)
    shape = (row_count, heads, HEAD_SIZE)
    return pl.pallas_call(
        functools.partial(attend_kernel, kv_width // HEAD_SIZE),
        grid_spec=pltpu.PrefetchScalarGridSpec(
            num_scalar_prefetch=1,
            grid=(row_count // block,),
            in_specs=[
                head_spec,
                cache_spec,
                cache_spec,
                pl.BlockSpec((block, kv_width), lambda i, *_: (i, 0)),
            ]
            + [pl.BlockSpec(memory_space=pl.ANY) for _ in after],
            out_specs=[head_spec, head_spec],
        ),
        out_shape=[jax.ShapeDtypeStruct(shape, jnp.float32)] * 2,
        compiler_params=pltpu.CompilerParams(vmem_limit_bytes=VMEM_LIMIT),
        cost_estimate=SHORT,
    )(
        lengths,
        queries.reshape(shape),
        pltpu.with_memory_space_constraint(cached_key_rows, pltpu.HBM),
        pltpu.with_memory_space_constraint(cached_value_rows, pltpu.HBM),
        fresh_keys.astype(jnp.float32),
        *after,
    )


def per_device(
    decode_hidden_input,
    queries,
    cached_key_rows,
    cached_value_rows,
    lengths,
    decode_adapter_index,
    key_matrix,
    value_matrix,
    adapter_down_map,
    adapter_up_map,
    training_hidden_input,
    cotangent,
    training_adapter_index,
    rewards,
):
    core_bit, *chip_bits = axis_bits("wide")
    masks = [m for m in range(lax.axis_size("wide")) if not m & core_bit]
    me = lax.axis_index("wide")
    owner_totals, rank, down_width = adapter_down_map.shape
    up_width = adapter_up_map.shape[2]
    row_count = decode_hidden_input.shape[0]
    token_count = training_hidden_input.shape[0]
    parts = len(chip_bits) if owner_totals % len(chip_bits) == 0 else 1
    orders = [chip_bits[p:] + chip_bits[:p] for p in range(parts)]
    part_adapters = owner_totals // parts
    part_rows = part_adapters * rank

    flattened_down = adapter_down_map.reshape(-1, down_width)
    flattened_up = adapter_up_map.reshape(-1, up_width)

    far = [m for m in masks if m.bit_count() > 1]
    near = [m for m in masks if m.bit_count() == 1]

    numbers = jnp.concatenate([training_adapter_index, rewards, decode_adapter_index])
    mate_numbers = swap(numbers, "wide", core_bit)
    mate_cotangent = swap(wait_for(cotangent, mate_numbers), "wide", core_bit)
    up_maps = {0: flattened_up}
    own_parts = cut(flattened_down, parts)
    own_parts, own_buffers = own_parts[:parts], own_parts[parts:]
    for m in near:
        up_maps[m] = swap(wait_for(flattened_up, *own_parts), "wide", m)
    for m in far:
        up_maps[m] = swap(wait_for(flattened_up, mate_numbers), "wide", m)
    mate_hidden = swap(wait_for(training_hidden_input, mate_numbers), "wide", core_bit)
    decode_slice = lax.dynamic_slice_in_dim(
        decode_hidden_input, lax.axis_index("narrow") * down_width, down_width, 1
    )
    mate_slice = swap(wait_for(decode_slice, mate_cotangent), "wide", core_bit)

    def codes_of(ids):
        return (((ids // owner_totals) ^ me) * owner_totals + ids % owner_totals)[None, :]

    token_codes = codes_of(
        jnp.concatenate([training_adapter_index, mate_numbers[:token_count]])
    )
    token_rewards = jnp.concatenate([rewards, mate_numbers[token_count : 2 * token_count]])[
        None, :
    ]
    row_codes = codes_of(
        jnp.concatenate([decode_adapter_index, mate_numbers[2 * token_count :]])
    )
    tile = token_tile(token_count, down_width)
    all_codes = jnp.concatenate(
        [token_codes, jnp.pad(row_codes, ((0, 0), (0, tile - 2 * row_count)), constant_values=-1)],
        axis=1,
    )
    up_chunks = [([m * owner_totals], up_maps[m]) for m in masks]
    hidden_rows = wait_for(decode_hidden_input, mate_numbers, *[up_maps[m] for m in near])
    fresh_keys = jnp.dot(
        hidden_rows, key_matrix, preferred_element_type=jnp.float32
    ).astype(jnp.bfloat16)
    base_values = jnp.dot(hidden_rows, value_matrix, preferred_element_type=jnp.float32)

    cached, own_weight = attend_cached(
        queries, cached_key_rows, cached_value_rows, lengths, fresh_keys
    )

    stages, second_sent = [], []
    down_parts = {(0, p): own_parts[p] for p in range(parts)}
    for p, order in enumerate(orders):
        held = [0]
        for bit in order:
            sent = own_parts[p]
            if len(held) > 1:
                sent = own_buffers[p]
                if len(held) > 2:
                    sent = jnp.pad(sent, ((0, (len(held) - 2) * part_rows), (0, 0)))
                for k, m in enumerate(held[1:], 1):
                    sent, token = place(sent, down_parts[m, p], k, (cached, base_values))
                    second_sent.append(token)
            came = swap(sent, "wide", bit)
            for k, m in enumerate(held):
                down_parts[m | bit, p] = came[k * part_rows : (k + 1) * part_rows]
            if bit == order[0]:
                down_stages = [(bit, p, [bit], came)]
            else:
                down_stages.append((bit, p, [m | bit for m in held], came))
            held = held + [m | bit for m in held]
        stages.extend(down_stages)
    last_maps = [came for bit, p, _, came in stages if bit == orders[p][-1]]
    first_maps = [came for bit, p, _, came in stages if bit == orders[p][0]]

    def down_code(m, p):
        return m * owner_totals + p * part_adapters

    down_chunks = [([0], flattened_down)] + [
        ([down_code(m, p) for m in came_from], came) for _, p, came_from, came in stages
    ]

    part_back, sent_back = project_tokens(
        all_codes,
        [cotangent, mate_cotangent],
        up_chunks,
        rank,
        after=second_sent,
    )
    back = sum_over("narrow", part_back, sent_back)

    groups = {}
    for m in far + near:
        for p, order in enumerate(orders):
            level = max(k for k, bit in enumerate(order) if m & bit)
            groups.setdefault((level, p, m == order[level]), []).append(m)
    group_keys = sorted(groups, key=lambda key: (-key[0], key[2]))
    last_level = len(chip_bits) - 1
    own_down, *results, token = gradient_chunks(
        token_codes,
        token_rewards,
        back,
        training_hidden_input,
        mate_hidden,
        [([0], owner_totals, jnp.float32, ())]
        + [
            (
                [down_code(m, p) for m in groups[level, p, direct]],
                part_adapters * len(groups[level, p, direct]),
                jnp.bfloat16 if level == last_level else jnp.float32,
                (),
            )
            for level, p, direct in group_keys
        ],
        (mate_slice,),
    )
    grads = dict(zip(group_keys, results))
    arrived = {(m, p): [] for m in masks for p in range(parts)}

    def send_level(level):
        for key in group_keys:
            if key[0] == level:
                bit = orders[key[1]][level]
                came = swap(wait_for(grads[key], *last_maps), "wide", bit)
                for k, m in enumerate(groups[key]):
                    arrived[m ^ bit, key[1]].append((came, k))

    send_level(last_level)

    part_hidden, sent_hidden = project_tokens(
        all_codes,
        [training_hidden_input, mate_hidden],
        down_chunks,
        rank,
        rows=(decode_slice, mate_slice),
        after=(token,),
    )
    token = sent_hidden
    for level in reversed(range(last_level)):
        added = [key for key in group_keys if key[0] == level]
        *sums, token = add_arrived(
            [(grads[key], [arrived[m, key[1]] for m in groups[key]]) for key in added], (token,)
        )
        grads.update(zip(added, sums))
        send_level(level)
    early = [[arrived[0, p][:-1] for p in range(parts)]]
    own_down, own_token = add_arrived([(own_down, *early)], (token,), jnp.float32)
    last_down = [arrived[0, p][-1:] for p in range(parts)]

    hidden = sum_over(
        "narrow",
        part_hidden,
        sent_hidden,
        [(token,), (own_token,)],
    )
    own_up, *up_results, token = gradient_chunks(
        token_codes,
        token_rewards,
        hidden,
        cotangent,
        mate_cotangent,
        [([m * owner_totals], owner_totals, jnp.bfloat16 if m else jnp.float32, ()) for m in masks],
    )
    own_delta, mate_delta = row_deltas(
        row_codes, hidden, 2 * token_count, tile, up_chunks, (token,)
    )
    mate_delta = wait_for(mate_delta, *[came for part in last_down for came, _ in part])
    came_up = [(swap(result, "wide", m), 0) for m, result in zip(masks[1:], up_results)]
    grad_down, token = add_arrived([(own_down, last_down)], (), jnp.float32)
    attended, fresh_values = finish_rows(
        cached, own_weight, base_values, own_delta, swap(mate_delta, "wide", core_bit)
    )
    grad_up, _ = add_arrived([(own_up, [came_up])], (token,), jnp.float32)
    return (
        attended,
        fresh_values,
        grad_down.reshape(adapter_down_map.shape),
        grad_up.reshape(adapter_up_map.shape),
    )


def solution(mesh):
    return jax.shard_map(
        per_device,
        mesh=mesh,
        in_specs=(
            P("wide", None),
            P("wide", "narrow"),
            P("wide", None, "narrow"),
            P("wide", None, "narrow"),
            P("wide"),
            P("wide"),
            P(None, "narrow"),
            P(None, "narrow"),
            P("wide", None, "narrow"),
            P("wide", None, "narrow"),
            P("wide", "narrow"),
            P("wide", "narrow"),
            P("wide"),
            P("wide"),
        ),
        out_specs=(
            P("wide", "narrow"),
            P("wide", "narrow"),
            P("wide", None, "narrow"),
            P("wide", None, "narrow"),
        ),
        check_vma=False,
    )
```

```python
import functools
import math

import jax
import jax.numpy as jnp
from jax import lax
from jax.experimental import pallas as pl
from jax.experimental.pallas import tpu as pltpu
from jax.sharding import PartitionSpec as P

HEAD_SIZE = 128

ADAPTER_SCALE = 2.0
NEG_FILL = -1e30
VMEM_LIMIT = 48 * 1024 * 1024
TOKEN = jax.ShapeDtypeStruct((8, 128), jnp.float32)
TOKEN_SPEC = pl.BlockSpec(TOKEN.shape, lambda *_: (0, 0))
SENT = pltpu.HBM
SHORT = pl.CostEstimate(flops=1, bytes_accessed=1, transcendentals=0)


def swap(array, axis, mask):
    count = lax.axis_size(axis)
    return lax.ppermute(array, axis, [(i, i ^ mask) for i in range(count)])


def axis_bits(axis):
    count = lax.axis_size(axis)
    assert count & (count - 1) == 0, "axis size"
    return [1 << k for k in range(count.bit_length() - 1)]


def highest_in(order, mask):
    return [bit for bit in order if bit & mask][-1]


def largest_tile(length, limit):
    tile = length
    while tile > limit and tile % 2 == 0:
        tile //= 2
    return tile


def code_list(chunks, rank):
    return [
        base + j
        for bases, rows in chunks
        for base in bases
        for j in range(rows // rank // len(bases))
    ]


def pick(codes, products, row_codes, rank):
    total = jnp.zeros((rank, products.shape[1]), jnp.float32)
    for k, code in enumerate(row_codes):
        total += jnp.where(codes == code, products[k * rank : (k + 1) * rank], 0.0)
    return total


def spread(codes, values, row_codes, out_ref):
    rank = values.shape[0]
    for k, code in enumerate(row_codes):
        out_ref[k * rank : (k + 1) * rank, :] = jnp.where(codes == code, values, 0.0).astype(
            out_ref.dtype
        )


def join(maps, joined_ref):
    first = 0
    for chunk in maps:
        joined_ref[first : first + chunk.shape[0], :] = chunk[...]
        first += chunk.shape[0]


def times_transposed(maps, tokens):
    return lax.dot_general(
        maps, tokens, (((1,), (1,)), ((), ())), preferred_element_type=jnp.float32
    )


def token_kernel(map_codes, rank, tiles, source_count, has_rows, map_count, codes_ref, *refs):
    refs = list(refs)
    sources = [refs.pop(0) for _ in range(source_count)]
    row_refs = [refs.pop(0) for _ in range(2 * has_rows)]
    maps = refs[:map_count]
    out_ref, sent_ref, joined_ref, *rest = refs[-3 - has_rows :]
    step = pl.program_id(0)

    @pl.when(step == 0)
    def _():
        join(maps, joined_ref)

    def project(tokens):
        products = times_transposed(joined_ref[...], tokens)
        return pick(codes_ref[:, : tokens.shape[0]], products, map_codes, rank)

    def store(total):
        out_ref[...] = total
        sent_ref[...] = total.astype(sent_ref.dtype)

    for k, source_ref in enumerate(sources):
        pl.when(step // tiles == k)(lambda ref=source_ref: store(project(ref[...])))
    if has_rows:
        rows_ref = rest[0]

        @pl.when(step == source_count * tiles)
        def _():
            rows_ref[...] = jnp.zeros_like(rows_ref)
            join(row_refs, rows_ref)
            total = project(rows_ref[...])
            rest_shape = (total.shape[0], out_ref.shape[1] - total.shape[1])
            store(jnp.concatenate([total, jnp.zeros(rest_shape, jnp.float32)], axis=1))


def token_tile(token_count, width=0):
    return largest_tile(token_count, 512 if width > 512 else 1024)


def project_tokens(codes, sources, chunks, rank, rows=(), after=(), cost=SHORT):
    token_count, width = sources[0].shape
    tile = token_tile(token_count, width)
    tiles = token_count // tile
    map_rows = sum(chunk.shape[0] for _, chunk in chunks)
    scratch = [pltpu.VMEM((map_rows, width), jnp.bfloat16)]
    if rows:
        padded = -(-2 * rows[0].shape[0] // 128) * 128
        assert padded <= tile, "row count"
        scratch.append(pltpu.VMEM((padded, width), jnp.bfloat16))
    steps = len(sources) * tiles + bool(rows)
    across = lambda i: (0, i)
    whole = lambda i: (0, 0)
    operands = [codes, *sources, *rows, *[chunk for _, chunk in chunks], *after]
    return pl.pallas_call(
        functools.partial(
            token_kernel,
            code_list([(bases, chunk.shape[0]) for bases, chunk in chunks], rank),
            rank,
            tiles,
            len(sources),
            bool(rows),
            len(chunks),
        ),
        grid=(steps,),
        in_specs=[pl.BlockSpec((1, tile), across)]
        + [
            pl.BlockSpec((tile, width), lambda i, k=k: (jnp.clip(i - k * tiles, 0, tiles - 1), 0))
            for k in range(len(sources))
        ]
        + [pl.BlockSpec(a.shape, whole) for a in rows]
        + [pl.BlockSpec(chunk.shape, whole) for _, chunk in chunks]
        + [pl.BlockSpec(memory_space=pl.ANY) for _ in after],
        out_specs=[pl.BlockSpec((rank, tile), across)] * 2,
        out_shape=[
            jax.ShapeDtypeStruct((rank, steps * tile), dtype)
            for dtype in (jnp.float32, jnp.bfloat16)
        ],
        scratch_shapes=scratch,
        compiler_params=pltpu.CompilerParams(vmem_limit_bytes=VMEM_LIMIT),
        cost_estimate=cost,
    )(*operands)


def delta_kernel(chunk_codes, codes_ref, rank_ref, *refs):
    maps = refs[: len(chunk_codes)]
    own_ref, mate_ref, spread_ref = refs[-3:]
    count = codes_ref.shape[1]
    values = rank_ref[:, :count].astype(jnp.bfloat16).astype(jnp.float32)
    total = jnp.zeros((count, own_ref.shape[1]), jnp.float32)
    for map_codes, chunk in zip(chunk_codes, maps):
        spread(codes_ref[...], values, map_codes, spread_ref)
        total += lax.dot_general(
            spread_ref[...].T.astype(jnp.bfloat16),
            chunk[...],
            (((1,), (0,)), ((), ())),
            preferred_element_type=jnp.float32,
        )
    deltas = ADAPTER_SCALE * total
    own_ref[...] = deltas[: count // 2].astype(own_ref.dtype)
    mate_ref[...] = deltas[count // 2 :].astype(mate_ref.dtype)


def row_deltas(codes, ranks, first, width_of_ranks, chunks, after=()):
    rank = ranks.shape[0]
    row_count = codes.shape[1]
    chunk_rows, width = chunks[0][1].shape
    whole = lambda i: (0, 0)
    return pl.pallas_call(
        functools.partial(
            delta_kernel, [code_list([(bases, chunk_rows)], rank) for bases, _ in chunks]
        ),
        grid=(1,),
        in_specs=[
            pl.BlockSpec(codes.shape, whole),
            pl.BlockSpec((rank, width_of_ranks), lambda i: (0, first // width_of_ranks)),
        ]
        + [pl.BlockSpec((chunk_rows, width), whole) for _ in chunks]
        + [pl.BlockSpec(memory_space=pl.ANY) for _ in after],
        out_specs=[pl.BlockSpec((row_count // 2, width), whole)] * 2,
        out_shape=[jax.ShapeDtypeStruct((row_count // 2, width), jnp.bfloat16)] * 2,
        scratch_shapes=[pltpu.VMEM((chunk_rows, row_count), jnp.float32)],
        compiler_params=pltpu.CompilerParams(vmem_limit_bytes=VMEM_LIMIT),
    )(codes, ranks, *[chunk for _, chunk in chunks], *after)


def cut_kernel(maps_ref, *refs):
    half = len(refs) // 2
    rows = refs[0].shape[0]
    for p in range(half):
        part = maps_ref[p * rows : (p + 1) * rows, :]
        refs[p][...] = part
        refs[half + p][:rows, :] = part


def cut(maps, parts):
    rows, width = maps.shape[0] // parts, maps.shape[1]
    return pl.pallas_call(
        cut_kernel,
        out_shape=[SENT((rows, width), maps.dtype)] * parts
        + [SENT((2 * rows, width), maps.dtype)] * parts,
        compiler_params=pltpu.CompilerParams(vmem_limit_bytes=VMEM_LIMIT),
        cost_estimate=SHORT,
    )(pltpu.with_memory_space_constraint(maps, pltpu.HBM))


def place_kernel(buffer_ref, piece_ref, *refs):
    out_ref, token_ref = refs[-2:]
    out_ref[...] = piece_ref[...]
    token_ref[...] = jnp.zeros_like(token_ref)


def place(buffer, piece, k, after=()):
    return pl.pallas_call(
        place_kernel,
        grid=(1,),
        in_specs=[
            pl.BlockSpec(memory_space=pl.ANY),
            pl.BlockSpec(piece.shape, lambda i: (0, 0)),
        ]
        + [pl.BlockSpec(memory_space=pl.ANY) for _ in after],
        out_specs=[pl.BlockSpec(piece.shape, lambda i: (k, 0)), TOKEN_SPEC],
        out_shape=[SENT(buffer.shape, buffer.dtype), TOKEN],
        input_output_aliases={0: 0},
        compiler_params=pltpu.CompilerParams(vmem_limit_bytes=VMEM_LIMIT),
        cost_estimate=SHORT,
    )(buffer, piece, *after)


def finish_rows_kernel(
    cached_ref, weight_ref, base_ref, own_ref, mate_ref, attended_ref, fresh_ref, token_ref
):
    token_ref[...] = jnp.zeros_like(token_ref)
    delta = own_ref[...].astype(jnp.float32) + mate_ref[...].astype(jnp.float32)
    fresh = (base_ref[...] + delta).astype(jnp.bfloat16)
    fresh_ref[...] = fresh
    heads = cached_ref.shape[1]
    group = heads * HEAD_SIZE // fresh.shape[1]
    for j in range(heads):
        value = slice(j // group * HEAD_SIZE, (j // group + 1) * HEAD_SIZE)
        attended = cached_ref[:, j, :] + weight_ref[:, j, :] * fresh[:, value].astype(jnp.float32)
        attended_ref[:, j * HEAD_SIZE : (j + 1) * HEAD_SIZE] = attended.astype(jnp.bfloat16)


def finish_rows(cached, own_weight, base_values, own_delta, mate_delta):
    row_count, heads, size = cached.shape
    return pl.pallas_call(
        finish_rows_kernel,
        out_shape=[
            jax.ShapeDtypeStruct((row_count, heads * size), jnp.bfloat16),
            jax.ShapeDtypeStruct(base_values.shape, jnp.bfloat16),
            TOKEN,
        ],
        compiler_params=pltpu.CompilerParams(vmem_limit_bytes=VMEM_LIMIT),
        cost_estimate=SHORT,
    )(cached, own_weight, base_values, own_delta, mate_delta)


def gradient_kernel(
    row_codes, arrived_counts, codes_ref, rewards_ref, factor_ref, own_ref, mate_ref, *refs
):
    arrived = list(refs[: sum(arrived_counts)])
    *outs, token_ref, spread_ref = refs[-2 - len(arrived_counts) :]
    token_count = own_ref.shape[0]

    @pl.when(pl.program_id(0) == 0)
    def _():
        token_ref[...] = jnp.zeros_like(token_ref)
        scale = ADAPTER_SCALE * rewards_ref[...].astype(jnp.float32)
        scaled = (scale * factor_ref[...]).astype(jnp.bfloat16).astype(jnp.float32)
        spread(codes_ref[...], scaled, row_codes, spread_ref)

    total = jnp.dot(
        spread_ref[:, :token_count], own_ref[...], preferred_element_type=jnp.float32
    ) + jnp.dot(spread_ref[:, token_count:], mate_ref[...], preferred_element_type=jnp.float32)
    first = 0
    for out_ref, count in zip(outs, arrived_counts):
        rows = out_ref.shape[0]
        piece = total[first : first + rows]
        for _ in range(count):
            piece += arrived.pop(0)[...].astype(jnp.float32)
        out_ref[...] = piece.astype(out_ref.dtype)
        first += rows


def gradient_chunks(codes, rewards, factor, own, mate, chunks, after=(), cost=SHORT):
    rank = factor.shape[0]
    token_count, width = own.shape
    tile = largest_tile(width, 512)
    out_rows = [adapters * rank for _, adapters, _, _ in chunks]
    arrived = [(a, rows) for (_, _, _, arrays), rows in zip(chunks, out_rows) for a in arrays]
    whole = lambda i: (0, 0)
    across = lambda i: (0, i)
    return pl.pallas_call(
        functools.partial(
            gradient_kernel,
            code_list([(chunk[0], rows) for chunk, rows in zip(chunks, out_rows)], rank),
            [len(arrays) for _, _, _, arrays in chunks],
        ),
        grid=(width // tile,),
        in_specs=[
            pl.BlockSpec((1, 2 * token_count), whole),
            pl.BlockSpec(rewards.shape, whole),
            pl.BlockSpec((rank, 2 * token_count), whole),
            pl.BlockSpec((token_count, tile), across),
            pl.BlockSpec((token_count, tile), across),
        ]
        + [pl.BlockSpec((rows, tile), across) for _, rows in arrived]
        + [pl.BlockSpec(memory_space=pl.ANY) for _ in after],
        out_specs=[pl.BlockSpec((rows, tile), across) for rows in out_rows] + [TOKEN_SPEC],
        out_shape=[
            (SENT if dtype == jnp.bfloat16 else jax.ShapeDtypeStruct)((rows, width), dtype)
            for rows, (_, _, dtype, _) in zip(out_rows, chunks)
        ]
        + [TOKEN],
        scratch_shapes=[pltpu.VMEM((sum(out_rows), 2 * token_count), jnp.bfloat16)],
        compiler_params=pltpu.CompilerParams(vmem_limit_bytes=VMEM_LIMIT),
        cost_estimate=cost,
    )(codes, rewards, factor, own, mate, *[a for a, _ in arrived], *after)


def add_kernel(groups, *refs):
    starts, refs = refs[: len(groups)], refs[len(groups) :]
    *outs, token_ref = refs[-1 - len(groups) :]
    token_ref[...] = jnp.zeros_like(token_ref)
    arrived = list(refs)
    for places, start_ref, out_ref in zip(groups, starts, outs):
        rows = out_ref.shape[0] // len(places)
        for p, firsts in enumerate(places):
            part = slice(p * rows, (p + 1) * rows)
            total = start_ref[part, :]
            for k in firsts:
                total += arrived.pop(0)[k * rows : (k + 1) * rows, :].astype(jnp.float32)
            out_ref[part, :] = total.astype(out_ref.dtype)


def add_arrived(groups, after=(), dtype=jnp.bfloat16):
    width = groups[0][0].shape[1]
    tile = largest_tile(width, 1024)
    arrays = [start for start, _ in groups]
    arrays += [a for _, parts in groups for arrived in parts for a, _ in arrived]
    across = lambda i: (0, i)
    return pl.pallas_call(
        functools.partial(
            add_kernel, [[[k for _, k in arrived] for arrived in parts] for _, parts in groups]
        ),
        grid=(width // tile,),
        in_specs=[pl.BlockSpec((a.shape[0], tile), across) for a in arrays]
        + [pl.BlockSpec(memory_space=pl.ANY) for _ in after],
        out_specs=[pl.BlockSpec((start.shape[0], tile), across) for start, _ in groups]
        + [TOKEN_SPEC],
        out_shape=[
            (SENT if dtype == jnp.bfloat16 else jax.ShapeDtypeStruct)(start.shape, dtype)
            for start, _ in groups
        ]
        + [TOKEN],
        compiler_params=pltpu.CompilerParams(vmem_limit_bytes=VMEM_LIMIT),
        cost_estimate=SHORT,
    )(*arrays, *after)


def wait_for(array, *others):
    return lax.optimization_barrier((array, *others))[0]


def step_kernel(piece_ref, came_ref, *refs):
    out_ref, sent_ref = refs[-2:]
    total = piece_ref[...] + came_ref[...].astype(jnp.float32)
    out_ref[...] = total
    sent_ref[...] = total.astype(sent_ref.dtype)


def sum_over(axis, piece, sent, waits=()):
    for k, bit in enumerate(axis_bits(axis)):
        came = swap(sent, axis, bit)
        after = waits[k] if k < len(waits) else ()
        whole = pl.BlockSpec(piece.shape, lambda: (0, 0))
        piece, sent = pl.pallas_call(
            step_kernel,
            in_specs=[whole, whole] + [pl.BlockSpec(memory_space=pl.ANY) for _ in after],
            out_specs=[whole, whole],
            out_shape=[
                jax.ShapeDtypeStruct(piece.shape, dtype) for dtype in (jnp.float32, jnp.bfloat16)
            ],
            compiler_params=pltpu.CompilerParams(vmem_limit_bytes=VMEM_LIMIT),
            cost_estimate=SHORT,
        )(piece, came, *after)
    return piece


def attend_kernel(kv_local, lengths_ref, queries_ref, keys_ref, values_ref, fresh_ref, *refs):
    out_ref, own_ref = refs[-2:]
    block, heads, size = queries_ref.shape
    slots = keys_ref.shape[1]
    group = heads // kv_local
    first_row = pl.program_id(0) * block
    inverse = 1.0 / math.sqrt(size)
    head_of = lax.broadcasted_iota(jnp.int32, (heads, size), 0) // group
    slot = lax.broadcasted_iota(jnp.int32, (heads, slots), 1)

    scores, own_scores = [], []
    for r in range(block):
        queries = queries_ref[r].astype(jnp.float32)
        spread_queries = jnp.concatenate(
            [jnp.where(head_of == h, queries, 0.0) for h in range(kv_local)], axis=1
        )
        products = times_transposed(spread_queries.astype(jnp.bfloat16), keys_ref[r])
        scores.append(jnp.where(slot < lengths_ref[first_row + r], inverse * products, NEG_FILL))
        own_scores.append(spread_queries * fresh_ref[r : r + 1, :])
    scores = jnp.concatenate(scores)
    own_score = inverse * jnp.sum(jnp.concatenate(own_scores), axis=1, keepdims=True)
    highest = jnp.maximum(jnp.max(scores, axis=1, keepdims=True), own_score)
    cache_exp = jnp.exp(scores - highest)
    own_exp = jnp.exp(own_score - highest)
    denominator = jnp.sum(cache_exp, axis=1, keepdims=True) + own_exp
    weights = cache_exp / denominator
    own_weight = (own_exp / denominator).astype(jnp.bfloat16).astype(jnp.float32)
    for r in range(block):
        mine = slice(r * heads, (r + 1) * heads)
        summed = jnp.dot(
            weights[mine].astype(jnp.bfloat16), values_ref[r], preferred_element_type=jnp.float32
        )
        chosen = summed[:, :size]
        for h in range(1, kv_local):
            chosen = jnp.where(head_of == h, summed[:, h * size : (h + 1) * size], chosen)
        out_ref[r] = chosen
        own_ref[r] = jnp.broadcast_to(own_weight[mine], (heads, size))


def attend_cached(queries, cached_key_rows, cached_value_rows, lengths, fresh_keys, after=()):
    row_count, slots, kv_width = cached_key_rows.shape
    heads = queries.shape[1] // HEAD_SIZE
    block = largest_tile(row_count, 8)
    rows_of = lambda i, *_: (i, 0, 0)
    head_spec = pl.BlockSpec((block, heads, HEAD_SIZE), rows_of)
    cache_spec = pl.BlockSpec((block, slots, kv_width), rows_of)
    shape = (row_count, heads, HEAD_SIZE)
    return pl.pallas_call(
        functools.partial(attend_kernel, kv_width // HEAD_SIZE),
        grid_spec=pltpu.PrefetchScalarGridSpec(
            num_scalar_prefetch=1,
            grid=(row_count // block,),
            in_specs=[
                head_spec,
                cache_spec,
                cache_spec,
                pl.BlockSpec((block, kv_width), lambda i, *_: (i, 0)),
            ]
            + [pl.BlockSpec(memory_space=pl.ANY) for _ in after],
            out_specs=[head_spec, head_spec],
        ),
        out_shape=[jax.ShapeDtypeStruct(shape, jnp.float32)] * 2,
        compiler_params=pltpu.CompilerParams(vmem_limit_bytes=VMEM_LIMIT),
        cost_estimate=SHORT,
    )(
        lengths,
        queries.reshape(shape),
        pltpu.with_memory_space_constraint(cached_key_rows, pltpu.HBM),
        pltpu.with_memory_space_constraint(cached_value_rows, pltpu.HBM),
        fresh_keys.astype(jnp.float32),
        *after,
    )


def per_device(
    decode_hidden_input,
    queries,
    cached_key_rows,
    cached_value_rows,
    lengths,
    decode_adapter_index,
    key_matrix,
    value_matrix,
    adapter_down_map,
    adapter_up_map,
    training_hidden_input,
    cotangent,
    training_adapter_index,
    rewards,
):
    core_bit, *chip_bits = axis_bits("wide")
    masks = [m for m in range(lax.axis_size("wide")) if not m & core_bit]
    me = lax.axis_index("wide")
    owner_totals, rank, down_width = adapter_down_map.shape
    up_width = adapter_up_map.shape[2]
    row_count = decode_hidden_input.shape[0]
    token_count = training_hidden_input.shape[0]
    parts = len(chip_bits) if owner_totals % len(chip_bits) == 0 else 1
    orders = [chip_bits[p:] + chip_bits[:p] for p in range(parts)]
    part_adapters = owner_totals // parts
    part_rows = part_adapters * rank

    flattened_down = adapter_down_map.reshape(-1, down_width)
    flattened_up = adapter_up_map.reshape(-1, up_width)

    far = [m for m in masks if m.bit_count() > 1]
    near = [m for m in masks if m.bit_count() == 1]

    numbers = jnp.concatenate([training_adapter_index, rewards, decode_adapter_index])
    mate_numbers = swap(numbers, "wide", core_bit)
    mate_cotangent = swap(wait_for(cotangent, mate_numbers), "wide", core_bit)
    up_maps = {0: flattened_up}
    own_parts = cut(flattened_down, parts)
    own_parts, own_buffers = own_parts[:parts], own_parts[parts:]
    for m in near:
        up_maps[m] = swap(wait_for(flattened_up, *own_parts), "wide", m)
    for m in far:
        up_maps[m] = swap(wait_for(flattened_up, mate_numbers), "wide", m)
    mate_hidden = swap(wait_for(training_hidden_input, mate_numbers), "wide", core_bit)
    decode_slice = lax.dynamic_slice_in_dim(
        decode_hidden_input, lax.axis_index("narrow") * down_width, down_width, 1
    )
    mate_slice = swap(wait_for(decode_slice, mate_cotangent), "wide", core_bit)

    def codes_of(ids):
        return (((ids // owner_totals) ^ me) * owner_totals + ids % owner_totals)[None, :]

    token_codes = codes_of(
        jnp.concatenate([training_adapter_index, mate_numbers[:token_count]])
    )
    token_rewards = jnp.concatenate([rewards, mate_numbers[token_count : 2 * token_count]])[
        None, :
    ]
    row_codes = codes_of(
        jnp.concatenate([decode_adapter_index, mate_numbers[2 * token_count :]])
    )
    tile = token_tile(token_count, down_width)
    all_codes = jnp.concatenate(
        [token_codes, jnp.pad(row_codes, ((0, 0), (0, tile - 2 * row_count)), constant_values=-1)],
        axis=1,
    )
    up_chunks = [([m * owner_totals], up_maps[m]) for m in masks]
    hidden_rows = wait_for(decode_hidden_input, mate_numbers, *[up_maps[m] for m in near])
    fresh_keys = jnp.dot(
        hidden_rows, key_matrix, preferred_element_type=jnp.float32
    ).astype(jnp.bfloat16)
    base_values = jnp.dot(hidden_rows, value_matrix, preferred_element_type=jnp.float32)

    cached, own_weight = attend_cached(
        queries, cached_key_rows, cached_value_rows, lengths, fresh_keys
    )

    stages, second_sent = [], []
    down_parts = {(0, p): own_parts[p] for p in range(parts)}
    for p, order in enumerate(orders):
        held = [0]
        for bit in order:
            sent = own_parts[p]
            if len(held) > 1:
                sent = own_buffers[p]
                if len(held) > 2:
                    sent = jnp.pad(sent, ((0, (len(held) - 2) * part_rows), (0, 0)))
                for k, m in enumerate(held[1:], 1):
                    sent, token = place(sent, down_parts[m, p], k, (cached, base_values))
                    second_sent.append(token)
            came = swap(sent, "wide", bit)
            for k, m in enumerate(held):
                down_parts[m | bit, p] = came[k * part_rows : (k + 1) * part_rows]
            if bit == order[0]:
                down_stages = [(bit, p, [bit], came)]
            else:
                down_stages.append((bit, p, [m | bit for m in held], came))
            held = held + [m | bit for m in held]
        stages.extend(down_stages)
    last_maps = [came for bit, p, _, came in stages if bit == orders[p][-1]]
    first_maps = [came for bit, p, _, came in stages if bit == orders[p][0]]

    def down_code(m, p):
        return m * owner_totals + p * part_adapters

    down_chunks = [([0], flattened_down)] + [
        ([down_code(m, p) for m in came_from], came) for _, p, came_from, came in stages
    ]

    part_back, sent_back = project_tokens(
        all_codes,
        [cotangent, mate_cotangent],
        up_chunks,
        rank,
        after=second_sent,
    )
    back = sum_over("narrow", part_back, sent_back)

    groups = {}
    for m in far + near:
        for p, order in enumerate(orders):
            level = max(k for k, bit in enumerate(order) if m & bit)
            groups.setdefault((level, p, m == order[level]), []).append(m)
    group_keys = sorted(groups, key=lambda key: (-key[0], key[2]))
    last_level = len(chip_bits) - 1
    own_down, *results, token = gradient_chunks(
        token_codes,
        token_rewards,
        back,
        training_hidden_input,
        mate_hidden,
        [([0], owner_totals, jnp.float32, ())]
        + [
            (
                [down_code(m, p) for m in groups[level, p, direct]],
                part_adapters * len(groups[level, p, direct]),
                jnp.bfloat16 if level == last_level else jnp.float32,
                (),
            )
            for level, p, direct in group_keys
        ],
        (mate_slice,),
    )
    grads = dict(zip(group_keys, results))
    arrived = {(m, p): [] for m in masks for p in range(parts)}

    def send_level(level):
        for key in group_keys:
            if key[0] == level:
                bit = orders[key[1]][level]
                came = swap(wait_for(grads[key], *last_maps), "wide", bit)
                for k, m in enumerate(groups[key]):
                    arrived[m ^ bit, key[1]].append((came, k))

    send_level(last_level)

    part_hidden, sent_hidden = project_tokens(
        all_codes,
        [training_hidden_input, mate_hidden],
        down_chunks,
        rank,
        rows=(decode_slice, mate_slice),
        after=(token,),
    )
    token = sent_hidden
    for level in reversed(range(last_level)):
        added = [key for key in group_keys if key[0] == level]
        *sums, token = add_arrived(
            [(grads[key], [arrived[m, key[1]] for m in groups[key]]) for key in added], (token,)
        )
        grads.update(zip(added, sums))
        send_level(level)
    early = [[arrived[0, p][:-1] for p in range(parts)]]
    own_down, own_token = add_arrived([(own_down, *early)], (token,), jnp.float32)
    last_down = [arrived[0, p][-1:] for p in range(parts)]

    hidden = sum_over(
        "narrow",
        part_hidden,
        sent_hidden,
        [(token,), (own_token,)],
    )
    own_up, *up_results, token = gradient_chunks(
        token_codes,
        token_rewards,
        hidden,
        cotangent,
        mate_cotangent,
        [([m * owner_totals], owner_totals, jnp.bfloat16 if m else jnp.float32, ()) for m in masks],
    )
    own_delta, mate_delta = row_deltas(
        row_codes, hidden, 2 * token_count, tile, up_chunks, (token,)
    )
    mate_delta = wait_for(mate_delta, *[came for part in last_down for came, _ in part])
    came_up = [(swap(result, "wide", m), 0) for m, result in zip(masks[1:], up_results)]
    grad_down, token = add_arrived([(own_down, last_down)], (), jnp.float32)
    attended, fresh_values, rows_token = finish_rows(
        cached, own_weight, base_values, own_delta, swap(mate_delta, "wide", core_bit)
    )
    grad_up, _ = add_arrived([(own_up, [came_up])], (token, rows_token), jnp.float32)
    return (
        attended,
        fresh_values,
        grad_down.reshape(adapter_down_map.shape),
        grad_up.reshape(adapter_up_map.shape),
    )


def solution(mesh):
    return jax.shard_map(
        per_device,
        mesh=mesh,
        in_specs=(
            P("wide", None),
            P("wide", "narrow"),
            P("wide", None, "narrow"),
            P("wide", None, "narrow"),
            P("wide"),
            P("wide"),
            P(None, "narrow"),
            P(None, "narrow"),
            P("wide", None, "narrow"),
            P("wide", None, "narrow"),
            P("wide", "narrow"),
            P("wide", "narrow"),
            P("wide"),
            P("wide"),
        ),
        out_specs=(
            P("wide", "narrow"),
            P("wide", "narrow"),
            P("wide", None, "narrow"),
            P("wide", None, "narrow"),
        ),
        check_vma=False,
    )
```

```python
import functools
import math

import jax
import jax.numpy as jnp
from jax import lax
from jax.experimental import pallas as pl
from jax.experimental.pallas import tpu as pltpu
from jax.sharding import PartitionSpec as P

HEAD_SIZE = 128

ADAPTER_SCALE = 2.0
NEG_FILL = -1e30
VMEM_LIMIT = 40 * 1024 * 1024
TOKEN = jax.ShapeDtypeStruct((8, 128), jnp.float32)
TOKEN_SPEC = pl.BlockSpec(TOKEN.shape, lambda *_: (0, 0))
SENT = pltpu.HBM
SHORT = pl.CostEstimate(flops=1, bytes_accessed=1, transcendentals=0)


def swap(array, axis, mask):
    count = lax.axis_size(axis)
    return lax.ppermute(array, axis, [(i, i ^ mask) for i in range(count)])


def axis_bits(axis):
    count = lax.axis_size(axis)
    assert count & (count - 1) == 0, "axis size"
    return [1 << k for k in range(count.bit_length() - 1)]


def highest_in(order, mask):
    return [bit for bit in order if bit & mask][-1]


def largest_tile(length, limit):
    tile = length
    while tile > limit and tile % 2 == 0:
        tile //= 2
    return tile


def code_list(chunks, rank):
    return [
        base + j
        for bases, rows in chunks
        for base in bases
        for j in range(rows // rank // len(bases))
    ]


def pick(codes, products, row_codes, rank):
    total = jnp.zeros((rank, products.shape[1]), jnp.float32)
    for k, code in enumerate(row_codes):
        total += jnp.where(codes == code, products[k * rank : (k + 1) * rank], 0.0)
    return total


def spread(codes, values, row_codes, out_ref):
    rank = values.shape[0]
    for k, code in enumerate(row_codes):
        out_ref[k * rank : (k + 1) * rank, :] = jnp.where(codes == code, values, 0.0).astype(
            out_ref.dtype
        )


def join(maps, joined_ref):
    first = 0
    for chunk in maps:
        joined_ref[first : first + chunk.shape[0], :] = chunk[...]
        first += chunk.shape[0]


def times_transposed(maps, tokens):
    return lax.dot_general(
        maps, tokens, (((1,), (1,)), ((), ())), preferred_element_type=jnp.float32
    )


def token_kernel(map_codes, rank, tiles, source_count, has_rows, map_count, codes_ref, *refs):
    refs = list(refs)
    sources = [refs.pop(0) for _ in range(source_count)]
    row_refs = [refs.pop(0) for _ in range(2 * has_rows)]
    maps = refs[:map_count]
    out_ref, sent_ref, joined_ref, *rest = refs[-3 - has_rows :]
    step = pl.program_id(0)

    @pl.when(step == 0)
    def _():
        join(maps, joined_ref)

    def project(tokens):
        products = times_transposed(joined_ref[...], tokens)
        return pick(codes_ref[:, : tokens.shape[0]], products, map_codes, rank)

    def store(total):
        out_ref[...] = total
        sent_ref[...] = total.astype(sent_ref.dtype)

    for k, source_ref in enumerate(sources):
        pl.when(step // tiles == k)(lambda ref=source_ref: store(project(ref[...])))
    if has_rows:
        rows_ref = rest[0]

        @pl.when(step == source_count * tiles)
        def _():
            rows_ref[...] = jnp.zeros_like(rows_ref)
            join(row_refs, rows_ref)
            total = project(rows_ref[...])
            rest_shape = (total.shape[0], out_ref.shape[1] - total.shape[1])
            store(jnp.concatenate([total, jnp.zeros(rest_shape, jnp.float32)], axis=1))


def token_tile(token_count, width=0):
    return largest_tile(token_count, 512 if width > 512 else 1024)


def project_tokens(codes, sources, chunks, rank, rows=(), after=(), cost=SHORT):
    token_count, width = sources[0].shape
    tile = token_tile(token_count, width)
    tiles = token_count // tile
    map_rows = sum(chunk.shape[0] for _, chunk in chunks)
    scratch = [pltpu.VMEM((map_rows, width), jnp.bfloat16)]
    if rows:
        padded = -(-2 * rows[0].shape[0] // 128) * 128
        assert padded <= tile, "row count"
        scratch.append(pltpu.VMEM((padded, width), jnp.bfloat16))
    steps = len(sources) * tiles + bool(rows)
    across = lambda i: (0, i)
    whole = lambda i: (0, 0)
    operands = [codes, *sources, *rows, *[chunk for _, chunk in chunks], *after]
    return pl.pallas_call(
        functools.partial(
            token_kernel,
            code_list([(bases, chunk.shape[0]) for bases, chunk in chunks], rank),
            rank,
            tiles,
            len(sources),
            bool(rows),
            len(chunks),
        ),
        grid=(steps,),
        in_specs=[pl.BlockSpec((1, tile), across)]
        + [
            pl.BlockSpec((tile, width), lambda i, k=k: (jnp.clip(i - k * tiles, 0, tiles - 1), 0))
            for k in range(len(sources))
        ]
        + [pl.BlockSpec(a.shape, whole) for a in rows]
        + [pl.BlockSpec(chunk.shape, whole) for _, chunk in chunks]
        + [pl.BlockSpec(memory_space=pl.ANY) for _ in after],
        out_specs=[pl.BlockSpec((rank, tile), across)] * 2,
        out_shape=[
            jax.ShapeDtypeStruct((rank, steps * tile), dtype)
            for dtype in (jnp.float32, jnp.bfloat16)
        ],
        scratch_shapes=scratch,
        compiler_params=pltpu.CompilerParams(vmem_limit_bytes=VMEM_LIMIT),
        cost_estimate=cost,
    )(*operands)


def delta_kernel(chunk_codes, codes_ref, rank_ref, *refs):
    maps = refs[: len(chunk_codes)]
    own_ref, mate_ref, spread_ref = refs[-3:]
    count = codes_ref.shape[1]
    values = rank_ref[:, :count].astype(jnp.bfloat16).astype(jnp.float32)
    total = jnp.zeros((count, own_ref.shape[1]), jnp.float32)
    for map_codes, chunk in zip(chunk_codes, maps):
        spread(codes_ref[...], values, map_codes, spread_ref)
        total += lax.dot_general(
            spread_ref[...].T.astype(jnp.bfloat16),
            chunk[...],
            (((1,), (0,)), ((), ())),
            preferred_element_type=jnp.float32,
        )
    deltas = ADAPTER_SCALE * total
    own_ref[...] = deltas[: count // 2].astype(own_ref.dtype)
    mate_ref[...] = deltas[count // 2 :].astype(mate_ref.dtype)


def row_deltas(codes, ranks, first, width_of_ranks, chunks, after=()):
    rank = ranks.shape[0]
    row_count = codes.shape[1]
    chunk_rows, width = chunks[0][1].shape
    whole = lambda i: (0, 0)
    return pl.pallas_call(
        functools.partial(
            delta_kernel, [code_list([(bases, chunk_rows)], rank) for bases, _ in chunks]
        ),
        grid=(1,),
        in_specs=[
            pl.BlockSpec(codes.shape, whole),
            pl.BlockSpec((rank, width_of_ranks), lambda i: (0, first // width_of_ranks)),
        ]
        + [pl.BlockSpec((chunk_rows, width), whole) for _ in chunks]
        + [pl.BlockSpec(memory_space=pl.ANY) for _ in after],
        out_specs=[pl.BlockSpec((row_count // 2, width), whole)] * 2,
        out_shape=[jax.ShapeDtypeStruct((row_count // 2, width), jnp.bfloat16)] * 2,
        scratch_shapes=[pltpu.VMEM((chunk_rows, row_count), jnp.float32)],
        compiler_params=pltpu.CompilerParams(vmem_limit_bytes=VMEM_LIMIT),
    )(codes, ranks, *[chunk for _, chunk in chunks], *after)


def cut_kernel(maps_ref, *refs):
    half = len(refs) // 2
    rows = refs[0].shape[0]
    for p in range(half):
        part = maps_ref[p * rows : (p + 1) * rows, :]
        refs[p][...] = part
        refs[half + p][:rows, :] = part


def cut(maps, parts):
    rows, width = maps.shape[0] // parts, maps.shape[1]
    return pl.pallas_call(
        cut_kernel,
        out_shape=[SENT((rows, width), maps.dtype)] * parts
        + [SENT((2 * rows, width), maps.dtype)] * parts,
        compiler_params=pltpu.CompilerParams(vmem_limit_bytes=VMEM_LIMIT),
        cost_estimate=SHORT,
    )(pltpu.with_memory_space_constraint(maps, pltpu.HBM))


def place_kernel(buffer_ref, piece_ref, *refs):
    out_ref, token_ref = refs[-2:]
    out_ref[...] = piece_ref[...]
    token_ref[...] = jnp.zeros_like(token_ref)


def place(buffer, piece, k, after=()):
    return pl.pallas_call(
        place_kernel,
        grid=(1,),
        in_specs=[
            pl.BlockSpec(memory_space=pl.ANY),
            pl.BlockSpec(piece.shape, lambda i: (0, 0)),
        ]
        + [pl.BlockSpec(memory_space=pl.ANY) for _ in after],
        out_specs=[pl.BlockSpec(piece.shape, lambda i: (k, 0)), TOKEN_SPEC],
        out_shape=[SENT(buffer.shape, buffer.dtype), TOKEN],
        input_output_aliases={0: 0},
        compiler_params=pltpu.CompilerParams(vmem_limit_bytes=VMEM_LIMIT),
        cost_estimate=SHORT,
    )(buffer, piece, *after)


def finish_rows_kernel(
    cached_ref, weight_ref, base_ref, own_ref, mate_ref, attended_ref, fresh_ref, token_ref
):
    token_ref[...] = jnp.zeros_like(token_ref)
    delta = own_ref[...].astype(jnp.float32) + mate_ref[...].astype(jnp.float32)
    fresh = (base_ref[...] + delta).astype(jnp.bfloat16)
    fresh_ref[...] = fresh
    heads = cached_ref.shape[1]
    group = heads * HEAD_SIZE // fresh.shape[1]
    for j in range(heads):
        value = slice(j // group * HEAD_SIZE, (j // group + 1) * HEAD_SIZE)
        attended = cached_ref[:, j, :] + weight_ref[:, j, :] * fresh[:, value].astype(jnp.float32)
        attended_ref[:, j * HEAD_SIZE : (j + 1) * HEAD_SIZE] = attended.astype(jnp.bfloat16)


def finish_rows(cached, own_weight, base_values, own_delta, mate_delta):
    row_count, heads, size = cached.shape
    return pl.pallas_call(
        finish_rows_kernel,
        out_shape=[
            jax.ShapeDtypeStruct((row_count, heads * size), jnp.bfloat16),
            jax.ShapeDtypeStruct(base_values.shape, jnp.bfloat16),
            TOKEN,
        ],
        compiler_params=pltpu.CompilerParams(vmem_limit_bytes=VMEM_LIMIT),
        cost_estimate=SHORT,
    )(cached, own_weight, base_values, own_delta, mate_delta)


def gradient_kernel(
    row_codes, arrived_counts, codes_ref, rewards_ref, factor_ref, own_ref, mate_ref, *refs
):
    arrived = list(refs[: sum(arrived_counts)])
    *outs, token_ref, spread_ref = refs[-2 - len(arrived_counts) :]
    token_count = own_ref.shape[0]

    @pl.when(pl.program_id(0) == 0)
    def _():
        token_ref[...] = jnp.zeros_like(token_ref)
        scale = ADAPTER_SCALE * rewards_ref[...].astype(jnp.float32)
        scaled = (scale * factor_ref[...]).astype(jnp.bfloat16).astype(jnp.float32)
        spread(codes_ref[...], scaled, row_codes, spread_ref)

    total = jnp.dot(
        spread_ref[:, :token_count], own_ref[...], preferred_element_type=jnp.float32
    ) + jnp.dot(spread_ref[:, token_count:], mate_ref[...], preferred_element_type=jnp.float32)
    first = 0
    for out_ref, count in zip(outs, arrived_counts):
        rows = out_ref.shape[0]
        piece = total[first : first + rows]
        for _ in range(count):
            piece += arrived.pop(0)[...].astype(jnp.float32)
        out_ref[...] = piece.astype(out_ref.dtype)
        first += rows


def gradient_chunks(codes, rewards, factor, own, mate, chunks, after=(), cost=SHORT):
    rank = factor.shape[0]
    token_count, width = own.shape
    tile = largest_tile(width, 512)
    out_rows = [adapters * rank for _, adapters, _, _ in chunks]
    arrived = [(a, rows) for (_, _, _, arrays), rows in zip(chunks, out_rows) for a in arrays]
    whole = lambda i: (0, 0)
    across = lambda i: (0, i)
    return pl.pallas_call(
        functools.partial(
            gradient_kernel,
            code_list([(chunk[0], rows) for chunk, rows in zip(chunks, out_rows)], rank),
            [len(arrays) for _, _, _, arrays in chunks],
        ),
        grid=(width // tile,),
        in_specs=[
            pl.BlockSpec((1, 2 * token_count), whole),
            pl.BlockSpec(rewards.shape, whole),
            pl.BlockSpec((rank, 2 * token_count), whole),
            pl.BlockSpec((token_count, tile), across),
            pl.BlockSpec((token_count, tile), across),
        ]
        + [pl.BlockSpec((rows, tile), across) for _, rows in arrived]
        + [pl.BlockSpec(memory_space=pl.ANY) for _ in after],
        out_specs=[pl.BlockSpec((rows, tile), across) for rows in out_rows] + [TOKEN_SPEC],
        out_shape=[
            (SENT if dtype == jnp.bfloat16 else jax.ShapeDtypeStruct)((rows, width), dtype)
            for rows, (_, _, dtype, _) in zip(out_rows, chunks)
        ]
        + [TOKEN],
        scratch_shapes=[pltpu.VMEM((sum(out_rows), 2 * token_count), jnp.bfloat16)],
        compiler_params=pltpu.CompilerParams(vmem_limit_bytes=VMEM_LIMIT),
        cost_estimate=cost,
    )(codes, rewards, factor, own, mate, *[a for a, _ in arrived], *after)


def add_kernel(groups, *refs):
    starts, refs = refs[: len(groups)], refs[len(groups) :]
    *outs, token_ref = refs[-1 - len(groups) :]
    token_ref[...] = jnp.zeros_like(token_ref)
    arrived = list(refs)
    for places, start_ref, out_ref in zip(groups, starts, outs):
        rows = out_ref.shape[0] // len(places)
        for p, firsts in enumerate(places):
            part = slice(p * rows, (p + 1) * rows)
            total = start_ref[part, :]
            for k in firsts:
                total += arrived.pop(0)[k * rows : (k + 1) * rows, :].astype(jnp.float32)
            out_ref[part, :] = total.astype(out_ref.dtype)


def add_arrived(groups, after=(), dtype=jnp.bfloat16):
    width = groups[0][0].shape[1]
    tile = largest_tile(width, 1024)
    arrays = [start for start, _ in groups]
    arrays += [a for _, parts in groups for arrived in parts for a, _ in arrived]
    across = lambda i: (0, i)
    return pl.pallas_call(
        functools.partial(
            add_kernel, [[[k for _, k in arrived] for arrived in parts] for _, parts in groups]
        ),
        grid=(width // tile,),
        in_specs=[pl.BlockSpec((a.shape[0], tile), across) for a in arrays]
        + [pl.BlockSpec(memory_space=pl.ANY) for _ in after],
        out_specs=[pl.BlockSpec((start.shape[0], tile), across) for start, _ in groups]
        + [TOKEN_SPEC],
        out_shape=[
            (SENT if dtype == jnp.bfloat16 else jax.ShapeDtypeStruct)(start.shape, dtype)
            for start, _ in groups
        ]
        + [TOKEN],
        compiler_params=pltpu.CompilerParams(vmem_limit_bytes=VMEM_LIMIT),
        cost_estimate=SHORT,
    )(*arrays, *after)


def wait_for(array, *others):
    return lax.optimization_barrier((array, *others))[0]


def step_kernel(piece_ref, came_ref, *refs):
    out_ref, sent_ref = refs[-2:]
    total = piece_ref[...] + came_ref[...].astype(jnp.float32)
    out_ref[...] = total
    sent_ref[...] = total.astype(sent_ref.dtype)


def sum_over(axis, piece, sent, waits=()):
    for k, bit in enumerate(axis_bits(axis)):
        came = swap(sent, axis, bit)
        after = waits[k] if k < len(waits) else ()
        whole = pl.BlockSpec(piece.shape, lambda: (0, 0))
        piece, sent = pl.pallas_call(
            step_kernel,
            in_specs=[whole, whole] + [pl.BlockSpec(memory_space=pl.ANY) for _ in after],
            out_specs=[whole, whole],
            out_shape=[
                jax.ShapeDtypeStruct(piece.shape, dtype) for dtype in (jnp.float32, jnp.bfloat16)
            ],
            compiler_params=pltpu.CompilerParams(vmem_limit_bytes=VMEM_LIMIT),
            cost_estimate=SHORT,
        )(piece, came, *after)
    return piece


def attend_kernel(kv_local, lengths_ref, queries_ref, keys_ref, values_ref, fresh_ref, *refs):
    out_ref, own_ref = refs[-2:]
    block, heads, size = queries_ref.shape
    slots = keys_ref.shape[1]
    group = heads // kv_local
    first_row = pl.program_id(0) * block
    inverse = 1.0 / math.sqrt(size)
    head_of = lax.broadcasted_iota(jnp.int32, (heads, size), 0) // group
    slot = lax.broadcasted_iota(jnp.int32, (heads, slots), 1)

    scores, own_scores = [], []
    for r in range(block):
        queries = queries_ref[r].astype(jnp.float32)
        spread_queries = jnp.concatenate(
            [jnp.where(head_of == h, queries, 0.0) for h in range(kv_local)], axis=1
        )
        products = times_transposed(spread_queries.astype(jnp.bfloat16), keys_ref[r])
        scores.append(jnp.where(slot < lengths_ref[first_row + r], inverse * products, NEG_FILL))
        own_scores.append(spread_queries * fresh_ref[r : r + 1, :])
    scores = jnp.concatenate(scores)
    own_score = inverse * jnp.sum(jnp.concatenate(own_scores), axis=1, keepdims=True)
    highest = jnp.maximum(jnp.max(scores, axis=1, keepdims=True), own_score)
    cache_exp = jnp.exp(scores - highest)
    own_exp = jnp.exp(own_score - highest)
    denominator = jnp.sum(cache_exp, axis=1, keepdims=True) + own_exp
    weights = cache_exp / denominator
    own_weight = (own_exp / denominator).astype(jnp.bfloat16).astype(jnp.float32)
    for r in range(block):
        mine = slice(r * heads, (r + 1) * heads)
        summed = jnp.dot(
            weights[mine].astype(jnp.bfloat16), values_ref[r], preferred_element_type=jnp.float32
        )
        chosen = summed[:, :size]
        for h in range(1, kv_local):
            chosen = jnp.where(head_of == h, summed[:, h * size : (h + 1) * size], chosen)
        out_ref[r] = chosen
        own_ref[r] = jnp.broadcast_to(own_weight[mine], (heads, size))


def attend_cached(queries, cached_key_rows, cached_value_rows, lengths, fresh_keys, after=()):
    row_count, slots, kv_width = cached_key_rows.shape
    heads = queries.shape[1] // HEAD_SIZE
    block = largest_tile(row_count, 8)
    rows_of = lambda i, *_: (i, 0, 0)
    head_spec = pl.BlockSpec((block, heads, HEAD_SIZE), rows_of)
    cache_spec = pl.BlockSpec((block, slots, kv_width), rows_of)
    shape = (row_count, heads, HEAD_SIZE)
    return pl.pallas_call(
        functools.partial(attend_kernel, kv_width // HEAD_SIZE),
        grid_spec=pltpu.PrefetchScalarGridSpec(
            num_scalar_prefetch=1,
            grid=(row_count // block,),
            in_specs=[
                head_spec,
                cache_spec,
                cache_spec,
                pl.BlockSpec((block, kv_width), lambda i, *_: (i, 0)),
            ]
            + [pl.BlockSpec(memory_space=pl.ANY) for _ in after],
            out_specs=[head_spec, head_spec],
        ),
        out_shape=[jax.ShapeDtypeStruct(shape, jnp.float32)] * 2,
        compiler_params=pltpu.CompilerParams(vmem_limit_bytes=VMEM_LIMIT),
        cost_estimate=SHORT,
    )(
        lengths,
        queries.reshape(shape),
        pltpu.with_memory_space_constraint(cached_key_rows, pltpu.HBM),
        pltpu.with_memory_space_constraint(cached_value_rows, pltpu.HBM),
        fresh_keys.astype(jnp.float32),
        *after,
    )


def per_device(
    decode_hidden_input,
    queries,
    cached_key_rows,
    cached_value_rows,
    lengths,
    decode_adapter_index,
    key_matrix,
    value_matrix,
    adapter_down_map,
    adapter_up_map,
    training_hidden_input,
    cotangent,
    training_adapter_index,
    rewards,
):
    core_bit, *chip_bits = axis_bits("wide")
    masks = [m for m in range(lax.axis_size("wide")) if not m & core_bit]
    me = lax.axis_index("wide")
    owner_totals, rank, down_width = adapter_down_map.shape
    up_width = adapter_up_map.shape[2]
    row_count = decode_hidden_input.shape[0]
    token_count = training_hidden_input.shape[0]
    parts = len(chip_bits) if owner_totals % len(chip_bits) == 0 else 1
    orders = [chip_bits[p:] + chip_bits[:p] for p in range(parts)]
    part_adapters = owner_totals // parts
    part_rows = part_adapters * rank

    flattened_down = adapter_down_map.reshape(-1, down_width)
    flattened_up = adapter_up_map.reshape(-1, up_width)

    far = [m for m in masks if m.bit_count() > 1]
    near = [m for m in masks if m.bit_count() == 1]

    numbers = jnp.concatenate([training_adapter_index, rewards, decode_adapter_index])
    mate_numbers = swap(numbers, "wide", core_bit)
    mate_cotangent = swap(wait_for(cotangent, mate_numbers), "wide", core_bit)
    up_maps = {0: flattened_up}
    own_parts = cut(flattened_down, parts)
    own_parts, own_buffers = own_parts[:parts], own_parts[parts:]
    for m in near:
        up_maps[m] = swap(wait_for(flattened_up, *own_parts), "wide", m)
    for m in far:
        up_maps[m] = swap(wait_for(flattened_up, mate_numbers), "wide", m)
    mate_hidden = swap(wait_for(training_hidden_input, mate_numbers), "wide", core_bit)
    decode_slice = lax.dynamic_slice_in_dim(
        decode_hidden_input, lax.axis_index("narrow") * down_width, down_width, 1
    )
    mate_slice = swap(wait_for(decode_slice, mate_cotangent), "wide", core_bit)

    def codes_of(ids):
        return (((ids // owner_totals) ^ me) * owner_totals + ids % owner_totals)[None, :]

    token_codes = codes_of(
        jnp.concatenate([training_adapter_index, mate_numbers[:token_count]])
    )
    token_rewards = jnp.concatenate([rewards, mate_numbers[token_count : 2 * token_count]])[
        None, :
    ]
    row_codes = codes_of(
        jnp.concatenate([decode_adapter_index, mate_numbers[2 * token_count :]])
    )
    tile = token_tile(token_count, down_width)
    all_codes = jnp.concatenate(
        [token_codes, jnp.pad(row_codes, ((0, 0), (0, tile - 2 * row_count)), constant_values=-1)],
        axis=1,
    )
    up_chunks = [([m * owner_totals], up_maps[m]) for m in masks]
    hidden_rows = wait_for(decode_hidden_input, mate_numbers, *[up_maps[m] for m in near])
    fresh_keys = jnp.dot(
        hidden_rows, key_matrix, preferred_element_type=jnp.float32
    ).astype(jnp.bfloat16)
    base_values = jnp.dot(hidden_rows, value_matrix, preferred_element_type=jnp.float32)

    cached, own_weight = attend_cached(
        queries, cached_key_rows, cached_value_rows, lengths, fresh_keys
    )

    stages, second_sent = [], []
    down_parts = {(0, p): own_parts[p] for p in range(parts)}
    for p, order in enumerate(orders):
        held = [0]
        for bit in order:
            sent = own_parts[p]
            if len(held) > 1:
                sent = own_buffers[p]
                if len(held) > 2:
                    sent = jnp.pad(sent, ((0, (len(held) - 2) * part_rows), (0, 0)))
                for k, m in enumerate(held[1:], 1):
                    sent, token = place(sent, down_parts[m, p], k, (cached,))
                    second_sent.append(token)
            came = swap(sent, "wide", bit)
            for k, m in enumerate(held):
                down_parts[m | bit, p] = came[k * part_rows : (k + 1) * part_rows]
            if bit == order[0]:
                down_stages = [(bit, p, [bit], came)]
            else:
                down_stages.append((bit, p, [m | bit for m in held], came))
            held = held + [m | bit for m in held]
        stages.extend(down_stages)
    last_maps = [came for bit, p, _, came in stages if bit == orders[p][-1]]
    first_maps = [came for bit, p, _, came in stages if bit == orders[p][0]]

    def down_code(m, p):
        return m * owner_totals + p * part_adapters

    down_chunks = [([0], flattened_down)] + [
        ([down_code(m, p) for m in came_from], came) for _, p, came_from, came in stages
    ]

    part_back, sent_back = project_tokens(
        all_codes,
        [cotangent, mate_cotangent],
        up_chunks,
        rank,
        after=second_sent,
    )
    back = sum_over("narrow", part_back, sent_back, [(), (base_values,)])

    groups = {}
    for m in far + near:
        for p, order in enumerate(orders):
            level = max(k for k, bit in enumerate(order) if m & bit)
            groups.setdefault((level, p, m == order[level]), []).append(m)
    group_keys = sorted(groups, key=lambda key: (-key[0], key[2]))
    last_level = len(chip_bits) - 1
    own_down, *results, token = gradient_chunks(
        token_codes,
        token_rewards,
        back,
        training_hidden_input,
        mate_hidden,
        [([0], owner_totals, jnp.float32, ())]
        + [
            (
                [down_code(m, p) for m in groups[level, p, direct]],
                part_adapters * len(groups[level, p, direct]),
                jnp.bfloat16 if level == last_level else jnp.float32,
                (),
            )
            for level, p, direct in group_keys
        ],
        (mate_slice,),
    )
    grads = dict(zip(group_keys, results))
    arrived = {(m, p): [] for m in masks for p in range(parts)}

    def send_level(level):
        for key in group_keys:
            if key[0] == level:
                bit = orders[key[1]][level]
                came = swap(wait_for(grads[key], *last_maps), "wide", bit)
                for k, m in enumerate(groups[key]):
                    arrived[m ^ bit, key[1]].append((came, k))

    send_level(last_level)

    part_hidden, sent_hidden = project_tokens(
        all_codes,
        [training_hidden_input, mate_hidden],
        down_chunks,
        rank,
        rows=(decode_slice, mate_slice),
        after=(token,),
    )
    token = sent_hidden
    for level in reversed(range(last_level)):
        added = [key for key in group_keys if key[0] == level]
        *sums, token = add_arrived(
            [(grads[key], [arrived[m, key[1]] for m in groups[key]]) for key in added], (token,)
        )
        grads.update(zip(added, sums))
        send_level(level)
    early = [[arrived[0, p][:-1] for p in range(parts)]]
    own_down, own_token = add_arrived([(own_down, *early)], (token,), jnp.float32)
    last_down = [arrived[0, p][-1:] for p in range(parts)]

    hidden = sum_over(
        "narrow",
        part_hidden,
        sent_hidden,
        [(token,), (own_token,)],
    )
    own_up, *up_results, token = gradient_chunks(
        token_codes,
        token_rewards,
        hidden,
        cotangent,
        mate_cotangent,
        [([m * owner_totals], owner_totals, jnp.bfloat16 if m else jnp.float32, ()) for m in masks],
    )
    own_delta, mate_delta = row_deltas(
        row_codes, hidden, 2 * token_count, tile, up_chunks, (token,)
    )
    mate_delta = wait_for(mate_delta, *[came for part in last_down for came, _ in part])
    came_up = [(swap(result, "wide", m), 0) for m, result in zip(masks[1:], up_results)]
    grad_down, token = add_arrived([(own_down, last_down)], (), jnp.float32)
    attended, fresh_values, rows_token = finish_rows(
        cached, own_weight, base_values, own_delta, swap(mate_delta, "wide", core_bit)
    )
    grad_up, _ = add_arrived([(own_up, [came_up])], (token, rows_token), jnp.float32)
    return (
        attended,
        fresh_values,
        grad_down.reshape(adapter_down_map.shape),
        grad_up.reshape(adapter_up_map.shape),
    )


def solution(mesh):
    return jax.shard_map(
        per_device,
        mesh=mesh,
        in_specs=(
            P("wide", None),
            P("wide", "narrow"),
            P("wide", None, "narrow"),
            P("wide", None, "narrow"),
            P("wide"),
            P("wide"),
            P(None, "narrow"),
            P(None, "narrow"),
            P("wide", None, "narrow"),
            P("wide", None, "narrow"),
            P("wide", "narrow"),
            P("wide", "narrow"),
            P("wide"),
            P("wide"),
        ),
        out_specs=(
            P("wide", "narrow"),
            P("wide", "narrow"),
            P("wide", None, "narrow"),
            P("wide", None, "narrow"),
        ),
        check_vma=False,
    )
```
